256 devices in a mesh: dp: 4 (over x_hi, core), mx: 8 (over z), my: 8 (over x_lo, y).
Axes of the slice: x: 4 (x_hi: 2, x_lo: 2; x = x_hi * 2 + x_lo), y: 4, z: 8, core: 2. Of those that a mesh axis runs over, the one named last changes fastest.
Arguments:
- tokens: bfloat16 [8, 256, 6144], P(None, 'dp', ('mx', 'my')), may hold values from -170 to 170
- w_qkv: bfloat16 [6144, 3, 3072], P(('mx', 'dp'), None, 'my'), may hold values from -2 to 2
- w_up: bfloat16 [6144, 12288], P(('mx', 'dp'), 'my'), may hold values from -2 to 2
- w_proj: bfloat16 [3072, 6144], P('my', ('mx', 'dp')), may hold values from -0.109375 to 0.109375
- w_down: bfloat16 [12288, 6144], P('my', ('mx', 'dp')), may hold values from -0.0546875 to 0.0546875
- cotangent: bfloat16 [8, 256, 6144], P(None, 'dp', ('mx', 'my')), may hold values from -6 to 6
Outputs:
- update: bfloat16 [8, 256, 6144], P(None, 'dp', ('mx', 'my'))
- tokens_grad: bfloat16 [8, 256, 6144], P(None, 'dp', ('mx', 'my'))
- g_qkv: bfloat16 [6144, 3, 3072], P(('mx', 'dp'), None, 'my')
- g_up: bfloat16 [6144, 12288], P(('mx', 'dp'), 'my')
- g_proj: bfloat16 [3072, 6144], P('my', ('mx', 'dp'))
- g_down: bfloat16 [12288, 6144], P('my', ('mx', 'dp'))
The draws below stay inside these ranges and needn't reach their ends.
All inputs are finite; a program needn't handle non-finite values.
Results may differ from the reference program's by a relative error of at most 0.034.
Values may be sent and summed in bfloat16 or wider, within the bound.
A program may use at most 64 MiB of HBM per device.

```python
import jax
import jax.numpy as jnp
from jax import lax

D = 6144
HEADS = 24
HD = 128
FFN = 12288
PATCHES = 256
IMAGES = 8
TOKENS = 2048
E = 3072
N_DP = 4
N_MX = 8


def draw_tokens(key, part):
    key = jax.random.fold_in(key, 11)
    keys_all = jax.random.split(key, 5)
    position = jnp.arange(D, dtype=jnp.float32) / D
    base_draw = jnp.clip(jax.random.normal(keys_all[0], (TOKENS, D)), -6.0, 6.0)
    offset = jax.random.uniform(keys_all[1], (D,), minval=0.3, maxval=1.0)
    row_scale = jnp.exp(jax.random.uniform(keys_all[2], (TOKENS, 1)) * jnp.log(10.0))
    col_scale = jnp.exp(position * jnp.log(3.0) + jax.random.uniform(keys_all[3], (D,)) * jnp.log(10.0 / 3.0))
    token_sign = jax.random.uniform(keys_all[4], (TOKENS, 1), minval=-1.0, maxval=1.0)
    values = 0.2 * row_scale * col_scale[None, :] * (base_draw + token_sign * offset[None, :])
    return values.reshape(IMAGES, PATCHES, D).astype(jnp.bfloat16)


def add_rising(key, noise_part, columns, common_weight):
    keys_all = jax.random.split(key, 2)
    position = jnp.arange(D, dtype=jnp.float32) / D
    rise_rows = jnp.exp(position * jnp.log(3.0) + jax.random.uniform(keys_all[0], (D,)) * jnp.log(2.0))
    common = jnp.clip(jax.random.normal(keys_all[1], (columns,)), -3.0, 3.0) * common_weight
    return (noise_part + rise_rows[:, None] * common[None, :]) / jnp.sqrt(jnp.float32(D))


def draw_w_qkv(key, part):
    key = jax.random.fold_in(key, 23)
    noise_key, rest_key = jax.random.split(key)
    columns = 3 * HEADS * HD
    noise_part = jnp.clip(jax.random.normal(noise_key, (D, columns)), -6.0, 6.0)
    common_weight = jnp.where(jnp.arange(columns) < 2 * HEADS * HD, 0.05, 0.5)
    values = add_rising(rest_key, noise_part, columns, common_weight)
    return values.reshape(D, 3, HEADS * HD).astype(jnp.bfloat16)


def draw_w_up(key, part):
    key = jax.random.fold_in(key, 37)
    noise_key, rest_key = jax.random.split(key)
    noise_part = jnp.clip(jax.random.normal(noise_key, (D, FFN)), -6.0, 6.0)
    return add_rising(rest_key, noise_part, FFN, 0.5).astype(jnp.bfloat16)


def steps_of(stream_key, shape, shards, smallest, top_value):
    loudness, own = 1.0, jax.random.fold_in(stream_key, 6)
    for axis_at, shards_of in shards:
        heights = jnp.exp(jax.random.uniform(jax.random.fold_in(own, axis_at), (shards_of,), jnp.float32, smallest / len(shards), top_value / len(shards)))
        loudness = loudness * jnp.repeat(heights, shape[axis_at] // shards_of).reshape([-1 if axis == axis_at else 1 for axis in range(len(shape))])
    return loudness


def scatter_about(own_key, shape, scale, reach, cuts=(), held_as=jnp.bfloat16):
    array = jax.random.normal(own_key, shape, jnp.float32) * scale
    if len(cuts) > 0:
        array = steps_of(own_key, shape, cuts, -0.22, 0.18) * array
    return jnp.clip(array, min=-reach, max=reach).astype(held_as)


def setup_inputs(seed: int = 0) -> dict:
    streams_of = jax.random.split(jax.random.key(seed), 7)
    return {
        "tokens": draw_tokens(jax.random.fold_in(streams_of[6], 71), 0),
        "w_qkv": draw_w_qkv(jax.random.fold_in(streams_of[6], 71), 0),
        "w_up": draw_w_up(jax.random.fold_in(streams_of[6], 71), 0),
        "w_proj": scatter_about(streams_of[3], (E, D), E ** -0.5, 0.109375, ((0, 8), (1, 32))),
        "w_down": scatter_about(streams_of[4], (FFN, D), FFN ** -0.5, 0.0546875, ((0, 8), (1, 32))),
        "cotangent": scatter_about(streams_of[5], (IMAGES, PATCHES, D), 1.0, 6.0, ((1, 4), (2, 64))),
    }


EPS = 1e-06

def gelu_exact(values):
    return jax.nn.gelu(values, approximate=False)

def head_norm(head_block):
    average = lax.optimization_barrier(jnp.mean(head_block, axis=-1, keepdims=True))
    centered = head_block - average
    inverse = lax.rsqrt(lax.optimization_barrier(jnp.mean(centered * centered, axis=-1, keepdims=True)) + EPS)
    return (centered * inverse, inverse)

def head_norm_back(upstream, normal, inverse):
    return inverse * (upstream - lax.optimization_barrier(jnp.mean(upstream, axis=-1, keepdims=True)) - normal * lax.optimization_barrier(jnp.mean(upstream * normal, axis=-1, keepdims=True)))

def round_kept(values):
    rounded = lax.optimization_barrier(values.astype(jnp.bfloat16))
    return rounded.astype(jnp.float32)

def group_rows(values, group_index):
    block = PATCHES // N_DP
    shaped = values.reshape(IMAGES, PATCHES, values.shape[-1])
    return shaped[:, group_index * block:(group_index + 1) * block].reshape(IMAGES * block, values.shape[-1])

def reference(tokens, w_qkv, w_up, w_proj, w_down, cotangent):
    x_float = tokens.reshape(TOKENS, D).astype(jnp.float32)
    cot_rows = cotangent.reshape(TOKENS, D)
    average = lax.optimization_barrier(jnp.mean(x_float, axis=1, keepdims=True))
    centered = x_float - average
    inverse = lax.rsqrt(lax.optimization_barrier(jnp.mean(centered * centered, axis=1, keepdims=True)) + EPS)
    standard = centered * inverse
    normed = standard.astype(jnp.bfloat16)
    inner_width = HEADS * HD
    qkv_cols = 3 * inner_width
    first_weights = jnp.concatenate([w_qkv.reshape(D, qkv_cols), w_up], axis=1)
    second_weights = jnp.concatenate([w_proj, w_down], axis=0)
    feat_block = D // N_MX
    branch_in = jnp.zeros((TOKENS, first_weights.shape[1]), jnp.float32)
    for block_index in range(N_MX):
        first_row = block_index * feat_block
        last_row = first_row + feat_block
        branch_in = branch_in + round_kept(jnp.dot(normed[:, first_row:last_row], first_weights[first_row:last_row], preferred_element_type=jnp.float32))
    projected = branch_in[:, :qkv_cols].reshape(IMAGES, PATCHES, 3, HEADS, HD)
    query_hat, query_inv = head_norm(projected[:, :, 0])
    key_hat, key_inv = head_norm(projected[:, :, 1])
    query_low = query_hat.astype(jnp.bfloat16)
    key_low = key_hat.astype(jnp.bfloat16)
    value_low = projected[:, :, 2].astype(jnp.bfloat16)
    factor = HD ** (-0.5)
    scores = jnp.einsum('iqhd,ikhd->ihqk', query_low.astype(jnp.float32), key_low.astype(jnp.float32)) * factor
    raised = jnp.exp(scores)
    attn_probs = raised / lax.optimization_barrier(jnp.sum(raised, axis=-1, keepdims=True))
    probs_low = attn_probs.astype(jnp.bfloat16)
    attended = jnp.einsum('ihqk,ikhd->iqhd', probs_low.astype(jnp.float32), value_low.astype(jnp.float32)).astype(jnp.bfloat16)
    hidden_pre = branch_in[:, qkv_cols:]
    gelu_value, gelu_back = jax.vjp(gelu_exact, hidden_pre)
    activated = gelu_value.astype(jnp.bfloat16)
    branch_out = jnp.concatenate([attended.reshape(TOKENS, inner_width), activated], axis=1)
    update = jnp.dot(branch_out, second_weights, preferred_element_type=jnp.float32).astype(jnp.bfloat16)
    branch_grad = jnp.zeros((TOKENS, second_weights.shape[0]), jnp.float32)
    for block_index in range(N_MX):
        first_row = block_index * feat_block
        last_row = first_row + feat_block
        branch_grad = branch_grad + round_kept(jnp.dot(cot_rows[:, first_row:last_row], second_weights[:, first_row:last_row].T, preferred_element_type=jnp.float32))
    attn_grad = branch_grad[:, :inner_width].astype(jnp.bfloat16).reshape(IMAGES, PATCHES, HEADS, HD)
    hid_grad = gelu_back(branch_grad[:, inner_width:])[0].astype(jnp.bfloat16)
    value_grad = jnp.einsum('ihqk,iqhd->ikhd', probs_low.astype(jnp.float32), attn_grad.astype(jnp.float32)).astype(jnp.bfloat16)
    prob_grad = jnp.einsum('iqhd,ikhd->ihqk', attn_grad.astype(jnp.float32), value_low.astype(jnp.float32))
    score_grad = attn_probs * (prob_grad - lax.optimization_barrier(jnp.sum(attn_probs * prob_grad, axis=-1, keepdims=True)))
    score_low = (score_grad * factor).astype(jnp.bfloat16)
    qn_grad = jnp.einsum('ihqk,ikhd->iqhd', score_low.astype(jnp.float32), key_low.astype(jnp.float32))
    kn_grad = jnp.einsum('ihqk,iqhd->ikhd', score_low.astype(jnp.float32), query_low.astype(jnp.float32))
    query_grad = head_norm_back(qn_grad, query_hat, query_inv).astype(jnp.bfloat16)
    key_grad = head_norm_back(kn_grad, key_hat, key_inv).astype(jnp.bfloat16)
    stacked = jnp.stack([query_grad, key_grad, value_grad], axis=2).reshape(TOKENS, qkv_cols)
    input_grad = jnp.concatenate([stacked, hid_grad], axis=1)
    grad_second = jnp.zeros(second_weights.shape, jnp.float32)
    grad_first = jnp.zeros(first_weights.shape, jnp.float32)
    for group_index in range(N_DP):
        grad_second = grad_second + round_kept(jnp.dot(group_rows(branch_out, group_index).T, group_rows(cot_rows, group_index), preferred_element_type=jnp.float32))
        grad_first = grad_first + round_kept(jnp.dot(group_rows(normed, group_index).T, group_rows(input_grad, group_index), preferred_element_type=jnp.float32))
    grad_second = grad_second.astype(jnp.bfloat16)
    grad_first = grad_first.astype(jnp.bfloat16)
    feat_grad = jnp.dot(input_grad, first_weights.T, preferred_element_type=jnp.float32)
    sum_grad = lax.optimization_barrier(jnp.mean(feat_grad, axis=1, keepdims=True))
    sum_cross = lax.optimization_barrier(jnp.mean(feat_grad * standard, axis=1, keepdims=True))
    tokens_grad = (inverse * (feat_grad - sum_grad - standard * sum_cross)).astype(jnp.bfloat16)
    g_qkv = grad_first[:, :qkv_cols].reshape(D, 3, inner_width)
    g_up = grad_first[:, qkv_cols:]
    g_proj = grad_second[:inner_width]
    g_down = grad_second[inner_width:]
    return (update.reshape(IMAGES, PATCHES, D), tokens_grad.reshape(IMAGES, PATCHES, D), g_qkv, g_up, g_proj, g_down)
```

```python
import functools

import jax
import jax.numpy as jnp
from jax import lax
from jax.experimental import pallas as pl
from jax.experimental.pallas import tpu as pltpu
from jax.sharding import PartitionSpec as P

MESH = pl.DeviceIdType.MESH
F32, BF16 = jnp.float32, jnp.bfloat16

D = 6144
HD = 128
EPS = 1e-06
DP, MX, MY = 4, 8, 8
IMG, PAT = 8, 64
TOK = IMG * PAT
FW = 96
KB = MY * FW
KS = KB // DP
CW = 384
NC = 12
HEADS = CW // HD
FACTOR = HD ** (-0.5)
AG0 = 12
LAST = AG0 + NC + 4

NN = (((1,), (0,)), ((), ()))
NT = (((1,), (1,)), ((), ()))


def dot(a, b, dims=NN):
    return lax.dot_general(a, b, dims, preferred_element_type=F32)


def rcopy(src, dst, ssem, rsem, dev):
    return pltpu.make_async_remote_copy(
        src_ref=src, dst_ref=dst, send_sem=ssem, recv_sem=rsem, device_id=dev, device_id_type=MESH
    )


def rs_id(c):
    one = jnp.int32(1)
    ge4 = jnp.where(c >= 4, one, 0)
    ge8 = jnp.where(c >= 8, one, 0)
    return c + 4 * ge4 - 8 * ge8


def kind(i):
    return jnp.where((i < 4) | (i == 8), 0, 1).astype(jnp.int32)


def head_norm(x):
    hats, invs = [], []
    for h in range(HEADS):
        part = x[:, h * HD : (h + 1) * HD]
        cen = part - jnp.mean(part, axis=1, keepdims=True)
        inv = lax.rsqrt(jnp.mean(cen * cen, axis=1, keepdims=True) + EPS)
        hats.append(cen * inv)
        invs.append(jnp.broadcast_to(inv, cen.shape))
    return jnp.concatenate(hats, axis=1), jnp.concatenate(invs, axis=1)


def head_norm_back(up, hat, inv):
    outs = []
    for h in range(HEADS):
        s = slice(h * HD, (h + 1) * HD)
        u, n = up[:, s], hat[:, s]
        outs.append(
            inv[:, s]
            * (u - jnp.mean(u, axis=1, keepdims=True) - n * jnp.mean(u * n, axis=1, keepdims=True))
        )
    return jnp.concatenate(outs, axis=1)


def kernel(
    xt, ct, w, upd, tgr, gout,
    wg, part, rsl, rss, br, rows, fm, ft, std, acc, gp, gc, gs, gx,
    stage, yrec, xsend, xrec, st_own, st_in, st_fin, st_tot, fs_own, fs_z, fs_mid, fs_y,
    qlow, kvg, kvp, kvr, hats, qn,
    loc_sem, my_ss, my_rs, w_ss, w_rs, rl_ss, rl_rs, rsh_ss, rsh_rs, al_ss, al_rs, ash_ss, ash_rs,
    g_ss, g_rs, kv_ss, kv_rs, kp_ss, kp_rs, y_ss, y_rs, x_ss, x_rs, st_ss, st_rs, fz_ss, fz_rs, fy_ss, fy_rs,
):
    dp, m, my = lax.axis_index("dp"), lax.axis_index("mx"), lax.axis_index("my")
    xh, co = dp // 2, lax.rem(dp, 2)
    xl, yy = my // 4, lax.rem(my, 4)
    dp_x = lax.rem(dp + 2, 4)
    dp_c = xh * 2 + 1 - co
    my_x = lax.rem(my + 4, 8)

    def at_dp(i):
        return {"dp": i, "mx": m, "my": my}

    def at_mx(i):
        return {"dp": dp, "mx": lax.rem(i + 16, 8), "my": my}

    def at_my(i):
        return {"dp": dp, "mx": m, "my": i}

    def y_of(k):
        return lax.rem(yy + k, 4)

    barrier = pltpu.get_barrier_semaphore()
    peers = [at_dp(lax.rem(dp + k, 4)) for k in (1, 2, 3)]
    peers += [at_mx(m + k) for k in range(1, 8)]
    peers += [at_my(lax.rem(my + k, 8)) for k in range(1, 8)]
    for p in peers:
        pl.semaphore_signal(barrier, inc=1, device_id=p, device_id_type=MESH)

    own_w = pltpu.make_async_copy(w, wg.at[:, dp], loc_sem.at[0])
    own_c = pltpu.make_async_copy(ct, ft.at[0, my], loc_sem.at[1])
    own_x = pltpu.make_async_copy(xt, ft.at[1, my], loc_sem.at[2])
    own_c.start()
    own_w.start()
    own_x.start()
    acc[...] = jnp.zeros_like(acc)
    pl.semaphore_wait(barrier, len(peers))

    def my_first(j, src):
        return rcopy(src, ft.at[j, my], my_ss.at[j, 0], my_rs.at[j, 0], at_my(my_x))

    def my_own(j, k, src):
        return rcopy(src, ft.at[j, my], my_ss.at[j, k], my_rs.at[j, k], at_my(xl * 4 + y_of(k)))

    def my_fwd(j, k):
        return rcopy(ft.at[j, my_x], ft.at[j, my_x], my_ss.at[j, 3 + k], my_rs.at[j, 3 + k], at_my(xl * 4 + y_of(k)))

    def my_wait_first(j):
        rcopy(ft.at[j, my_x], ft.at[j, my_x], my_ss.at[j, 0], my_rs.at[j, 0], at_my(my_x)).wait_recv()

    def my_wait(j):
        for k in (1, 3, 2):
            a = xl * 4 + y_of(4 - k)
            b = (1 - xl) * 4 + y_of(4 - k)
            rcopy(ft.at[j, a], ft.at[j, a], my_ss.at[j, k], my_rs.at[j, k], at_my(my_x)).wait_recv()
            rcopy(ft.at[j, b], ft.at[j, b], my_ss.at[j, 3 + k], my_rs.at[j, 3 + k], at_my(my_x)).wait_recv()

    def w_x(i):
        return rcopy(w.at[i], wg.at[i, dp], w_ss.at[i, 0], w_rs.at[i, 0], at_dp(dp_x))

    def w_c(i):
        return rcopy(w.at[i], wg.at[i, dp], w_ss.at[i, 1], w_rs.at[i, 1], at_dp(dp_c))

    def w_f(i):
        return rcopy(wg.at[i, dp_x], wg.at[i, dp_x], w_ss.at[i, 2], w_rs.at[i, 2], at_dp(dp_c))

    def w_wait(i, step, who):
        rcopy(wg.at[i, who], wg.at[i, who], w_ss.at[i, step], w_rs.at[i, step], at_dp(dp_c)).wait_recv()

    my_first(0, ct).start()
    for k in (1, 3, 2):
        my_own(0, k, ct).start()

    def w_start(c, _):
        i = rs_id(c)
        w_x(i).start()
        w_c(i).start()
        return 0

    lax.fori_loop(0, NC, w_start, 0)
    my_first(1, xt).start()
    my_wait_first(0)
    for k in (1, 3, 2):
        my_fwd(0, k).start()
    for k in (1, 3, 2):
        my_own(1, k, xt).start()
    my_wait_first(1)
    for k in (1, 3, 2):
        my_fwd(1, k).start()
    own_w.wait()
    own_c.wait()
    own_x.wait()

    def w_forward(i):
        w_wait(i, 0, dp_x)
        w_f(i).start()

    w_forward(jnp.int32(0))
    my_wait(0)
    fm[0] = jnp.transpose(ft[0].reshape(KB, TOK), (1, 0))

    def stats_send():
        my_wait(1)
        for k in (1, 3, 2):
            my_fwd(1, k).wait_send()
        xs = ft[1].reshape(KB, TOK).astype(F32)
        std[...] = xs
        total = jnp.sum(xs, axis=0, keepdims=True)
        cen = xs - total * (1.0 / KB)
        st_own[0:1, :] = total
        st_own[1:2, :] = jnp.sum(cen * cen, axis=0, keepdims=True)
        for k in range(1, 8):
            rcopy(st_own, st_in.at[k - 1], st_ss.at[k - 1], st_rs.at[k - 1], at_mx(m + k)).start()

    def stats_done():
        for k in range(1, 8):
            rcopy(st_own, st_in.at[k - 1], st_ss.at[k - 1], st_rs.at[k - 1], at_mx(m + k)).wait()
        total = st_own[0:1, :]
        for k in range(7):
            total = total + st_in[k, 0:1, :]
        mean = total * (1.0 / D)
        spread = jnp.zeros_like(mean)
        for k in range(8):
            s, q = (st_own[0:1, :], st_own[1:2, :]) if k == 7 else (st_in[k, 0:1, :], st_in[k, 1:2, :])
            off = s * (1.0 / KB) - mean
            spread = spread + q + KB * off * off
        inv = lax.rsqrt(spread * (1.0 / D) + EPS)
        st_tot[0:1, :] = mean
        st_tot[1:2, :] = inv
        for j in range(MY):
            r = slice(j * FW, (j + 1) * FW)
            s = (std[r, :] - mean) * inv
            std[r, :] = s
            ft[1, j] = s.astype(BF16)
        fm[1] = jnp.transpose(ft[1].reshape(KB, TOK), (1, 0))

    def attn_open():
        q_hat, q_inv = head_norm(br[9])
        k_hat, k_inv = head_norm(br[10])
        hats[0], hats[1], hats[2], hats[3] = q_hat, q_inv, k_hat, k_inv
        qlow[...] = q_hat.astype(BF16)
        kvg[dp, :, :CW] = k_hat.astype(BF16)
        kvg[dp, :, CW:] = br[11].astype(BF16)
        for k in (1, 2, 3):
            rcopy(kvg.at[dp], kvg.at[dp], kv_ss.at[k - 1], kv_rs.at[k - 1], at_dp(lax.rem(dp + k, 4))).start()

    def attn_mid():
        for k in (1, 2, 3):
            s = lax.rem(dp + 4 - k, 4)
            rcopy(kvg.at[s], kvg.at[s], kv_ss.at[k - 1], kv_rs.at[k - 1], at_dp(dp_c)).wait_recv()
            rcopy(kvg.at[dp], kvg.at[dp], kv_ss.at[k - 1], kv_rs.at[k - 1], at_dp(dp_c)).wait_send()
        for h in range(HEADS):
            s = slice(h * HD, (h + 1) * HD)
            q = qlow[:, s]
            keys = kvg[:, :, s].reshape(DP * PAT, HD)
            vals = kvg[:, :, CW + h * HD : CW + (h + 1) * HD].reshape(DP * PAT, HD)
            ag = br[8, :, s].astype(BF16)
            raised = jnp.exp(dot(q, keys, NT) * FACTOR)
            probs = raised / jnp.sum(raised, axis=1, keepdims=True)
            plow = probs.astype(BF16)
            rows[8, m, :, s] = dot(plow, vals).astype(BF16)
            pgrad = dot(ag, vals, NT)
            sgrad = probs * (pgrad - jnp.sum(probs * pgrad, axis=1, keepdims=True))
            slow = (sgrad * FACTOR).astype(BF16)
            qn[:, s] = dot(slow, keys)
            vpart = dot(jnp.transpose(plow.astype(F32), (1, 0)).astype(BF16), ag)
            kpart = dot(jnp.transpose(slow.astype(F32), (1, 0)).astype(BF16), q)
            kvp[:, :, s] = kpart.astype(BF16).reshape(DP, PAT, HD)
            kvp[:, :, CW + h * HD : CW + (h + 1) * HD] = vpart.astype(BF16).reshape(DP, PAT, HD)
        for k in (1, 2, 3):
            t = lax.rem(dp + k, 4)
            rcopy(kvp.at[t], kvr.at[k - 1], kp_ss.at[k - 1], kp_rs.at[k - 1], at_dp(t)).start()

    def attn_close():
        sums = kvp[dp].astype(F32)
        for k in (1, 2, 3):
            t = lax.rem(dp + k, 4)
            rcopy(kvp.at[t], kvr.at[k - 1], kp_ss.at[k - 1], kp_rs.at[k - 1], at_dp(t)).wait()
            sums = sums + kvr[k - 1].astype(F32)
        rows[9, m] = head_norm_back(qn[...], hats[0], hats[1]).astype(BF16)
        rows[10, m] = head_norm_back(sums[:, :CW], hats[2], hats[3]).astype(BF16)
        rows[11, m] = sums[:, CW:].astype(BF16)

    def y_copy(j, k, half):
        t = half * 4 + y_of(k)
        return rcopy(
            stage.at[j, t], yrec.at[j, k - 1, half], y_ss.at[j, k - 1, half], y_rs.at[j, k - 1, half], at_my(xl * 4 + y_of(k))
        )

    def x_copy(j):
        return rcopy(xsend.at[j], xrec.at[j], x_ss.at[j], x_rs.at[j], at_my(my_x))

    def sum_open(j):
        stage[j] = acc[j].astype(BF16)
        for k in (1, 3, 2):
            for half in (0, 1):
                y_copy(j, k, half).start()

    def sum_mid(j):
        total = acc[j, my_x]
        for k in (1, 3, 2):
            for half in (0, 1):
                y_copy(j, k, half).wait()
        for k in (1, 2, 3):
            total = total + yrec[j, k - 1, 1 - xl].astype(F32)
        xsend[j] = total.astype(BF16)
        x_copy(j).start()

    def sum_close(j):
        total = acc[j, my]
        for k in (1, 2, 3):
            total = total + yrec[j, k - 1, xl].astype(F32)
        x_copy(j).wait()
        return total + xrec[j].astype(F32)

    def sign(c):
        return 1 - 2 * lax.rem(c, 2)

    def img(x):
        return lax.rem(x + 16, 8)

    def rl(c, step):
        i, g = rs_id(c), sign(c)
        b = part.at[i, img(m - g * (4 - step))]
        return rcopy(b, rsl.at[i, step], rl_ss.at[c, step], rl_rs.at[c, step], at_mx(m - g))

    def rsh(c, step):
        i, g = rs_id(c), sign(c)
        b = part.at[i, img(m + g * (3 - step))]
        return rcopy(b, rss.at[i, step], rsh_ss.at[c, step], rsh_rs.at[c, step], at_mx(m + g))

    def rs_middle(c, s):
        i, g = rs_id(c), sign(c)
        rl(c, s - 1).wait_recv()
        b = img(m - g * (4 - s))
        part[i, b] = (part[i, b].astype(F32) + rsl[i, s - 1].astype(F32)).astype(BF16)
        rl(c, s).start()
        if s <= 2:
            rsh(c, s - 1).wait_recv()
            b = img(m + g * (3 - s))
            part[i, b] = (part[i, b].astype(F32) + rss[i, s - 1].astype(F32)).astype(BF16)
            rsh(c, s).start()

    def rs_open(c):
        i = rs_id(c)
        w_wait(i, 1, dp_c)
        w_wait(i, 2, xh * 0 + 3 - dp)
        wv = wg[i].reshape(KB, CW)
        j = kind(i)
        for half in range(2):
            res = dot(fm[j, half * 256 : (half + 1) * 256, :], wv).astype(BF16)
            part[i, half * 4 : (half + 1) * 4] = res.reshape(4, PAT, CW)
        rl(c, 0).start()
        rsh(c, 0).start()

    def rs_final(c):
        i = rs_id(c)
        rl(c, 3).wait_recv()
        rsh(c, 2).wait_recv()
        br[i] = part[i, m].astype(F32) + rsl[i, 3].astype(F32) + rss[i, 2].astype(F32)

    def gelu(c):
        i = rs_id(c)
        u = br[i]
        phi = 0.5 + 0.5 * lax.erf(u * 0.7071067811865476)
        rows[i - 4, m] = (u * phi).astype(BF16)
        slope = phi + u * (0.3989422804014327 * jnp.exp(-0.5 * u * u))
        rows[i, m] = (br[i - 4] * slope).astype(BF16)

    def al(a, step):
        g = sign(a)
        b = rows.at[a, img(m + g * step)]
        return rcopy(b, b, al_ss.at[a, step], al_rs.at[a, step], at_mx(m - g))

    def ash(a, step):
        g = sign(a)
        b = rows.at[a, img(m - g * step)]
        return rcopy(b, b, ash_ss.at[a, step], ash_rs.at[a, step], at_mx(m + g))

    def al_wait(a, step):
        b = rows.at[a, img(m + sign(a) * (step + 1))]
        rcopy(b, b, al_ss.at[a, step], al_rs.at[a, step], at_mx(m + 1)).wait_recv()

    def ash_wait(a, step):
        b = rows.at[a, img(m - sign(a) * (step + 1))]
        rcopy(b, b, ash_ss.at[a, step], ash_rs.at[a, step], at_mx(m + 1)).wait_recv()

    def g_c(a, h):
        return rcopy(gp.at[a, h * 2 + 1 - co], gc.at[a, h], g_ss.at[a, h], g_rs.at[a, h], at_dp(dp_c))

    def g_x(a):
        return rcopy(gs.at[a], gx.at[a], g_ss.at[a, 2], g_rs.at[a, 2], at_dp(dp_x))

    def g_open(a):
        al_wait(a, 3)
        ash_wait(a, 2)
        r = rows[a].reshape(TOK, CW)
        j = kind(a)
        for h in range(4):
            gp[a, h] = dot(ft[j, 2 * h : 2 * h + 2].reshape(KS, TOK), r).astype(BF16)
        for h in range(2):
            g_c(a, h).start()
        for h in range(4):
            v = dot(wg[a, h], r, NT).reshape(2, FW, TOK)
            acc[j, 2 * h : 2 * h + 2] = acc[j, 2 * h : 2 * h + 2] + v

    def g_mid(a):
        for h in range(2):
            g_c(a, h).wait()
        gs[a] = (gp[a, dp_x].astype(F32) + gc[a, 1 - xh].astype(F32)).astype(BF16)
        g_x(a).start()

    def g_close(a):
        g_x(a).wait()
        gout[a] = (gp[a, dp].astype(F32) + gc[a, xh].astype(F32) + gx[a].astype(F32)).astype(BF16)

    def when_in(v, lo, hi):
        return pl.when((v >= lo) & (v < hi))

    def tick(t, _):
        for s in (3, 2, 1):
            when_in(t - s, 0, NC)(functools.partial(rs_middle, t - s, s))

        for s in (3, 2, 1):
            a = t - AG0 - s

            @when_in(a, 0, NC)
            def _(a=a, s=s):
                al_wait(a, s - 1)
                al(a, s).start()
                if s <= 2:
                    ash_wait(a, s - 1)
                    ash(a, s).start()

        @pl.when(t + 1 < NC)
        def _():
            w_forward(rs_id(t + 1))

        when_in(t, 0, NC)(functools.partial(rs_open, t))

        @when_in(t - 4, 0, NC)
        def _():
            rs_final(t - 4)

        when_in(t - 4, 8, NC)(functools.partial(gelu, t - 4))

        @when_in(t - AG0, 0, NC)
        def _():
            al(t - AG0, 0).start()
            ash(t - AG0, 0).start()

        pl.when(t == 2)(stats_send)
        pl.when(t == 4)(stats_done)
        pl.when(t == 11)(attn_open)
        pl.when(t == 13)(attn_mid)
        pl.when(t == 16)(attn_close)

        when_in(t - AG0 - 4, 0, NC)(functools.partial(g_open, t - AG0 - 4))
        when_in(t - AG0 - 5, 0, NC - 1)(functools.partial(g_mid, t - AG0 - 5))
        when_in(t - AG0 - 7, 0, NC - 3)(functools.partial(g_close, t - AG0 - 7))

        pl.when(t == AG0 + 13)(functools.partial(sum_open, 0))
        pl.when(t == AG0 + 15)(functools.partial(sum_mid, 0))

        for s in (4, 3, 2, 1):
            c = t - s

            @when_in(c, 0, NC)
            def _(c=c, s=s):
                rl(c, s - 1).wait_send()
                if s <= 3:
                    rsh(c, s - 1).wait_send()

            a = t - AG0 - s

            @when_in(a, 0, NC)
            def _(a=a, s=s):
                al(a, s - 1).wait_send()
                if s <= 3:
                    ash(a, s - 1).wait_send()

        return 0

    lax.fori_loop(0, LAST, tick, 0)

    sum_open(1)
    fsum = jnp.zeros((1, TOK), F32)
    fcross = jnp.zeros((1, TOK), F32)
    for j in range(MY):
        v = acc[1, j]
        fsum = fsum + jnp.sum(v, axis=0, keepdims=True)
        fcross = fcross + jnp.sum(v * std[j * FW : (j + 1) * FW, :], axis=0, keepdims=True)
    fs_own[0:1, :] = fsum
    fs_own[1:2, :] = fcross

    def fz(k):
        return rcopy(fs_own, fs_z.at[k - 1], fz_ss.at[k - 1], fz_rs.at[k - 1], at_mx(m + k))

    def fy(k):
        return rcopy(fs_mid, fs_y.at[k - 1], fy_ss.at[k - 1], fy_rs.at[k - 1], at_my(lax.rem(my + k, 8)))

    for k in range(1, 8):
        fz(k).start()
    g_mid(NC - 1)
    upd[...] = sum_close(0).astype(BF16)
    for k in range(1, 8):
        fz(k).wait()
    tot = fs_own[...]
    for k in range(7):
        tot = tot + fs_z[k]
    fs_mid[...] = tot
    for k in range(1, 8):
        fy(k).start()
    g_close(NC - 3)
    g_close(NC - 2)
    g_close(NC - 1)
    sum_mid(1)
    for k in range(1, 8):
        fy(k).wait()
    tot = fs_mid[...]
    for k in range(7):
        tot = tot + fs_y[k]
    mean_g = tot[0:1, :] * (1.0 / D)
    mean_c = tot[1:2, :] * (1.0 / D)
    fg = sum_close(1)
    own = std[pl.ds(pl.multiple_of(my * FW, FW), FW), :]
    tgr[...] = (st_tot[1:2, :] * (fg - mean_g - own * mean_c)).astype(BF16)

    for j, src in ((0, ct), (1, xt)):
        my_first(j, src).wait_send()
        for k in (1, 3, 2):
            my_own(j, k, src).wait_send()
    for k in (1, 3, 2):
        my_fwd(0, k).wait_send()

    def w_done(i, _):
        w_x(i).wait_send()
        w_c(i).wait_send()
        w_f(i).wait_send()
        return 0

    lax.fori_loop(0, NC, w_done, 0)


def fused(xt, ct, w):
    vm, sem = pltpu.VMEM, pltpu.SemaphoreType.DMA
    scratch = [
        vm((NC, DP, KS, CW), BF16),
        vm((NC, IMG, PAT, CW), BF16),
        vm((NC, 4, PAT, CW), BF16),
        vm((NC, 3, PAT, CW), BF16),
        vm((NC, PAT, CW), F32),
        vm((NC, IMG, PAT, CW), BF16),
        vm((2, TOK, KB), BF16),
        vm((2, MY, FW, TOK), BF16),
        vm((KB, TOK), F32),
        vm((2, MY, FW, TOK), F32),
        vm((NC, DP, KS, CW), BF16),
        vm((NC, 2, KS, CW), BF16),
        vm((NC, KS, CW), BF16),
        vm((NC, KS, CW), BF16),
        vm((2, MY, FW, TOK), BF16),
        vm((2, 3, 2, FW, TOK), BF16),
        vm((2, FW, TOK), BF16),
        vm((2, FW, TOK), BF16),
        vm((2, TOK), F32),
        vm((7, 2, TOK), F32),
        vm((7, 2, TOK), F32),
        vm((2, TOK), F32),
        vm((2, TOK), F32),
        vm((7, 2, TOK), F32),
        vm((2, TOK), F32),
        vm((7, 2, TOK), F32),
        vm((PAT, CW), BF16),
        vm((DP, PAT, 2 * CW), BF16),
        vm((DP, PAT, 2 * CW), BF16),
        vm((3, PAT, 2 * CW), BF16),
        vm((4, PAT, CW), F32),
        vm((PAT, CW), F32),
        sem((3,)),
        sem((2, 7)), sem((2, 7)),
        sem((NC, 3)), sem((NC, 3)),
        sem((NC, 4)), sem((NC, 4)),
        sem((NC, 3)), sem((NC, 3)),
        sem((NC, 4)), sem((NC, 4)),
        sem((NC, 3)), sem((NC, 3)),
        sem((NC, 3)), sem((NC, 3)),
        sem((3,)), sem((3,)),
        sem((3,)), sem((3,)),
        sem((2, 3, 2)), sem((2, 3, 2)),
        sem((2,)), sem((2,)),
        sem((7,)), sem((7,)),
        sem((7,)), sem((7,)),
        sem((7,)), sem((7,)),
    ]
    whole = pl.BlockSpec(memory_space=pltpu.VMEM)
    return pl.pallas_call(
        kernel,
        out_shape=(
            jax.ShapeDtypeStruct((FW, TOK), BF16),
            jax.ShapeDtypeStruct((FW, TOK), BF16),
            jax.ShapeDtypeStruct((NC, KS, CW), BF16),
        ),
        in_specs=[whole] * 3,
        out_specs=(whole,) * 3,
        scratch_shapes=scratch,
        compiler_params=pltpu.CompilerParams(
            collective_id=0, has_side_effects=True, vmem_limit_bytes=60 * 2**20
        ),
    )(xt, ct, w)


def body(tokens, w_qkv, w_up, w_proj, w_down, cotangent):
    xt = tokens.reshape(TOK, FW).T
    ct = cotangent.reshape(TOK, FW).T
    w = jnp.concatenate(
        [
            w_down.reshape(4, CW, KS).transpose(0, 2, 1),
            w_up.reshape(KS, 4, CW).transpose(1, 0, 2),
            w_proj.T[None],
            w_qkv.transpose(1, 0, 2),
        ],
        axis=0,
    )
    upd, tgr, g = fused(xt, ct, w)
    update = upd.T.reshape(IMG, PAT, FW)
    tokens_grad = tgr.T.reshape(IMG, PAT, FW)
    g_down = g[0:4].transpose(0, 2, 1).reshape(4 * CW, KS)
    g_up = g[4:8].transpose(1, 0, 2).reshape(KS, 4 * CW)
    g_proj = g[8].T
    g_qkv = g[9:12].transpose(1, 0, 2)
    return (update, tokens_grad, g_qkv, g_up, g_proj, g_down)


def solution(mesh):
    in_specs = (
        P(None, "dp", ("mx", "my")),
        P(("mx", "dp"), None, "my"),
        P(("mx", "dp"), "my"),
        P("my", ("mx", "dp")),
        P("my", ("mx", "dp")),
        P(None, "dp", ("mx", "my")),
    )
    out_specs = (
        P(None, "dp", ("mx", "my")),
        P(None, "dp", ("mx", "my")),
        P(("mx", "dp"), None, "my"),
        P(("mx", "dp"), "my"),
        P("my", ("mx", "dp")),
        P("my", ("mx", "dp")),
    )
    return jax.shard_map(body, mesh=mesh, in_specs=in_specs, out_specs=out_specs, check_vma=False)
```

```python
import functools

import jax
import jax.numpy as jnp
from jax import lax
from jax.experimental import pallas as pl
from jax.experimental.pallas import tpu as pltpu
from jax.sharding import PartitionSpec as P

MESH = pl.DeviceIdType.MESH
F32, BF16 = jnp.float32, jnp.bfloat16

D = 6144
HD = 128
EPS = 1e-06
DP, MX, MY = 4, 8, 8
IMG, PAT = 8, 64
TOK = IMG * PAT
FW = 96
KB = MY * FW
KS = KB // DP
CW = 384
NC = 12
HEADS = CW // HD
FACTOR = HD ** (-0.5)
AG0 = 12
LAST = AG0 + NC + 4
ORDER = (0, 1, 2, 3, 8, 9, 10, 11, 4, 5, 6, 7)

NN = (((1,), (0,)), ((), ()))
NT = (((1,), (1,)), ((), ()))


def dot(a, b, dims=NN):
    return lax.dot_general(a, b, dims, preferred_element_type=F32)


def rcopy(src, dst, ssem, rsem, dev):
    return pltpu.make_async_remote_copy(
        src_ref=src, dst_ref=dst, send_sem=ssem, recv_sem=rsem, device_id=dev, device_id_type=MESH
    )


def rs_id(c):
    one = jnp.int32(1)
    ge4 = jnp.where(c >= 4, one, 0)
    ge8 = jnp.where(c >= 8, one, 0)
    return c + 4 * ge4 - 8 * ge8


def kind(i):
    return jnp.where((i < 4) | (i == 8), 0, 1).astype(jnp.int32)


def head_norm(x):
    hats, invs = [], []
    for h in range(HEADS):
        part = x[:, h * HD : (h + 1) * HD]
        cen = part - jnp.mean(part, axis=1, keepdims=True)
        inv = lax.rsqrt(jnp.mean(cen * cen, axis=1, keepdims=True) + EPS)
        hats.append(cen * inv)
        invs.append(jnp.broadcast_to(inv, cen.shape))
    return jnp.concatenate(hats, axis=1), jnp.concatenate(invs, axis=1)


def head_norm_back(up, hat, inv):
    outs = []
    for h in range(HEADS):
        s = slice(h * HD, (h + 1) * HD)
        u, n = up[:, s], hat[:, s]
        outs.append(
            inv[:, s]
            * (u - jnp.mean(u, axis=1, keepdims=True) - n * jnp.mean(u * n, axis=1, keepdims=True))
        )
    return jnp.concatenate(outs, axis=1)


def kernel(
    tok, cot, wd, wu, wp, wq, upd, tgr, gd, gu, gw, gq,
    xraw, craw, xt, ct, gout,
    wg, part, rsl, rss, br, rows, fm, ft, std, acc, gp, gc, gs, gx,
    stage, yrec, xsend, xrec, st_own, st_in, st_fin, st_tot, fs_own, fs_z, fs_mid, fs_y,
    qlow, kvg, kvp, kvr, hats, qn,
    loc_sem, wl_sem, my_ss, my_rs, w_ss, w_rs, rl_ss, rl_rs, rsh_ss, rsh_rs, al_ss, al_rs, ash_ss, ash_rs,
    g_ss, g_rs, kv_ss, kv_rs, kp_ss, kp_rs, y_ss, y_rs, x_ss, x_rs, st_ss, st_rs, fz_ss, fz_rs, fy_ss, fy_rs,
):
    dp, m, my = lax.axis_index("dp"), lax.axis_index("mx"), lax.axis_index("my")
    xh, co = dp // 2, lax.rem(dp, 2)
    xl, yy = my // 4, lax.rem(my, 4)
    dp_x = lax.rem(dp + 2, 4)
    dp_c = xh * 2 + 1 - co
    my_x = lax.rem(my + 4, 8)

    def at_dp(i):
        return {"dp": i, "mx": m, "my": my}

    def at_mx(i):
        return {"dp": dp, "mx": lax.rem(i + 16, 8), "my": my}

    def at_my(i):
        return {"dp": dp, "mx": m, "my": i}

    def y_of(k):
        return lax.rem(yy + k, 4)

    barrier = pltpu.get_barrier_semaphore()
    peers = [at_dp(lax.rem(dp + k, 4)) for k in (1, 2, 3)]
    peers += [at_mx(m + k) for k in range(1, 8)]
    peers += [at_my(lax.rem(my + k, 8)) for k in range(1, 8)]
    for p in peers:
        pl.semaphore_signal(barrier, inc=1, device_id=p, device_id_type=MESH)

    def piece(i, down, up, proj, qkv):
        if i < 4:
            return down.at[:, i * CW : (i + 1) * CW]
        if i < 8:
            return up.at[:, (i - 4) * CW : (i - 3) * CW]
        return proj if i == 8 else qkv.at[i - 9]

    own_c = pltpu.make_async_copy(cot, craw, loc_sem.at[0])
    own_x = pltpu.make_async_copy(tok, xraw, loc_sem.at[1])
    own_c.start()
    own_x.start()
    own_w = [pltpu.make_async_copy(piece(i, wd, wu, wp, wq), wg.at[i, dp], wl_sem.at[i]) for i in range(NC)]
    for i in ORDER:
        own_w[i].start()
    own_c.wait()
    ct[...] = jnp.transpose(craw[...].astype(F32), (1, 0)).astype(BF16)
    ft[0, my] = ct[...]
    own_x.wait()
    xt[...] = jnp.transpose(xraw[...].astype(F32), (1, 0)).astype(BF16)
    ft[1, my] = xt[...]
    pl.semaphore_wait(barrier, len(peers))

    def my_first(j, src):
        return rcopy(src, ft.at[j, my], my_ss.at[j, 0], my_rs.at[j, 0], at_my(my_x))

    def my_own(j, k, src):
        return rcopy(src, ft.at[j, my], my_ss.at[j, k], my_rs.at[j, k], at_my(xl * 4 + y_of(k)))

    def my_fwd(j, k):
        return rcopy(ft.at[j, my_x], ft.at[j, my_x], my_ss.at[j, 3 + k], my_rs.at[j, 3 + k], at_my(xl * 4 + y_of(k)))

    def my_wait_first(j):
        rcopy(ft.at[j, my_x], ft.at[j, my_x], my_ss.at[j, 0], my_rs.at[j, 0], at_my(my_x)).wait_recv()

    def my_wait(j):
        for k in (1, 3, 2):
            a = xl * 4 + y_of(4 - k)
            b = (1 - xl) * 4 + y_of(4 - k)
            rcopy(ft.at[j, a], ft.at[j, a], my_ss.at[j, k], my_rs.at[j, k], at_my(my_x)).wait_recv()
            rcopy(ft.at[j, b], ft.at[j, b], my_ss.at[j, 3 + k], my_rs.at[j, 3 + k], at_my(my_x)).wait_recv()

    def w_x(i):
        return rcopy(wg.at[i, dp], wg.at[i, dp], w_ss.at[i, 0], w_rs.at[i, 0], at_dp(dp_x))

    def w_c(i):
        return rcopy(wg.at[i, dp], wg.at[i, dp], w_ss.at[i, 1], w_rs.at[i, 1], at_dp(dp_c))

    def w_f(i):
        return rcopy(wg.at[i, dp_x], wg.at[i, dp_x], w_ss.at[i, 2], w_rs.at[i, 2], at_dp(dp_c))

    def w_wait(i, step, who):
        rcopy(wg.at[i, who], wg.at[i, who], w_ss.at[i, step], w_rs.at[i, step], at_dp(dp_c)).wait_recv()

    my_first(0, ct).start()
    for k in (1, 3, 2):
        my_own(0, k, ct).start()
    my_first(1, xt).start()
    for i in ORDER:
        own_w[i].wait()
        w_x(i).start()
        w_c(i).start()
    acc[...] = jnp.zeros_like(acc)
    my_wait_first(0)
    for k in (1, 3, 2):
        my_fwd(0, k).start()
    for k in (1, 3, 2):
        my_own(1, k, xt).start()
    my_wait_first(1)
    for k in (1, 3, 2):
        my_fwd(1, k).start()

    def w_forward(i):
        w_wait(i, 0, dp_x)
        w_f(i).start()

    w_forward(jnp.int32(0))
    my_wait(0)
    fm[0] = jnp.transpose(ft[0].reshape(KB, TOK), (1, 0))

    def stats_send():
        my_wait(1)
        for k in (1, 3, 2):
            my_fwd(1, k).wait_send()
        xs = ft[1].reshape(KB, TOK).astype(F32)
        std[...] = xs
        total = jnp.sum(xs, axis=0, keepdims=True)
        cen = xs - total * (1.0 / KB)
        st_own[0:1, :] = total
        st_own[1:2, :] = jnp.sum(cen * cen, axis=0, keepdims=True)
        for k in range(1, 8):
            rcopy(st_own, st_in.at[k - 1], st_ss.at[k - 1], st_rs.at[k - 1], at_mx(m + k)).start()

    def stats_done():
        for k in range(1, 8):
            rcopy(st_own, st_in.at[k - 1], st_ss.at[k - 1], st_rs.at[k - 1], at_mx(m + k)).wait()
        total = st_own[0:1, :]
        for k in range(7):
            total = total + st_in[k, 0:1, :]
        mean = total * (1.0 / D)
        spread = jnp.zeros_like(mean)
        for k in range(8):
            s, q = (st_own[0:1, :], st_own[1:2, :]) if k == 7 else (st_in[k, 0:1, :], st_in[k, 1:2, :])
            off = s * (1.0 / KB) - mean
            spread = spread + q + KB * off * off
        inv = lax.rsqrt(spread * (1.0 / D) + EPS)
        st_tot[0:1, :] = mean
        st_tot[1:2, :] = inv
        for j in range(MY):
            r = slice(j * FW, (j + 1) * FW)
            s = (std[r, :] - mean) * inv
            std[r, :] = s
            ft[1, j] = s.astype(BF16)
        fm[1] = jnp.transpose(ft[1].reshape(KB, TOK), (1, 0))

    def attn_open():
        q_hat, q_inv = head_norm(br[9])
        k_hat, k_inv = head_norm(br[10])
        hats[0], hats[1], hats[2], hats[3] = q_hat, q_inv, k_hat, k_inv
        qlow[...] = q_hat.astype(BF16)
        kvg[dp, :, :CW] = k_hat.astype(BF16)
        kvg[dp, :, CW:] = br[11].astype(BF16)
        for k in (1, 2, 3):
            rcopy(kvg.at[dp], kvg.at[dp], kv_ss.at[k - 1], kv_rs.at[k - 1], at_dp(lax.rem(dp + k, 4))).start()

    def attn_mid():
        for k in (1, 2, 3):
            s = lax.rem(dp + 4 - k, 4)
            rcopy(kvg.at[s], kvg.at[s], kv_ss.at[k - 1], kv_rs.at[k - 1], at_dp(dp_c)).wait_recv()
            rcopy(kvg.at[dp], kvg.at[dp], kv_ss.at[k - 1], kv_rs.at[k - 1], at_dp(dp_c)).wait_send()
        for h in range(HEADS):
            s = slice(h * HD, (h + 1) * HD)
            q = qlow[:, s]
            keys = kvg[:, :, s].reshape(DP * PAT, HD)
            vals = kvg[:, :, CW + h * HD : CW + (h + 1) * HD].reshape(DP * PAT, HD)
            ag = br[8, :, s].astype(BF16)
            raised = jnp.exp(dot(q, keys, NT) * FACTOR)
            probs = raised / jnp.sum(raised, axis=1, keepdims=True)
            plow = probs.astype(BF16)
            rows[8, m, :, s] = dot(plow, vals).astype(BF16)
            pgrad = dot(ag, vals, NT)
            sgrad = probs * (pgrad - jnp.sum(probs * pgrad, axis=1, keepdims=True))
            slow = (sgrad * FACTOR).astype(BF16)
            qn[:, s] = dot(slow, keys)
            vpart = dot(jnp.transpose(plow.astype(F32), (1, 0)).astype(BF16), ag)
            kpart = dot(jnp.transpose(slow.astype(F32), (1, 0)).astype(BF16), q)
            kvp[:, :, s] = kpart.astype(BF16).reshape(DP, PAT, HD)
            kvp[:, :, CW + h * HD : CW + (h + 1) * HD] = vpart.astype(BF16).reshape(DP, PAT, HD)
        for k in (1, 2, 3):
            t = lax.rem(dp + k, 4)
            rcopy(kvp.at[t], kvr.at[k - 1], kp_ss.at[k - 1], kp_rs.at[k - 1], at_dp(t)).start()

    def attn_close():
        sums = kvp[dp].astype(F32)
        for k in (1, 2, 3):
            t = lax.rem(dp + k, 4)
            rcopy(kvp.at[t], kvr.at[k - 1], kp_ss.at[k - 1], kp_rs.at[k - 1], at_dp(t)).wait()
            sums = sums + kvr[k - 1].astype(F32)
        rows[9, m] = head_norm_back(qn[...], hats[0], hats[1]).astype(BF16)
        rows[10, m] = head_norm_back(sums[:, :CW], hats[2], hats[3]).astype(BF16)
        rows[11, m] = sums[:, CW:].astype(BF16)

    def y_copy(j, k, half):
        t = half * 4 + y_of(k)
        return rcopy(
            stage.at[j, t], yrec.at[j, k - 1, half], y_ss.at[j, k - 1, half], y_rs.at[j, k - 1, half], at_my(xl * 4 + y_of(k))
        )

    def x_copy(j):
        return rcopy(xsend.at[j], xrec.at[j], x_ss.at[j], x_rs.at[j], at_my(my_x))

    def sum_open(j):
        stage[j] = acc[j].astype(BF16)
        for k in (1, 3, 2):
            for half in (0, 1):
                y_copy(j, k, half).start()

    def sum_mid(j):
        total = acc[j, my_x]
        for k in (1, 3, 2):
            for half in (0, 1):
                y_copy(j, k, half).wait()
        for k in (1, 2, 3):
            total = total + yrec[j, k - 1, 1 - xl].astype(F32)
        xsend[j] = total.astype(BF16)
        x_copy(j).start()

    def sum_close(j):
        total = acc[j, my]
        for k in (1, 2, 3):
            total = total + yrec[j, k - 1, xl].astype(F32)
        x_copy(j).wait()
        return total + xrec[j].astype(F32)

    def sign(c):
        return 1 - 2 * lax.rem(c, 2)

    def img(x):
        return lax.rem(x + 16, 8)

    def rl(c, step):
        i, g = rs_id(c), sign(c)
        b = part.at[i, img(m - g * (4 - step))]
        return rcopy(b, rsl.at[i, step], rl_ss.at[c, step], rl_rs.at[c, step], at_mx(m - g))

    def rsh(c, step):
        i, g = rs_id(c), sign(c)
        b = part.at[i, img(m + g * (3 - step))]
        return rcopy(b, rss.at[i, step], rsh_ss.at[c, step], rsh_rs.at[c, step], at_mx(m + g))

    def rs_middle(c, s):
        i, g = rs_id(c), sign(c)
        rl(c, s - 1).wait_recv()
        b = img(m - g * (4 - s))
        part[i, b] = (part[i, b].astype(F32) + rsl[i, s - 1].astype(F32)).astype(BF16)
        rl(c, s).start()
        if s <= 2:
            rsh(c, s - 1).wait_recv()
            b = img(m + g * (3 - s))
            part[i, b] = (part[i, b].astype(F32) + rss[i, s - 1].astype(F32)).astype(BF16)
            rsh(c, s).start()

    def rs_open(c):
        i = rs_id(c)
        w_wait(i, 1, dp_c)
        w_wait(i, 2, xh * 0 + 3 - dp)
        wv = wg[i].reshape(KB, CW)
        j = kind(i)
        for half in range(2):
            res = dot(fm[j, half * 256 : (half + 1) * 256, :], wv).astype(BF16)
            part[i, half * 4 : (half + 1) * 4] = res.reshape(4, PAT, CW)
        rl(c, 0).start()
        rsh(c, 0).start()

    def rs_final(c):
        i = rs_id(c)
        rl(c, 3).wait_recv()
        rsh(c, 2).wait_recv()
        br[i] = part[i, m].astype(F32) + rsl[i, 3].astype(F32) + rss[i, 2].astype(F32)

    def gelu(c):
        i = rs_id(c)
        u = br[i]
        phi = 0.5 + 0.5 * lax.erf(u * 0.7071067811865476)
        rows[i - 4, m] = (u * phi).astype(BF16)
        slope = phi + u * (0.3989422804014327 * jnp.exp(-0.5 * u * u))
        rows[i, m] = (br[i - 4] * slope).astype(BF16)

    def al(a, step):
        g = sign(a)
        b = rows.at[a, img(m + g * step)]
        return rcopy(b, b, al_ss.at[a, step], al_rs.at[a, step], at_mx(m - g))

    def ash(a, step):
        g = sign(a)
        b = rows.at[a, img(m - g * step)]
        return rcopy(b, b, ash_ss.at[a, step], ash_rs.at[a, step], at_mx(m + g))

    def al_wait(a, step):
        b = rows.at[a, img(m + sign(a) * (step + 1))]
        rcopy(b, b, al_ss.at[a, step], al_rs.at[a, step], at_mx(m + 1)).wait_recv()

    def ash_wait(a, step):
        b = rows.at[a, img(m - sign(a) * (step + 1))]
        rcopy(b, b, ash_ss.at[a, step], ash_rs.at[a, step], at_mx(m + 1)).wait_recv()

    def g_c(a, h):
        return rcopy(gp.at[a, h * 2 + 1 - co], gc.at[a, h], g_ss.at[a, h], g_rs.at[a, h], at_dp(dp_c))

    def g_x(a):
        return rcopy(gs.at[a], gx.at[a], g_ss.at[a, 2], g_rs.at[a, 2], at_dp(dp_x))

    def g_open(a):
        al_wait(a, 3)
        ash_wait(a, 2)
        r = rows[a].reshape(TOK, CW)
        j = kind(a)
        for h in range(4):
            gp[a, h] = dot(ft[j, 2 * h : 2 * h + 2].reshape(KS, TOK), r).astype(BF16)
        for h in range(2):
            g_c(a, h).start()
        for h in range(4):
            v = dot(wg[a, h], r, NT).reshape(2, FW, TOK)
            acc[j, 2 * h : 2 * h + 2] = acc[j, 2 * h : 2 * h + 2] + v

    def g_mid(a):
        for h in range(2):
            g_c(a, h).wait()
        gs[a] = (gp[a, dp_x].astype(F32) + gc[a, 1 - xh].astype(F32)).astype(BF16)
        g_x(a).start()

    def g_close(a):
        g_x(a).wait()
        gout[a] = (gp[a, dp].astype(F32) + gc[a, xh].astype(F32) + gx[a].astype(F32)).astype(BF16)

    def when_in(v, lo, hi):
        return pl.when((v >= lo) & (v < hi))

    def tick(t, _):
        for s in (3, 2, 1):
            when_in(t - s, 0, NC)(functools.partial(rs_middle, t - s, s))

        for s in (3, 2, 1):
            a = t - AG0 - s

            @when_in(a, 0, NC)
            def _(a=a, s=s):
                al_wait(a, s - 1)
                al(a, s).start()
                if s <= 2:
                    ash_wait(a, s - 1)
                    ash(a, s).start()

        @pl.when(t + 1 < NC)
        def _():
            w_forward(rs_id(t + 1))

        when_in(t, 0, NC)(functools.partial(rs_open, t))

        @when_in(t - 4, 0, NC)
        def _():
            rs_final(t - 4)

        when_in(t - 4, 8, NC)(functools.partial(gelu, t - 4))

        @when_in(t - AG0, 0, NC)
        def _():
            al(t - AG0, 0).start()
            ash(t - AG0, 0).start()

        pl.when(t == 2)(stats_send)
        pl.when(t == 4)(stats_done)
        pl.when(t == 11)(attn_open)
        pl.when(t == 13)(attn_mid)
        pl.when(t == 16)(attn_close)

        when_in(t - AG0 - 4, 0, NC)(functools.partial(g_open, t - AG0 - 4))
        when_in(t - AG0 - 5, 0, NC - 1)(functools.partial(g_mid, t - AG0 - 5))
        when_in(t - AG0 - 7, 0, NC - 3)(functools.partial(g_close, t - AG0 - 7))

        pl.when(t == AG0 + 13)(functools.partial(sum_open, 0))
        pl.when(t == AG0 + 15)(functools.partial(sum_mid, 0))

        for s in (4, 3, 2, 1):
            c = t - s

            @when_in(c, 0, NC)
            def _(c=c, s=s):
                rl(c, s - 1).wait_send()
                if s <= 3:
                    rsh(c, s - 1).wait_send()

            a = t - AG0 - s

            @when_in(a, 0, NC)
            def _(a=a, s=s):
                al(a, s - 1).wait_send()
                if s <= 3:
                    ash(a, s - 1).wait_send()

        return 0

    lax.fori_loop(0, LAST, tick, 0)

    out_copies = [pltpu.make_async_copy(gout.at[i], piece(i, gd, gu, gw, gq), wl_sem.at[i]) for i in range(NC)]
    for i in range(NC - 3):
        out_copies[i].start()
    sum_open(1)
    fsum = jnp.zeros((1, TOK), F32)
    fcross = jnp.zeros((1, TOK), F32)
    for j in range(MY):
        v = acc[1, j]
        fsum = fsum + jnp.sum(v, axis=0, keepdims=True)
        fcross = fcross + jnp.sum(v * std[j * FW : (j + 1) * FW, :], axis=0, keepdims=True)
    fs_own[0:1, :] = fsum
    fs_own[1:2, :] = fcross

    def fz(k):
        return rcopy(fs_own, fs_z.at[k - 1], fz_ss.at[k - 1], fz_rs.at[k - 1], at_mx(m + k))

    def fy(k):
        return rcopy(fs_mid, fs_y.at[k - 1], fy_ss.at[k - 1], fy_rs.at[k - 1], at_my(lax.rem(my + k, 8)))

    for k in range(1, 8):
        fz(k).start()
    g_mid(NC - 1)
    upd[...] = jnp.transpose(sum_close(0), (1, 0)).astype(BF16)
    for k in range(1, 8):
        fz(k).wait()
    tot = fs_own[...]
    for k in range(7):
        tot = tot + fs_z[k]
    fs_mid[...] = tot
    for k in range(1, 8):
        fy(k).start()
    for i in range(NC - 3, NC):
        g_close(i)
        out_copies[i].start()
    sum_mid(1)
    for k in range(1, 8):
        fy(k).wait()
    tot = fs_mid[...]
    for k in range(7):
        tot = tot + fs_y[k]
    mean_g = tot[0:1, :] * (1.0 / D)
    mean_c = tot[1:2, :] * (1.0 / D)
    fg = sum_close(1)
    own = std[pl.ds(pl.multiple_of(my * FW, FW), FW), :]
    tgr[...] = jnp.transpose(st_tot[1:2, :] * (fg - mean_g - own * mean_c), (1, 0)).astype(BF16)
    for c in out_copies:
        c.wait()

    for j, src in ((0, ct), (1, xt)):
        my_first(j, src).wait_send()
        for k in (1, 3, 2):
            my_own(j, k, src).wait_send()
    for k in (1, 3, 2):
        my_fwd(0, k).wait_send()

    def w_done(i, _):
        w_x(i).wait_send()
        w_c(i).wait_send()
        w_f(i).wait_send()
        return 0

    lax.fori_loop(0, NC, w_done, 0)


def fused(tok, cot, wd, wu, wp, wq):
    vm, sem = pltpu.VMEM, pltpu.SemaphoreType.DMA
    scratch = [
        vm((TOK, FW), BF16),
        vm((TOK, FW), BF16),
        vm((FW, TOK), BF16),
        vm((FW, TOK), BF16),
        vm((NC, KS, CW), BF16),
        vm((NC, DP, KS, CW), BF16),
        vm((NC, IMG, PAT, CW), BF16),
        vm((NC, 4, PAT, CW), BF16),
        vm((NC, 3, PAT, CW), BF16),
        vm((NC, PAT, CW), F32),
        vm((NC, IMG, PAT, CW), BF16),
        vm((2, TOK, KB), BF16),
        vm((2, MY, FW, TOK), BF16),
        vm((KB, TOK), F32),
        vm((2, MY, FW, TOK), F32),
        vm((NC, DP, KS, CW), BF16),
        vm((NC, 2, KS, CW), BF16),
        vm((NC, KS, CW), BF16),
        vm((NC, KS, CW), BF16),
        vm((2, MY, FW, TOK), BF16),
        vm((2, 3, 2, FW, TOK), BF16),
        vm((2, FW, TOK), BF16),
        vm((2, FW, TOK), BF16),
        vm((2, TOK), F32),
        vm((7, 2, TOK), F32),
        vm((7, 2, TOK), F32),
        vm((2, TOK), F32),
        vm((2, TOK), F32),
        vm((7, 2, TOK), F32),
        vm((2, TOK), F32),
        vm((7, 2, TOK), F32),
        vm((PAT, CW), BF16),
        vm((DP, PAT, 2 * CW), BF16),
        vm((DP, PAT, 2 * CW), BF16),
        vm((3, PAT, 2 * CW), BF16),
        vm((4, PAT, CW), F32),
        vm((PAT, CW), F32),
        sem((2,)), sem((NC,)),
        sem((2, 7)), sem((2, 7)),
        sem((NC, 3)), sem((NC, 3)),
        sem((NC, 4)), sem((NC, 4)),
        sem((NC, 3)), sem((NC, 3)),
        sem((NC, 4)), sem((NC, 4)),
        sem((NC, 3)), sem((NC, 3)),
        sem((NC, 3)), sem((NC, 3)),
        sem((3,)), sem((3,)),
        sem((3,)), sem((3,)),
        sem((2, 3, 2)), sem((2, 3, 2)),
        sem((2,)), sem((2,)),
        sem((7,)), sem((7,)),
        sem((7,)), sem((7,)),
        sem((7,)), sem((7,)),
    ]
    whole = pl.BlockSpec(memory_space=pltpu.VMEM)
    far = pl.BlockSpec(memory_space=pl.ANY)
    return pl.pallas_call(
        kernel,
        out_shape=(
            jax.ShapeDtypeStruct((TOK, FW), BF16),
            jax.ShapeDtypeStruct((TOK, FW), BF16),
            jax.ShapeDtypeStruct((KS, 4 * CW), BF16),
            jax.ShapeDtypeStruct((KS, 4 * CW), BF16),
            jax.ShapeDtypeStruct((KS, CW), BF16),
            jax.ShapeDtypeStruct((3, KS, CW), BF16),
        ),
        in_specs=[far] * 6,
        out_specs=(whole, whole, far, far, far, far),
        scratch_shapes=scratch,
        compiler_params=pltpu.CompilerParams(
            collective_id=0, has_side_effects=True, vmem_limit_bytes=60 * 2**20
        ),
    )(tok, cot, wd, wu, wp, wq)


def body(tokens, w_qkv, w_up, w_proj, w_down, cotangent):
    upd, tgr, gd, gu, gw, gq = fused(
        tokens.reshape(TOK, FW), cotangent.reshape(TOK, FW), w_down.T, w_up, w_proj.T, w_qkv.transpose(1, 0, 2)
    )
    shape = (IMG, PAT, FW)
    return (upd.reshape(shape), tgr.reshape(shape), gq.transpose(1, 0, 2), gu, gw.T, gd.T)


def solution(mesh):
    in_specs = (
        P(None, "dp", ("mx", "my")),
        P(("mx", "dp"), None, "my"),
        P(("mx", "dp"), "my"),
        P("my", ("mx", "dp")),
        P("my", ("mx", "dp")),
        P(None, "dp", ("mx", "my")),
    )
    out_specs = (
        P(None, "dp", ("mx", "my")),
        P(None, "dp", ("mx", "my")),
        P(("mx", "dp"), None, "my"),
        P(("mx", "dp"), "my"),
        P("my", ("mx", "dp")),
        P("my", ("mx", "dp")),
    )
    return jax.shard_map(body, mesh=mesh, in_specs=in_specs, out_specs=out_specs, check_vma=False)
```

```python
import functools

import jax
import jax.numpy as jnp
from jax import lax
from jax.experimental import pallas as pl
from jax.experimental.pallas import tpu as pltpu
from jax.sharding import PartitionSpec as P

MESH = pl.DeviceIdType.MESH
F32, BF16 = jnp.float32, jnp.bfloat16

D = 6144
HD = 128
EPS = 1e-06
DP, MX, MY = 4, 8, 8
IMG, PAT = 8, 64
TOK = IMG * PAT
HALF = PAT // 2
NP = IMG // 2
PT = 2 * PAT
FW = 96
KB = MY * FW
KS = KB // DP
CW = 384
NC = 12
HEADS = CW // HD
FACTOR = HD ** (-0.5)
AG0 = 12
LAST = AG0 + NC + 4
ORDER = (0, 1, 2, 3, 8, 9, 10, 11, 4, 5, 6, 7)

NN = (((1,), (0,)), ((), ()))
NT = (((1,), (1,)), ((), ()))


def dot(a, b, dims=NN):
    return lax.dot_general(a, b, dims, preferred_element_type=F32)


def rcopy(src, dst, ssem, rsem, dev):
    return pltpu.make_async_remote_copy(
        src_ref=src, dst_ref=dst, send_sem=ssem, recv_sem=rsem, device_id=dev, device_id_type=MESH
    )


def rs_id(c):
    one = jnp.int32(1)
    ge4 = jnp.where(c >= 4, one, 0)
    ge8 = jnp.where(c >= 8, one, 0)
    return c + 4 * ge4 - 8 * ge8


def kind(i):
    return jnp.where((i < 4) | (i == 8), 0, 1).astype(jnp.int32)


def head_norm(x):
    hats, invs = [], []
    for h in range(HEADS):
        part = x[:, h * HD : (h + 1) * HD]
        cen = part - jnp.mean(part, axis=1, keepdims=True)
        inv = lax.rsqrt(jnp.mean(cen * cen, axis=1, keepdims=True) + EPS)
        hats.append(cen * inv)
        invs.append(jnp.broadcast_to(inv, cen.shape))
    return jnp.concatenate(hats, axis=1), jnp.concatenate(invs, axis=1)


def head_norm_back(up, hat, inv):
    outs = []
    for h in range(HEADS):
        s = slice(h * HD, (h + 1) * HD)
        u, n = up[:, s], hat[:, s]
        outs.append(
            inv[:, s]
            * (u - jnp.mean(u, axis=1, keepdims=True) - n * jnp.mean(u * n, axis=1, keepdims=True))
        )
    return jnp.concatenate(outs, axis=1)


def kernel(
    tok, cot, wd, wu, wp, wq, upd, tgr, gd, gu, gw, gq,
    xraw, craw, gout,
    wg, part, rsd, rsu, br, rows, fm, ft, fl, std, acc, gp, gc, gs, gx,
    stage, yrec, xsend, xrec, st_own, st_in, st_tot, fs_own, fs_z, fs_mid, fs_y,
    qlow, kvg, kvp, kvr, hats, qn,
    loc_sem, wl_sem, my_ss, my_rs, w_ss, w_rs, rd_ss, rd_rs, ru_ss, ru_rs, ad_ss, ad_rs, au_ss, au_rs,
    g_ss, g_rs, kv_ss, kv_rs, kp_ss, kp_rs, y_ss, y_rs, x_ss, x_rs, st_ss, st_rs, fz_ss, fz_rs, fy_ss, fy_rs,
):
    dp, m, my = lax.axis_index("dp"), lax.axis_index("mx"), lax.axis_index("my")
    xh, co = dp // 2, lax.rem(dp, 2)
    xl, yy = my // 4, lax.rem(my, 4)
    dp_x = lax.rem(dp + 2, 4)
    dp_c = xh * 2 + 1 - co
    my_x = lax.rem(my + 4, 8)
    own_p = m // 2
    far_p, plus_p, minus_p = lax.rem(own_p + 2, 4), lax.rem(own_p + 1, 4), lax.rem(own_p + 3, 4)

    def at_dp(i):
        return {"dp": i, "mx": m, "my": my}

    def at_mx(i):
        return {"dp": dp, "mx": lax.rem(i + 16, 8), "my": my}

    def at_my(i):
        return {"dp": dp, "mx": m, "my": i}

    def y_of(k):
        return lax.rem(yy + k, 4)

    barrier = pltpu.get_barrier_semaphore()
    peers = [at_dp(lax.rem(dp + k, 4)) for k in (1, 2, 3)]
    peers += [at_mx(m + k) for k in range(1, 8)]
    peers += [at_my(lax.rem(my + k, 8)) for k in range(1, 8)]
    for p in peers:
        pl.semaphore_signal(barrier, inc=1, device_id=p, device_id_type=MESH)

    def piece(i, down, up, proj, qkv):
        if i < 4:
            return down.at[:, i * CW : (i + 1) * CW]
        if i < 8:
            return up.at[:, (i - 4) * CW : (i - 3) * CW]
        return proj if i == 8 else qkv.at[i - 9]

    own_c = pltpu.make_async_copy(cot, craw, loc_sem.at[0])
    own_x = pltpu.make_async_copy(tok, xraw, loc_sem.at[1])
    own_c.start()
    own_x.start()
    own_w = [pltpu.make_async_copy(piece(i, wd, wu, wp, wq), wg.at[i, dp], wl_sem.at[i]) for i in range(NC)]
    for i in ORDER:
        own_w[i].start()
    own_c.wait()
    for p in range(NP):
        ft[0, p, my] = jnp.transpose(craw[p * PT : (p + 1) * PT, :].astype(F32), (1, 0)).astype(BF16)
    own_x.wait()
    for p in range(NP):
        ft[1, p, my] = jnp.transpose(xraw[p * PT : (p + 1) * PT, :].astype(F32), (1, 0)).astype(BF16)
    pl.semaphore_wait(barrier, len(peers))

    def block(j, p, who):
        return ft.at[1, :, who] if j else ft.at[0, p, who]

    def slot(j, p):
        return NP if j else p

    def my_first(j, p):
        b, q = block(j, p, my), slot(j, p)
        return rcopy(b, b, my_ss.at[q, 0], my_rs.at[q, 0], at_my(my_x))

    def my_own(j, p, k):
        b, q = block(j, p, my), slot(j, p)
        return rcopy(b, b, my_ss.at[q, k], my_rs.at[q, k], at_my(xl * 4 + y_of(k)))

    def my_fwd(j, p, k):
        b, q = block(j, p, my_x), slot(j, p)
        return rcopy(b, b, my_ss.at[q, 3 + k], my_rs.at[q, 3 + k], at_my(xl * 4 + y_of(k)))

    def my_wait_first(j, p):
        b, q = block(j, p, my_x), slot(j, p)
        rcopy(b, b, my_ss.at[q, 0], my_rs.at[q, 0], at_my(my_x)).wait_recv()

    def my_wait(j, p):
        q = slot(j, p)
        for k in (1, 3, 2):
            a = block(j, p, xl * 4 + y_of(4 - k))
            b = block(j, p, (1 - xl) * 4 + y_of(4 - k))
            rcopy(a, a, my_ss.at[q, k], my_rs.at[q, k], at_my(my_x)).wait_recv()
            rcopy(b, b, my_ss.at[q, 3 + k], my_rs.at[q, 3 + k], at_my(my_x)).wait_recv()

    def my_sent(j, p):
        my_first(j, p).wait_send()
        for k in (1, 3, 2):
            my_own(j, p, k).wait_send()
            my_fwd(j, p, k).wait_send()

    def w_x(i):
        return rcopy(wg.at[i, dp], wg.at[i, dp], w_ss.at[i, 0], w_rs.at[i, 0], at_dp(dp_x))

    def w_c(i):
        return rcopy(wg.at[i, dp], wg.at[i, dp], w_ss.at[i, 1], w_rs.at[i, 1], at_dp(dp_c))

    def w_f(i):
        return rcopy(wg.at[i, dp_x], wg.at[i, dp_x], w_ss.at[i, 2], w_rs.at[i, 2], at_dp(dp_c))

    def w_wait(i, step, who):
        rcopy(wg.at[i, who], wg.at[i, who], w_ss.at[i, step], w_rs.at[i, step], at_dp(dp_c)).wait_recv()

    def w_forward(i):
        w_wait(i, 0, dp_x)
        w_f(i).start()

    def start_own(j, p):
        for k in (1, 3, 2):
            my_own(j, p, k).start()

    def start_fwd(j, p):
        my_wait_first(j, p)
        for k in (1, 3, 2):
            my_fwd(j, p, k).start()

    my_first(0, far_p).start()
    own_w[0].wait()
    w_x(0).start()
    w_c(0).start()
    start_own(0, far_p)
    for p in (plus_p, minus_p, own_p):
        my_first(0, p).start()
    own_w[1].wait()
    w_x(1).start()
    w_c(1).start()
    start_own(0, plus_p)
    start_fwd(0, far_p)
    start_own(0, minus_p)
    start_fwd(0, plus_p)
    my_first(1, 0).start()
    for i in ORDER[2:]:
        own_w[i].wait()
        w_x(i).start()
        w_c(i).start()
    start_own(0, own_p)
    start_fwd(0, minus_p)
    start_fwd(0, own_p)
    start_own(1, 0)
    acc[...] = jnp.zeros_like(acc)
    w_forward(jnp.int32(0))

    def cot_pair(p):
        my_wait(0, p)
        v = ft[0, p].reshape(KB, PT)
        fm[0, p] = jnp.transpose(v.astype(F32), (1, 0)).astype(BF16)

    def stats_send():
        my_wait(1, 0)
        my_sent(1, 0)
        for p in range(NP):
            xs = ft[1, p].reshape(KB, PT).astype(F32)
            std[p] = xs
            total = jnp.sum(xs, axis=0, keepdims=True)
            cen = xs - total * (1.0 / KB)
            st_own[0:1, p * PT : (p + 1) * PT] = total
            st_own[1:2, p * PT : (p + 1) * PT] = jnp.sum(cen * cen, axis=0, keepdims=True)
            fl[0, :, p * PT : (p + 1) * PT] = ft[0, p].reshape(KB, PT)
        for k in range(1, 8):
            rcopy(st_own, st_in.at[k - 1], st_ss.at[k - 1], st_rs.at[k - 1], at_mx(m + k)).start()

    def stats_done():
        for k in range(1, 8):
            rcopy(st_own, st_in.at[k - 1], st_ss.at[k - 1], st_rs.at[k - 1], at_mx(m + k)).wait()
        total = st_own[0:1, :]
        for k in range(7):
            total = total + st_in[k, 0:1, :]
        mean = total * (1.0 / D)
        spread = jnp.zeros_like(mean)
        for k in range(8):
            s, q = (st_own[0:1, :], st_own[1:2, :]) if k == 7 else (st_in[k, 0:1, :], st_in[k, 1:2, :])
            off = s * (1.0 / KB) - mean
            spread = spread + q + KB * off * off
        inv = lax.rsqrt(spread * (1.0 / D) + EPS)
        st_tot[...] = inv
        for p in range(NP):
            c = slice(p * PT, (p + 1) * PT)
            v = (std[p] - mean[:, c]) * inv[:, c]
            std[p] = v
            fl[1, :, c] = v.astype(BF16)
            fm[1, p] = jnp.transpose(v, (1, 0)).astype(BF16)

    def attn_open():
        q_hat, q_inv = head_norm(br[9])
        k_hat, k_inv = head_norm(br[10])
        hats[0], hats[1], hats[2], hats[3] = q_hat, q_inv, k_hat, k_inv
        qlow[...] = q_hat.astype(BF16)
        kvg[dp, :, :CW] = k_hat.astype(BF16)
        kvg[dp, :, CW:] = br[11].astype(BF16)
        for k in (1, 2, 3):
            rcopy(kvg.at[dp], kvg.at[dp], kv_ss.at[k - 1], kv_rs.at[k - 1], at_dp(lax.rem(dp + k, 4))).start()

    def attn_mid():
        for k in (1, 2, 3):
            s = lax.rem(dp + 4 - k, 4)
            rcopy(kvg.at[s], kvg.at[s], kv_ss.at[k - 1], kv_rs.at[k - 1], at_dp(dp_c)).wait_recv()
            rcopy(kvg.at[dp], kvg.at[dp], kv_ss.at[k - 1], kv_rs.at[k - 1], at_dp(dp_c)).wait_send()
        for h in range(HEADS):
            s = slice(h * HD, (h + 1) * HD)
            q = qlow[:, s]
            keys = kvg[:, :, s].reshape(DP * PAT, HD)
            vals = kvg[:, :, CW + h * HD : CW + (h + 1) * HD].reshape(DP * PAT, HD)
            ag = br[8, :, s].astype(BF16)
            raised = jnp.exp(dot(q, keys, NT) * FACTOR)
            probs = raised / jnp.sum(raised, axis=1, keepdims=True)
            plow = probs.astype(BF16)
            rows[8, m, :, s] = dot(plow, vals).astype(BF16)
            pgrad = dot(ag, vals, NT)
            sgrad = probs * (pgrad - jnp.sum(probs * pgrad, axis=1, keepdims=True))
            slow = (sgrad * FACTOR).astype(BF16)
            qn[:, s] = dot(slow, keys)
            vpart = dot(jnp.transpose(plow.astype(F32), (1, 0)).astype(BF16), ag)
            kpart = dot(jnp.transpose(slow.astype(F32), (1, 0)).astype(BF16), q)
            kvp[:, :, s] = kpart.astype(BF16).reshape(DP, PAT, HD)
            kvp[:, :, CW + h * HD : CW + (h + 1) * HD] = vpart.astype(BF16).reshape(DP, PAT, HD)
        for k in (1, 2, 3):
            t = lax.rem(dp + k, 4)
            rcopy(kvp.at[t], kvr.at[k - 1], kp_ss.at[k - 1], kp_rs.at[k - 1], at_dp(t)).start()

    def attn_close():
        sums = kvp[dp].astype(F32)
        for k in (1, 2, 3):
            t = lax.rem(dp + k, 4)
            rcopy(kvp.at[t], kvr.at[k - 1], kp_ss.at[k - 1], kp_rs.at[k - 1], at_dp(t)).wait()
            sums = sums + kvr[k - 1].astype(F32)
        rows[9, m] = head_norm_back(qn[...], hats[0], hats[1]).astype(BF16)
        rows[10, m] = head_norm_back(sums[:, :CW], hats[2], hats[3]).astype(BF16)
        rows[11, m] = sums[:, CW:].astype(BF16)

    def y_copy(j, p, k):
        return rcopy(
            stage.at[j, p, y_of(k)], yrec.at[j, p, k - 1], y_ss.at[j, p, k - 1], y_rs.at[j, p, k - 1], at_my(xl * 4 + y_of(k))
        )

    def x_copy(j, p):
        return rcopy(xsend.at[j, p], xrec.at[j, p], x_ss.at[j, p], x_rs.at[j, p], at_my(my_x))

    def sum_open(j, p):
        for y in range(4):
            for half in range(2):
                stage[j, p, y, half] = acc[j, p, half * 4 + y].astype(BF16)
        for k in (1, 3, 2):
            y_copy(j, p, k).start()
        if j:
            v = acc[1, p].reshape(KB, PT)
            fs_own[p, 0:1, :] = jnp.sum(v, axis=0, keepdims=True)
            fs_own[p, 1:2, :] = jnp.sum(v * std[p], axis=0, keepdims=True)

    def sum_mid(j, p):
        total = acc[j, p, my_x]
        for k in (1, 3, 2):
            y_copy(j, p, k).wait()
        for k in (1, 2, 3):
            total = total + yrec[j, p, k - 1, 1 - xl].astype(F32)
        xsend[j, p] = total.astype(BF16)
        x_copy(j, p).start()

    def sum_close(j, p):
        total = acc[j, p, my]
        for k in (1, 2, 3):
            total = total + yrec[j, p, k - 1, xl].astype(F32)
        x_copy(j, p).wait()
        return total + xrec[j, p].astype(F32)

    def img(x):
        return lax.rem(x + 16, 8)

    def halfd(ref, s):
        return ref.at[pl.ds(0, HALF)] if s == 0 else ref

    def halfu(ref, s):
        return ref.at[pl.ds(HALF, HALF)] if s == 0 else ref

    def rd(c, s):
        i = rs_id(c)
        return rcopy(
            halfd(part.at[i, img(m - 4 + s)], s), halfd(rsd.at[i, s], s), rd_ss.at[c, s], rd_rs.at[c, s], at_mx(m - 1)
        )

    def ru(c, s):
        i = rs_id(c)
        return rcopy(
            halfu(part.at[i, img(m + 4 - s)], s), halfu(rsu.at[i, s], s), ru_ss.at[c, s], ru_rs.at[c, s], at_mx(m + 1)
        )

    def rs_middle(c, s):
        i = rs_id(c)
        lo, hi = (slice(0, HALF), slice(HALF, PAT)) if s == 1 else (slice(0, PAT), slice(0, PAT))
        rd(c, s - 1).wait_recv()
        b = img(m - 4 + s)
        part[i, b, lo] = (part[i, b, lo].astype(F32) + rsd[i, s - 1, lo].astype(F32)).astype(BF16)
        rd(c, s).start()
        ru(c, s - 1).wait_recv()
        b = img(m + 4 - s)
        part[i, b, hi] = (part[i, b, hi].astype(F32) + rsu[i, s - 1, hi].astype(F32)).astype(BF16)
        ru(c, s).start()

    def rs_pair(c, p):
        i = rs_id(c)
        res = dot(fm[kind(i), p], wg[i].reshape(KB, CW)).astype(BF16)
        part[i, pl.ds(2 * p, 2)] = res.reshape(2, PAT, CW)

    def rs_open(c):
        i = rs_id(c)
        w_wait(i, 1, dp_c)
        w_wait(i, 2, 3 - dp)
        rs_pair(c, far_p)
        rd(c, 0).start()
        ru(c, 0).start()

    def rs_final(c):
        i = rs_id(c)
        rd(c, 3).wait_recv()
        ru(c, 3).wait_recv()
        br[i] = part[i, m].astype(F32) + rsd[i, 3].astype(F32) + rsu[i, 3].astype(F32)

    def gelu(c):
        i = rs_id(c)
        u = br[i]
        phi = 0.5 + 0.5 * lax.erf(u * 0.7071067811865476)
        rows[i - 4, m] = (u * phi).astype(BF16)
        slope = phi + u * (0.3989422804014327 * jnp.exp(-0.5 * u * u))
        rows[i, m] = (br[i - 4] * slope).astype(BF16)

    def ad(a, s):
        b = halfd(rows.at[a, img(m + s)], 3 - s)
        return rcopy(b, b, ad_ss.at[a, s], ad_rs.at[a, s], at_mx(m - 1))

    def au(a, s):
        b = halfu(rows.at[a, img(m - s)], 3 - s)
        return rcopy(b, b, au_ss.at[a, s], au_rs.at[a, s], at_mx(m + 1))

    def ad_wait(a, s):
        b = halfd(rows.at[a, img(m + s + 1)], 3 - s)
        rcopy(b, b, ad_ss.at[a, s], ad_rs.at[a, s], at_mx(m - 1)).wait_recv()

    def au_wait(a, s):
        b = halfu(rows.at[a, img(m - s - 1)], 3 - s)
        rcopy(b, b, au_ss.at[a, s], au_rs.at[a, s], at_mx(m + 1)).wait_recv()

    def ag_open(a):
        ad(a, 0).start()
        au(a, 0).start()

    def ag_middle(a, s):
        ad_wait(a, s - 1)
        ad(a, s).start()
        au_wait(a, s - 1)
        au(a, s).start()

    def ag_pair(a, p):
        r = rows[a, pl.ds(2 * p, 2)].reshape(PT, CW)
        j = kind(a)
        acc[j, p] = acc[j, p] + dot(wg[a].reshape(KB, CW), r, NT).reshape(MY, FW, PT)

    def g_c(a, h):
        return rcopy(gp.at[a, h * 2 + 1 - co], gc.at[a, h], g_ss.at[a, h], g_rs.at[a, h], at_dp(dp_c))

    def g_x(a):
        return rcopy(gs.at[a], gx.at[a], g_ss.at[a, 2], g_rs.at[a, 2], at_dp(dp_x))

    def ag_far(a):
        ad_wait(a, 3)
        au_wait(a, 3)
        ag_pair(a, far_p)

    def g_open(a):
        r = rows[a].reshape(TOK, CW)
        j = kind(a)
        for h in range(4):
            gp[a, h] = dot(fl[j, h * KS : (h + 1) * KS, :], r).astype(BF16)
        for h in range(2):
            g_c(a, h).start()

    def g_mid(a):
        for h in range(2):
            g_c(a, h).wait()
        gs[a] = (gp[a, dp_x].astype(F32) + gc[a, 1 - xh].astype(F32)).astype(BF16)
        g_x(a).start()

    def g_close(a):
        g_x(a).wait()
        gout[a] = (gp[a, dp].astype(F32) + gc[a, xh].astype(F32) + gx[a].astype(F32)).astype(BF16)

    def when_in(v, lo, hi):
        return pl.when((v >= lo) & (v < hi))

    def tick(t, _):
        u = t - AG0
        for s in (3, 2, 1):
            when_in(t - s, 0, NC)(functools.partial(rs_middle, t - s, s))
        for s in (3, 2, 1):
            when_in(u - s, 0, NC)(functools.partial(ag_middle, u - s, s))

        @pl.when(u == NC + 3)
        def _():
            ag_far(u - 4)
            sum_open(1, far_p)

        @pl.when(t + 1 < NC)
        def _():
            w_forward(rs_id(t + 1))

        @pl.when(t == 0)
        def _():
            cot_pair(far_p)

        when_in(t, 0, NC)(functools.partial(rs_open, t))

        @when_in(t - 4, 0, NC)
        def _():
            rs_final(t - 4)

        when_in(t - 4, 8, NC)(functools.partial(gelu, t - 4))
        when_in(u, 0, NC)(functools.partial(ag_open, u))

        @pl.when(t == 0)
        def _():
            cot_pair(plus_p)
            cot_pair(minus_p)

        @when_in(t, 0, NC)
        def _():
            rs_pair(t, plus_p)
            rs_pair(t, minus_p)

        @pl.when(t == 1)
        def _():
            cot_pair(own_p)
            start_fwd(1, 0)

        @when_in(t - 1, 0, NC)
        def _():
            rs_pair(t - 1, own_p)

        pl.when(t == 3)(stats_send)
        pl.when(t == 4)(stats_done)
        pl.when(t == 11)(attn_open)
        pl.when(t == 13)(attn_mid)
        pl.when(t == 16)(attn_close)

        when_in(u - 4, 0, NC - 1)(functools.partial(ag_far, u - 4))

        @when_in(u - 3, 0, NC)
        def _():
            ag_pair(u - 3, plus_p)
            ag_pair(u - 3, minus_p)

        when_in(u - 1, 0, NC)(functools.partial(ag_pair, u - 1, own_p))

        when_in(u - 4, 0, NC)(functools.partial(g_open, u - 4))
        when_in(u - 5, 0, NC - 1)(functools.partial(g_mid, u - 5))
        when_in(u - 7, 0, NC - 3)(functools.partial(g_close, u - 7))

        for j, a in ((0, 8), (1, NC - 1)):
            pl.when(u == a + 1)(functools.partial(sum_open, j, own_p))

            @pl.when(u == a + 3)
            def _(j=j):
                sum_open(j, plus_p)
                sum_open(j, minus_p)
                sum_mid(j, own_p)

        pl.when(u == 12)(functools.partial(sum_open, 0, far_p))

        @pl.when(u == 13)
        def _():
            sum_mid(0, plus_p)
            sum_mid(0, minus_p)

        pl.when(u == 14)(functools.partial(sum_mid, 0, far_p))

        for s in (4, 3, 2, 1):
            c = t - s

            @when_in(c, 0, NC)
            def _(c=c, s=s):
                rd(c, s - 1).wait_send()
                ru(c, s - 1).wait_send()

            a = u - s

            @when_in(a, 0, NC)
            def _(a=a, s=s):
                ad(a, s - 1).wait_send()
                au(a, s - 1).wait_send()

        return 0

    lax.fori_loop(0, LAST, tick, 0)

    def fz(k):
        return rcopy(fs_own, fs_z.at[k - 1], fz_ss.at[k - 1], fz_rs.at[k - 1], at_mx(m + k))

    def fy(k):
        return rcopy(fs_mid, fs_y.at[k - 1], fy_ss.at[k - 1], fy_rs.at[k - 1], at_my(lax.rem(my + k, 8)))

    for k in range(1, 8):
        fz(k).start()
    sum_mid(1, plus_p)
    sum_mid(1, minus_p)
    g_mid(NC - 1)
    out_copies = [pltpu.make_async_copy(gout.at[i], piece(i, gd, gu, gw, gq), wl_sem.at[i]) for i in range(NC)]
    for i in range(NC - 3):
        out_copies[i].start()
    for k in range(1, 8):
        fz(k).wait()
    tot = fs_own[...]
    for k in range(7):
        tot = tot + fs_z[k]
    fs_mid[...] = tot
    for k in range(1, 8):
        fy(k).start()
    sum_mid(1, far_p)
    for p in range(NP):
        upd[p * PT : (p + 1) * PT, :] = jnp.transpose(sum_close(0, p), (1, 0)).astype(BF16)
    for i in range(NC - 3, NC):
        g_close(i)
        out_copies[i].start()
    for k in range(1, 8):
        fy(k).wait()
    tot = fs_mid[...]
    for k in range(7):
        tot = tot + fs_y[k]
    tot = tot * (1.0 / D)
    for p in range(NP):
        own = std[p, pl.ds(pl.multiple_of(my * FW, FW), FW), :]
        grad = sum_close(1, p) - tot[p, 0:1, :] - own * tot[p, 1:2, :]
        tgr[p * PT : (p + 1) * PT, :] = jnp.transpose(st_tot[:, p * PT : (p + 1) * PT] * grad, (1, 0)).astype(BF16)
    for c in out_copies:
        c.wait()

    for p in range(NP):
        my_sent(0, p)

    def w_done(i, _):
        w_x(i).wait_send()
        w_c(i).wait_send()
        w_f(i).wait_send()
        return 0

    lax.fori_loop(0, NC, w_done, 0)


def copy_kernel(*refs):
    n = len(refs) // 2
    for i in range(n):
        refs[n + i][...] = refs[i][...]


def copied(*arrays):
    whole = pl.BlockSpec(memory_space=pltpu.VMEM)
    return pl.pallas_call(
        copy_kernel,
        out_shape=tuple(jax.ShapeDtypeStruct(a.shape, a.dtype) for a in arrays),
        in_specs=[whole] * len(arrays),
        out_specs=(whole,) * len(arrays),
        compiler_params=pltpu.CompilerParams(vmem_limit_bytes=16 * 2**20),
    )(*arrays)


def fused(tok, cot, wd, wu, wp, wq):
    vm, sem = pltpu.VMEM, pltpu.SemaphoreType.DMA
    scratch = [
        vm((TOK, FW), BF16),
        vm((TOK, FW), BF16),
        vm((NC, KS, CW), BF16),
        vm((NC, DP, KS, CW), BF16),
        vm((NC, IMG, PAT, CW), BF16),
        vm((NC, 4, PAT, CW), BF16),
        vm((NC, 4, PAT, CW), BF16),
        vm((NC, PAT, CW), F32),
        vm((NC, IMG, PAT, CW), BF16),
        vm((2, NP, PT, KB), BF16),
        vm((2, NP, MY, FW, PT), BF16),
        vm((2, KB, TOK), BF16),
        vm((NP, KB, PT), F32),
        vm((2, NP, MY, FW, PT), F32),
        vm((NC, DP, KS, CW), BF16),
        vm((NC, 2, KS, CW), BF16),
        vm((NC, KS, CW), BF16),
        vm((NC, KS, CW), BF16),
        vm((2, NP, 4, 2, FW, PT), BF16),
        vm((2, NP, 3, 2, FW, PT), BF16),
        vm((2, NP, FW, PT), BF16),
        vm((2, NP, FW, PT), BF16),
        vm((2, TOK), F32),
        vm((7, 2, TOK), F32),
        vm((1, TOK), F32),
        vm((NP, 2, PT), F32),
        vm((7, NP, 2, PT), F32),
        vm((NP, 2, PT), F32),
        vm((7, NP, 2, PT), F32),
        vm((PAT, CW), BF16),
        vm((DP, PAT, 2 * CW), BF16),
        vm((DP, PAT, 2 * CW), BF16),
        vm((3, PAT, 2 * CW), BF16),
        vm((4, PAT, CW), F32),
        vm((PAT, CW), F32),
        sem((2,)), sem((NC,)),
        sem((NP + 1, 7)), sem((NP + 1, 7)),
        sem((NC, 3)), sem((NC, 3)),
        sem((NC, 4)), sem((NC, 4)),
        sem((NC, 4)), sem((NC, 4)),
        sem((NC, 4)), sem((NC, 4)),
        sem((NC, 4)), sem((NC, 4)),
        sem((NC, 3)), sem((NC, 3)),
        sem((3,)), sem((3,)),
        sem((3,)), sem((3,)),
        sem((2, NP, 3)), sem((2, NP, 3)),
        sem((2, NP)), sem((2, NP)),
        sem((7,)), sem((7,)),
        sem((7,)), sem((7,)),
        sem((7,)), sem((7,)),
    ]
    whole = pl.BlockSpec(memory_space=pltpu.VMEM)
    far = pl.BlockSpec(memory_space=pl.ANY)
    return pl.pallas_call(
        kernel,
        out_shape=(
            jax.ShapeDtypeStruct((TOK, FW), BF16),
            jax.ShapeDtypeStruct((TOK, FW), BF16),
            jax.ShapeDtypeStruct((KS, 4 * CW), BF16),
            jax.ShapeDtypeStruct((KS, 4 * CW), BF16),
            jax.ShapeDtypeStruct((KS, CW), BF16),
            jax.ShapeDtypeStruct((3, KS, CW), BF16),
        ),
        in_specs=[far] * 6,
        out_specs=(whole, whole, far, far, far, far),
        scratch_shapes=scratch,
        compiler_params=pltpu.CompilerParams(
            collective_id=0, has_side_effects=True, vmem_limit_bytes=60 * 2**20
        ),
    )(tok, cot, wd, wu, wp, wq)


def body(tokens, w_qkv, w_up, w_proj, w_down, cotangent):
    upd, tgr, gd, gu, gw, gq = copied(
        *fused(tokens.reshape(TOK, FW), cotangent.reshape(TOK, FW), w_down.T, w_up, w_proj.T, w_qkv.transpose(1, 0, 2))
    )
    shape = (IMG, PAT, FW)
    return (upd.reshape(shape), tgr.reshape(shape), gq.transpose(1, 0, 2), gu, gw.T, gd.T)


def solution(mesh):
    in_specs = (
        P(None, "dp", ("mx", "my")),
        P(("mx", "dp"), None, "my"),
        P(("mx", "dp"), "my"),
        P("my", ("mx", "dp")),
        P("my", ("mx", "dp")),
        P(None, "dp", ("mx", "my")),
    )
    out_specs = (
        P(None, "dp", ("mx", "my")),
        P(None, "dp", ("mx", "my")),
        P(("mx", "dp"), None, "my"),
        P(("mx", "dp"), "my"),
        P("my", ("mx", "dp")),
        P("my", ("mx", "dp")),
    )
    return jax.shard_map(body, mesh=mesh, in_specs=in_specs, out_specs=out_specs, check_vma=False)
```

```python
import functools

import jax
import jax.numpy as jnp
from jax import lax
from jax.experimental import pallas as pl
from jax.experimental.pallas import tpu as pltpu
from jax.sharding import PartitionSpec as P

MESH = pl.DeviceIdType.MESH
F32, BF16 = jnp.float32, jnp.bfloat16

D = 6144
HD = 128
EPS = 1e-06
DP, MX, MY = 4, 8, 8
IMG, PAT = 8, 64
TOK = IMG * PAT
HALF = PAT // 2
NP = IMG // 2
PT = 2 * PAT
FW = 96
KB = MY * FW
KS = KB // DP
CW = 384
NC = 12
HEADS = CW // HD
FACTOR = HD ** (-0.5)
POS = NC - 1
AG0 = 11
LAST = AG0 + NC + 4
ORDER = (0, 1, 2, 3, 8, 9, 10, 11, 4, 5, 6, 7)

NN = (((1,), (0,)), ((), ()))
NT = (((1,), (1,)), ((), ()))


def dot(a, b, dims=NN):
    return lax.dot_general(a, b, dims, preferred_element_type=F32)


def rcopy(src, dst, ssem, rsem, dev):
    return pltpu.make_async_remote_copy(
        src_ref=src, dst_ref=dst, send_sem=ssem, recv_sem=rsem, device_id=dev, device_id_type=MESH
    )


def rs_id(c):
    one = jnp.int32(1)
    ge4 = jnp.where(c >= 4, one, 0)
    ge8 = jnp.where(c >= 8, one, 0)
    return c + 4 * ge4 - 8 * ge8


def kind(i):
    return jnp.where((i < 4) | (i == 8), 0, 1).astype(jnp.int32)


def head_norm(x):
    hats, invs = [], []
    for h in range(HEADS):
        part = x[:, h * HD : (h + 1) * HD]
        cen = part - jnp.mean(part, axis=1, keepdims=True)
        inv = lax.rsqrt(jnp.mean(cen * cen, axis=1, keepdims=True) + EPS)
        hats.append(cen * inv)
        invs.append(jnp.broadcast_to(inv, cen.shape))
    return jnp.concatenate(hats, axis=1), jnp.concatenate(invs, axis=1)


def head_norm_back(up, hat, inv):
    outs = []
    for h in range(HEADS):
        s = slice(h * HD, (h + 1) * HD)
        u, n = up[:, s], hat[:, s]
        outs.append(
            inv[:, s]
            * (u - jnp.mean(u, axis=1, keepdims=True) - n * jnp.mean(u * n, axis=1, keepdims=True))
        )
    return jnp.concatenate(outs, axis=1)


def kernel(
    tok, cot, wd, wu, wp, wq, upd, tgr, gd, gu, gw, gq,
    xraw, craw, gout,
    wg, part, rsd, rsu, br, rows, fm, ft, fl, std, acc, gp, gc, gs, gx,
    stage, yrec, xsend, xrec, st_own, st_in, st_tot, fs_own, fs_z, fs_mid, fs_y,
    qlow, kvg, kvp, kvr, hats, qn,
    loc_sem, wl_sem, my_ss, my_rs, w_ss, w_rs, rd_ss, rd_rs, ru_ss, ru_rs, ad_ss, ad_rs, au_ss, au_rs,
    g_ss, g_rs, kv_ss, kv_rs, kp_ss, kp_rs, y_ss, y_rs, x_ss, x_rs, st_ss, st_rs, fz_ss, fz_rs, fy_ss, fy_rs,
):
    dp, m, my = lax.axis_index("dp"), lax.axis_index("mx"), lax.axis_index("my")
    xh, co = dp // 2, lax.rem(dp, 2)
    xl, yy = my // 4, lax.rem(my, 4)
    dp_x = lax.rem(dp + 2, 4)
    dp_c = xh * 2 + 1 - co
    my_x = lax.rem(my + 4, 8)
    own_p = m // 2
    far_p, plus_p, minus_p = lax.rem(own_p + 2, 4), lax.rem(own_p + 1, 4), lax.rem(own_p + 3, 4)

    def at_dp(i):
        return {"dp": i, "mx": m, "my": my}

    def at_mx(i):
        return {"dp": dp, "mx": lax.rem(i + 16, 8), "my": my}

    def at_my(i):
        return {"dp": dp, "mx": m, "my": i}

    def y_of(k):
        return lax.rem(yy + k, 4)

    barrier = pltpu.get_barrier_semaphore()
    peers = [at_dp(lax.rem(dp + k, 4)) for k in (1, 2, 3)]
    peers += [at_mx(m + k) for k in range(1, 8)]
    peers += [at_my(lax.rem(my + k, 8)) for k in range(1, 8)]
    for p in peers:
        pl.semaphore_signal(barrier, inc=1, device_id=p, device_id_type=MESH)

    def piece(i, down, up, proj, qkv):
        if i < 4:
            return down.at[:, i * CW : (i + 1) * CW]
        if i < 8:
            return up.at[:, (i - 4) * CW : (i - 3) * CW]
        return proj if i == 8 else qkv.at[i - 9]

    own_c = pltpu.make_async_copy(cot, craw, loc_sem.at[0])
    own_x = pltpu.make_async_copy(tok, xraw, loc_sem.at[1])
    own_c.start()
    own_x.start()
    own_w = [pltpu.make_async_copy(piece(i, wd, wu, wp, wq), wg.at[i, dp], wl_sem.at[i]) for i in range(NC)]
    for i in ORDER:
        own_w[i].start()
    own_c.wait()
    for p in range(NP):
        ft[0, p, my] = jnp.transpose(craw[p * PT : (p + 1) * PT, :].astype(F32), (1, 0)).astype(BF16)
    own_x.wait()
    for p in range(NP):
        ft[1, p, my] = jnp.transpose(xraw[p * PT : (p + 1) * PT, :].astype(F32), (1, 0)).astype(BF16)
    pl.semaphore_wait(barrier, len(peers))

    def block(j, p, who):
        return ft.at[1, :, who] if j else ft.at[0, p, who]

    def slot(j, p):
        return NP if j else p

    def my_first(j, p):
        b, q = block(j, p, my), slot(j, p)
        return rcopy(b, b, my_ss.at[q, 0], my_rs.at[q, 0], at_my(my_x))

    def my_own(j, p, k):
        b, q = block(j, p, my), slot(j, p)
        return rcopy(b, b, my_ss.at[q, k], my_rs.at[q, k], at_my(xl * 4 + y_of(k)))

    def my_fwd(j, p, k):
        b, q = block(j, p, my_x), slot(j, p)
        return rcopy(b, b, my_ss.at[q, 3 + k], my_rs.at[q, 3 + k], at_my(xl * 4 + y_of(k)))

    def my_wait_first(j, p):
        b, q = block(j, p, my_x), slot(j, p)
        rcopy(b, b, my_ss.at[q, 0], my_rs.at[q, 0], at_my(my_x)).wait_recv()

    def my_wait(j, p):
        q = slot(j, p)
        for k in (1, 3, 2):
            a = block(j, p, xl * 4 + y_of(4 - k))
            b = block(j, p, (1 - xl) * 4 + y_of(4 - k))
            rcopy(a, a, my_ss.at[q, k], my_rs.at[q, k], at_my(my_x)).wait_recv()
            rcopy(b, b, my_ss.at[q, 3 + k], my_rs.at[q, 3 + k], at_my(my_x)).wait_recv()

    def my_sent(j, p):
        my_first(j, p).wait_send()
        for k in (1, 3, 2):
            my_own(j, p, k).wait_send()
            my_fwd(j, p, k).wait_send()

    def w_x(i):
        return rcopy(wg.at[i, dp], wg.at[i, dp], w_ss.at[i, 0], w_rs.at[i, 0], at_dp(dp_x))

    def w_c(i):
        return rcopy(wg.at[i, dp], wg.at[i, dp], w_ss.at[i, 1], w_rs.at[i, 1], at_dp(dp_c))

    def w_f(i):
        return rcopy(wg.at[i, dp_x], wg.at[i, dp_x], w_ss.at[i, 2], w_rs.at[i, 2], at_dp(dp_c))

    def w_wait(i, step, who):
        rcopy(wg.at[i, who], wg.at[i, who], w_ss.at[i, step], w_rs.at[i, step], at_dp(dp_c)).wait_recv()

    def w_forward(i):
        w_wait(i, 0, dp_x)
        w_f(i).start()

    def start_own(j, p):
        for k in (1, 3, 2):
            my_own(j, p, k).start()

    def start_fwd(j, p):
        my_wait_first(j, p)
        for k in (1, 3, 2):
            my_fwd(j, p, k).start()

    my_first(0, far_p).start()
    own_w[0].wait()
    w_x(0).start()
    w_c(0).start()
    start_own(0, far_p)
    for p in (plus_p, minus_p, own_p):
        my_first(0, p).start()
    own_w[1].wait()
    w_x(1).start()
    w_c(1).start()
    start_own(0, plus_p)
    start_fwd(0, far_p)
    start_own(0, minus_p)
    start_fwd(0, plus_p)
    my_first(1, 0).start()
    for i in ORDER[2:]:
        own_w[i].wait()
        w_x(i).start()
        w_c(i).start()
    start_own(0, own_p)
    start_fwd(0, minus_p)
    start_fwd(0, own_p)
    start_own(1, 0)
    acc[...] = jnp.zeros_like(acc)

    def cot_pair(p):
        my_wait(0, p)
        v = ft[0, p].reshape(KB, PT)
        fm[0, p] = jnp.transpose(v.astype(F32), (1, 0)).astype(BF16)

    def stats_send():
        my_wait(1, 0)
        my_sent(1, 0)
        for p in range(NP):
            xs = ft[1, p].reshape(KB, PT).astype(F32)
            std[p] = xs
            total = jnp.sum(xs, axis=0, keepdims=True)
            cen = xs - total * (1.0 / KB)
            st_own[0:1, p * PT : (p + 1) * PT] = total
            st_own[1:2, p * PT : (p + 1) * PT] = jnp.sum(cen * cen, axis=0, keepdims=True)
            fl[0, :, p * PT : (p + 1) * PT] = ft[0, p].reshape(KB, PT)
        for k in range(1, 8):
            rcopy(st_own, st_in.at[k - 1], st_ss.at[k - 1], st_rs.at[k - 1], at_mx(m + k)).start()

    def stats_done():
        for k in range(1, 8):
            rcopy(st_own, st_in.at[k - 1], st_ss.at[k - 1], st_rs.at[k - 1], at_mx(m + k)).wait()
        total = st_own[0:1, :]
        for k in range(7):
            total = total + st_in[k, 0:1, :]
        mean = total * (1.0 / D)
        spread = jnp.zeros_like(mean)
        for k in range(8):
            s, q = (st_own[0:1, :], st_own[1:2, :]) if k == 7 else (st_in[k, 0:1, :], st_in[k, 1:2, :])
            off = s * (1.0 / KB) - mean
            spread = spread + q + KB * off * off
        inv = lax.rsqrt(spread * (1.0 / D) + EPS)
        st_tot[...] = inv
        for p in range(NP):
            c = slice(p * PT, (p + 1) * PT)
            v = (std[p] - mean[:, c]) * inv[:, c]
            std[p] = v
            fl[1, :, c] = v.astype(BF16)
            fm[1, p] = jnp.transpose(v, (1, 0)).astype(BF16)

    def attn_open():
        q_hat, q_inv = head_norm(br[9])
        k_hat, k_inv = head_norm(br[10])
        hats[0], hats[1], hats[2], hats[3] = q_hat, q_inv, k_hat, k_inv
        qlow[...] = q_hat.astype(BF16)
        kvg[dp, :, :CW] = k_hat.astype(BF16)
        kvg[dp, :, CW:] = br[11].astype(BF16)
        for k in (1, 2, 3):
            rcopy(kvg.at[dp], kvg.at[dp], kv_ss.at[k - 1], kv_rs.at[k - 1], at_dp(lax.rem(dp + k, 4))).start()

    def attn_mid():
        for k in (1, 2, 3):
            s = lax.rem(dp + 4 - k, 4)
            rcopy(kvg.at[s], kvg.at[s], kv_ss.at[k - 1], kv_rs.at[k - 1], at_dp(dp_c)).wait_recv()
            rcopy(kvg.at[dp], kvg.at[dp], kv_ss.at[k - 1], kv_rs.at[k - 1], at_dp(dp_c)).wait_send()
        for h in range(HEADS):
            s = slice(h * HD, (h + 1) * HD)
            q = qlow[:, s]
            keys = kvg[:, :, s].reshape(DP * PAT, HD)
            vals = kvg[:, :, CW + h * HD : CW + (h + 1) * HD].reshape(DP * PAT, HD)
            ag = br[8, :, s].astype(BF16)
            raised = jnp.exp(dot(q, keys, NT) * FACTOR)
            probs = raised / jnp.sum(raised, axis=1, keepdims=True)
            plow = probs.astype(BF16)
            rows[8, m, :, s] = dot(plow, vals).astype(BF16)
            pgrad = dot(ag, vals, NT)
            sgrad = probs * (pgrad - jnp.sum(probs * pgrad, axis=1, keepdims=True))
            slow = (sgrad * FACTOR).astype(BF16)
            qn[:, s] = dot(slow, keys)
            vpart = dot(jnp.transpose(plow.astype(F32), (1, 0)).astype(BF16), ag)
            kpart = dot(jnp.transpose(slow.astype(F32), (1, 0)).astype(BF16), q)
            kvp[:, :, s] = kpart.astype(BF16).reshape(DP, PAT, HD)
            kvp[:, :, CW + h * HD : CW + (h + 1) * HD] = vpart.astype(BF16).reshape(DP, PAT, HD)
        for k in (1, 2, 3):
            t = lax.rem(dp + k, 4)
            rcopy(kvp.at[t], kvr.at[k - 1], kp_ss.at[k - 1], kp_rs.at[k - 1], at_dp(t)).start()

    def attn_close():
        sums = kvp[dp].astype(F32)
        for k in (1, 2, 3):
            t = lax.rem(dp + k, 4)
            rcopy(kvp.at[t], kvr.at[k - 1], kp_ss.at[k - 1], kp_rs.at[k - 1], at_dp(t)).wait()
            sums = sums + kvr[k - 1].astype(F32)
        rows[9, m] = head_norm_back(qn[...], hats[0], hats[1]).astype(BF16)
        rows[10, m] = head_norm_back(sums[:, :CW], hats[2], hats[3]).astype(BF16)
        rows[11, m] = sums[:, CW:].astype(BF16)

    def y_copy(j, p, k):
        return rcopy(
            stage.at[j, p, y_of(k)], yrec.at[j, p, k - 1], y_ss.at[j, p, k - 1], y_rs.at[j, p, k - 1], at_my(xl * 4 + y_of(k))
        )

    def x_copy(j, p):
        return rcopy(xsend.at[j, p], xrec.at[j, p], x_ss.at[j, p], x_rs.at[j, p], at_my(my_x))

    def sum_open(j, p):
        for y in range(4):
            for half in range(2):
                stage[j, p, y, half] = acc[j, p, half * 4 + y].astype(BF16)
        for k in (1, 3, 2):
            y_copy(j, p, k).start()
        if j:
            v = acc[1, p].reshape(KB, PT)
            fs_own[p, 0:1, :] = jnp.sum(v, axis=0, keepdims=True)
            fs_own[p, 1:2, :] = jnp.sum(v * std[p], axis=0, keepdims=True)

    def sum_mid(j, p):
        total = acc[j, p, my_x]
        for k in (1, 3, 2):
            y_copy(j, p, k).wait()
        for k in (1, 2, 3):
            total = total + yrec[j, p, k - 1, 1 - xl].astype(F32)
        xsend[j, p] = total.astype(BF16)
        x_copy(j, p).start()

    def sum_close(j, p):
        total = acc[j, p, my]
        for k in (1, 2, 3):
            total = total + yrec[j, p, k - 1, xl].astype(F32)
        x_copy(j, p).wait()
        return total + xrec[j, p].astype(F32)

    def img(x):
        return lax.rem(x + 16, 8)

    def halfd(ref, s):
        return ref.at[pl.ds(0, HALF)] if s == 0 else ref

    def halfu(ref, s):
        return ref.at[pl.ds(HALF, HALF)] if s == 0 else ref

    def rd(c, s):
        i = rs_id(c)
        return rcopy(
            halfd(part.at[i, img(m - 4 + s)], s), halfd(rsd.at[i, s], s), rd_ss.at[c, s], rd_rs.at[c, s], at_mx(m - 1)
        )

    def ru(c, s):
        i = rs_id(c)
        return rcopy(
            halfu(part.at[i, img(m + 4 - s)], s), halfu(rsu.at[i, s], s), ru_ss.at[c, s], ru_rs.at[c, s], at_mx(m + 1)
        )

    def rs_middle(c, s):
        i = rs_id(c)
        lo, hi = (slice(0, HALF), slice(HALF, PAT)) if s == 1 else (slice(0, PAT), slice(0, PAT))
        rd(c, s - 1).wait_recv()
        b = img(m - 4 + s)
        part[i, b, lo] = (part[i, b, lo].astype(F32) + rsd[i, s - 1, lo].astype(F32)).astype(BF16)
        rd(c, s).start()
        ru(c, s - 1).wait_recv()
        b = img(m + 4 - s)
        part[i, b, hi] = (part[i, b, hi].astype(F32) + rsu[i, s - 1, hi].astype(F32)).astype(BF16)
        ru(c, s).start()

    def rs_pair(c, p):
        i = rs_id(c)
        res = dot(fm[kind(i), p], wg[i].reshape(KB, CW)).astype(BF16)
        part[i, pl.ds(2 * p, 2)] = res.reshape(2, PAT, CW)

    def rs_far(c):
        i = rs_id(c)
        w_wait(i, 1, dp_c)
        w_wait(i, 2, 3 - dp)
        rs_pair(c, far_p)

    def rs_send(c):
        rd(c, 0).start()
        ru(c, 0).start()

    def rs_final(c):
        i = rs_id(c)
        rd(c, 3).wait_recv()
        ru(c, 3).wait_recv()
        br[i] = part[i, m].astype(F32) + rsd[i, 3].astype(F32) + rsu[i, 3].astype(F32)

    def gelu(c):
        i = rs_id(c)
        u = br[i]
        phi = 0.5 + 0.5 * lax.erf(u * 0.7071067811865476)
        rows[i - 4, m] = (u * phi).astype(BF16)
        slope = phi + u * (0.3989422804014327 * jnp.exp(-0.5 * u * u))
        rows[i, m] = (br[i - 4] * slope).astype(BF16)

    def ad(a, s):
        b = halfd(rows.at[a, img(m + s)], 3 - s)
        return rcopy(b, b, ad_ss.at[a, s], ad_rs.at[a, s], at_mx(m - 1))

    def au(a, s):
        b = halfu(rows.at[a, img(m - s)], 3 - s)
        return rcopy(b, b, au_ss.at[a, s], au_rs.at[a, s], at_mx(m + 1))

    def ad_wait(a, s):
        b = halfd(rows.at[a, img(m + s + 1)], 3 - s)
        rcopy(b, b, ad_ss.at[a, s], ad_rs.at[a, s], at_mx(m - 1)).wait_recv()

    def au_wait(a, s):
        b = halfu(rows.at[a, img(m - s - 1)], 3 - s)
        rcopy(b, b, au_ss.at[a, s], au_rs.at[a, s], at_mx(m + 1)).wait_recv()

    def ag_open(a):
        ad(a, 0).start()
        au(a, 0).start()

    def ag_middle(a, s):
        ad_wait(a, s - 1)
        ad(a, s).start()
        au_wait(a, s - 1)
        au(a, s).start()

    def ag_pair(a, p):
        r = rows[a, pl.ds(2 * p, 2)].reshape(PT, CW)
        j = kind(a)
        acc[j, p] = acc[j, p] + dot(wg[a].reshape(KB, CW), r, NT).reshape(MY, FW, PT)

    def g_c(a, h):
        return rcopy(gp.at[a, h * 2 + 1 - co], gc.at[a, h], g_ss.at[a, h], g_rs.at[a, h], at_dp(dp_c))

    def g_x(a):
        return rcopy(gs.at[a], gx.at[a], g_ss.at[a, 2], g_rs.at[a, 2], at_dp(dp_x))

    def ag_far(a):
        ad_wait(a, 3)
        au_wait(a, 3)
        ag_pair(a, far_p)

    def g_open(a):
        r = rows[a].reshape(TOK, CW)
        j = kind(a)
        for h in range(4):
            gp[a, h] = dot(fl[j, h * KS : (h + 1) * KS, :], r).astype(BF16)
        for h in range(2):
            g_c(a, h).start()

    def g_mid(a):
        for h in range(2):
            g_c(a, h).wait()
        gs[a] = (gp[a, dp_x].astype(F32) + gc[a, 1 - xh].astype(F32)).astype(BF16)
        g_x(a).start()

    def g_close(a):
        g_x(a).wait()
        gout[a] = (gp[a, dp].astype(F32) + gc[a, xh].astype(F32) + gx[a].astype(F32)).astype(BF16)

    def when_in(v, lo, hi):
        return pl.when((v >= lo) & (v < hi))

    def at_pos(v, step, first=0):
        @when_in(v, 0, POS)
        def _():
            def one(c, _):
                step(c)
                return 0

            lax.fori_loop(jnp.where(v == 0, first, v + 1), v + 2, one, 0)

    w_forward(jnp.int32(0))
    cot_pair(far_p)
    rs_far(jnp.int32(0))
    rs_send(jnp.int32(0))
    start_fwd(1, 0)
    w_forward(jnp.int32(1))
    rs_far(jnp.int32(1))

    def tick(t, _):
        u = t - AG0
        at_pos(t, rs_send, first=1)
        for s in (1, 2, 3):
            at_pos(t - s, functools.partial(lambda s, c: rs_middle(c, s), s))
        at_pos(t - 4, rs_final)
        when_in(t - 3, 8, NC)(functools.partial(gelu, t - 3))
        when_in(u, 0, NC)(functools.partial(ag_open, u))
        for s in (1, 2, 3):
            when_in(u - s, 0, NC)(functools.partial(ag_middle, u - s, s))

        @pl.when(u == NC + 3)
        def _():
            ag_far(u - 4)
            sum_open(1, far_p)

        @pl.when(t == 0)
        def _():
            cot_pair(plus_p)
            cot_pair(minus_p)

        @pl.when(t + 2 < NC)
        def _():
            w_forward(rs_id(t + 2))

        def sides(c):
            rs_pair(c, plus_p)
            rs_pair(c, minus_p)

        at_pos(t, sides)

        @pl.when(t == 1)
        def _():
            cot_pair(own_p)

        at_pos(t - 1, lambda c: rs_pair(c, own_p))
        pl.when(t == 3)(stats_done)

        @pl.when(t + 2 < NC)
        def _():
            rs_far(t + 2)

        pl.when(t == 2)(stats_send)
        pl.when(t == 10)(attn_open)
        pl.when(t == 12)(attn_mid)
        pl.when(t == 15)(attn_close)

        when_in(u - 4, 0, NC - 1)(functools.partial(ag_far, u - 4))

        @when_in(u - 3, 0, NC)
        def _():
            ag_pair(u - 3, plus_p)
            ag_pair(u - 3, minus_p)

        when_in(u - 1, 0, NC)(functools.partial(ag_pair, u - 1, own_p))

        when_in(u - 4, 0, NC)(functools.partial(g_open, u - 4))
        when_in(u - 5, 0, NC - 1)(functools.partial(g_mid, u - 5))
        when_in(u - 7, 0, NC - 3)(functools.partial(g_close, u - 7))

        for j, a in ((0, 8), (1, NC - 1)):
            pl.when(u == a + 1)(functools.partial(sum_open, j, own_p))

            @pl.when(u == a + 3)
            def _(j=j):
                sum_open(j, plus_p)
                sum_open(j, minus_p)
                sum_mid(j, own_p)

        pl.when(u == 12)(functools.partial(sum_open, 0, far_p))

        @pl.when(u == 13)
        def _():
            sum_mid(0, plus_p)
            sum_mid(0, minus_p)

        pl.when(u == 14)(functools.partial(sum_mid, 0, far_p))

        for s in (4, 3, 2, 1):

            def sent(c, s=s):
                rd(c, s - 1).wait_send()
                ru(c, s - 1).wait_send()

            at_pos(t - s, sent)
            a = u - s

            @when_in(a, 0, NC)
            def _(a=a, s=s):
                ad(a, s - 1).wait_send()
                au(a, s - 1).wait_send()

        return 0

    lax.fori_loop(0, LAST, tick, 0)

    def fz(k):
        return rcopy(fs_own, fs_z.at[k - 1], fz_ss.at[k - 1], fz_rs.at[k - 1], at_mx(m + k))

    def fy(k):
        return rcopy(fs_mid, fs_y.at[k - 1], fy_ss.at[k - 1], fy_rs.at[k - 1], at_my(lax.rem(my + k, 8)))

    for k in range(1, 8):
        fz(k).start()
    sum_mid(1, plus_p)
    sum_mid(1, minus_p)
    g_mid(NC - 1)
    out_copies = [pltpu.make_async_copy(gout.at[i], piece(i, gd, gu, gw, gq), wl_sem.at[i]) for i in range(NC)]
    for i in range(NC - 3):
        out_copies[i].start()
    for k in range(1, 8):
        fz(k).wait()
    tot = fs_own[...]
    for k in range(7):
        tot = tot + fs_z[k]
    fs_mid[...] = tot
    for k in range(1, 8):
        fy(k).start()
    sum_mid(1, far_p)
    for p in range(NP):
        upd[p * PT : (p + 1) * PT, :] = jnp.transpose(sum_close(0, p), (1, 0)).astype(BF16)
    for i in range(NC - 3, NC):
        g_close(i)
        out_copies[i].start()
    for k in range(1, 8):
        fy(k).wait()
    tot = fs_mid[...]
    for k in range(7):
        tot = tot + fs_y[k]
    tot = tot * (1.0 / D)
    for p in range(NP):
        own = std[p, pl.ds(pl.multiple_of(my * FW, FW), FW), :]
        grad = sum_close(1, p) - tot[p, 0:1, :] - own * tot[p, 1:2, :]
        tgr[p * PT : (p + 1) * PT, :] = jnp.transpose(st_tot[:, p * PT : (p + 1) * PT] * grad, (1, 0)).astype(BF16)
    for c in out_copies:
        c.wait()

    for p in range(NP):
        my_sent(0, p)

    def w_done(i, _):
        w_x(i).wait_send()
        w_c(i).wait_send()
        w_f(i).wait_send()
        return 0

    lax.fori_loop(0, NC, w_done, 0)


def copy_kernel(*refs):
    n = (len(refs) - 2) // 3
    src, dst, held = refs[:n], refs[n : 2 * n], refs[2 * n : 3 * n]
    sin, sout = refs[3 * n :]
    come = [pltpu.make_async_copy(src[i], held[i], sin.at[i]) for i in range(n)]
    go = [pltpu.make_async_copy(held[i], dst[i], sout.at[i]) for i in range(n)]
    for c in come:
        c.start()
    for i in range(n):
        come[i].wait()
        go[i].start()
    for c in go:
        c.wait()


def copied(*arrays):
    far = pl.BlockSpec(memory_space=pl.ANY)
    n = len(arrays)
    return pl.pallas_call(
        copy_kernel,
        out_shape=tuple(jax.ShapeDtypeStruct(a.shape, a.dtype) for a in arrays),
        in_specs=[far] * n,
        out_specs=(far,) * n,
        scratch_shapes=[pltpu.VMEM(a.shape, a.dtype) for a in arrays] + [pltpu.SemaphoreType.DMA((n,))] * 2,
        compiler_params=pltpu.CompilerParams(vmem_limit_bytes=60 * 2**20),
    )(*arrays)


def fused(tok, cot, wd, wu, wp, wq):
    vm, sem = pltpu.VMEM, pltpu.SemaphoreType.DMA
    scratch = [
        vm((TOK, FW), BF16),
        vm((TOK, FW), BF16),
        vm((NC, KS, CW), BF16),
        vm((NC, DP, KS, CW), BF16),
        vm((NC, IMG, PAT, CW), BF16),
        vm((NC, 4, PAT, CW), BF16),
        vm((NC, 4, PAT, CW), BF16),
        vm((NC, PAT, CW), F32),
        vm((NC, IMG, PAT, CW), BF16),
        vm((2, NP, PT, KB), BF16),
        vm((2, NP, MY, FW, PT), BF16),
        vm((2, KB, TOK), BF16),
        vm((NP, KB, PT), F32),
        vm((2, NP, MY, FW, PT), F32),
        vm((NC, DP, KS, CW), BF16),
        vm((NC, 2, KS, CW), BF16),
        vm((NC, KS, CW), BF16),
        vm((NC, KS, CW), BF16),
        vm((2, NP, 4, 2, FW, PT), BF16),
        vm((2, NP, 3, 2, FW, PT), BF16),
        vm((2, NP, FW, PT), BF16),
        vm((2, NP, FW, PT), BF16),
        vm((2, TOK), F32),
        vm((7, 2, TOK), F32),
        vm((1, TOK), F32),
        vm((NP, 2, PT), F32),
        vm((7, NP, 2, PT), F32),
        vm((NP, 2, PT), F32),
        vm((7, NP, 2, PT), F32),
        vm((PAT, CW), BF16),
        vm((DP, PAT, 2 * CW), BF16),
        vm((DP, PAT, 2 * CW), BF16),
        vm((3, PAT, 2 * CW), BF16),
        vm((4, PAT, CW), F32),
        vm((PAT, CW), F32),
        sem((2,)), sem((NC,)),
        sem((NP + 1, 7)), sem((NP + 1, 7)),
        sem((NC, 3)), sem((NC, 3)),
        sem((NC, 4)), sem((NC, 4)),
        sem((NC, 4)), sem((NC, 4)),
        sem((NC, 4)), sem((NC, 4)),
        sem((NC, 4)), sem((NC, 4)),
        sem((NC, 3)), sem((NC, 3)),
        sem((3,)), sem((3,)),
        sem((3,)), sem((3,)),
        sem((2, NP, 3)), sem((2, NP, 3)),
        sem((2, NP)), sem((2, NP)),
        sem((7,)), sem((7,)),
        sem((7,)), sem((7,)),
        sem((7,)), sem((7,)),
    ]
    whole = pl.BlockSpec(memory_space=pltpu.VMEM)
    far = pl.BlockSpec(memory_space=pl.ANY)
    return pl.pallas_call(
        kernel,
        out_shape=(
            jax.ShapeDtypeStruct((TOK, FW), BF16),
            jax.ShapeDtypeStruct((TOK, FW), BF16),
            jax.ShapeDtypeStruct((KS, 4 * CW), BF16),
            jax.ShapeDtypeStruct((KS, 4 * CW), BF16),
            jax.ShapeDtypeStruct((KS, CW), BF16),
            jax.ShapeDtypeStruct((3, KS, CW), BF16),
        ),
        in_specs=[far] * 6,
        out_specs=(whole, whole, far, far, far, far),
        scratch_shapes=scratch,
        compiler_params=pltpu.CompilerParams(
            collective_id=0, has_side_effects=True, vmem_limit_bytes=60 * 2**20
        ),
    )(tok, cot, wd, wu, wp, wq)


def body(tokens, w_qkv, w_up, w_proj, w_down, cotangent):
    upd, tgr, gd, gu, gw, gq = copied(
        *fused(tokens.reshape(TOK, FW), cotangent.reshape(TOK, FW), w_down.T, w_up, w_proj.T, w_qkv.transpose(1, 0, 2))
    )
    shape = (IMG, PAT, FW)
    return (upd.reshape(shape), tgr.reshape(shape), gq.transpose(1, 0, 2), gu, gw.T, gd.T)


def solution(mesh):
    in_specs = (
        P(None, "dp", ("mx", "my")),
        P(("mx", "dp"), None, "my"),
        P(("mx", "dp"), "my"),
        P("my", ("mx", "dp")),
        P("my", ("mx", "dp")),
        P(None, "dp", ("mx", "my")),
    )
    out_specs = (
        P(None, "dp", ("mx", "my")),
        P(None, "dp", ("mx", "my")),
        P(("mx", "dp"), None, "my"),
        P(("mx", "dp"), "my"),
        P("my", ("mx", "dp")),
        P("my", ("mx", "dp")),
    )
    return jax.shard_map(body, mesh=mesh, in_specs=in_specs, out_specs=out_specs, check_vma=False)
```

```python
import functools

import jax
import jax.numpy as jnp
from jax import lax
from jax.experimental import pallas as pl
from jax.experimental.pallas import tpu as pltpu
from jax.sharding import PartitionSpec as P

MESH = pl.DeviceIdType.MESH
F32, BF16 = jnp.float32, jnp.bfloat16

D = 6144
HD = 128
EPS = 1e-06
DP, MX, MY = 4, 8, 8
IMG, PAT = 8, 64
TOK = IMG * PAT
HALF = PAT // 2
NP = IMG // 2
PT = 2 * PAT
FW = 96
KB = MY * FW
KS = KB // DP
CW = 384
NC = 12
HEADS = CW // HD
FACTOR = HD ** (-0.5)
POS = NC - 1
AG0 = 12
LAST = AG0 + NC + 3
ORDER = (0, 1, 2, 3, 8, 9, 10, 11, 4, 5, 6, 7)

NN = (((1,), (0,)), ((), ()))
NT = (((1,), (1,)), ((), ()))


def dot(a, b, dims=NN):
    return lax.dot_general(a, b, dims, preferred_element_type=F32)


def rcopy(src, dst, ssem, rsem, dev):
    return pltpu.make_async_remote_copy(
        src_ref=src, dst_ref=dst, send_sem=ssem, recv_sem=rsem, device_id=dev, device_id_type=MESH
    )


def rs_id(c):
    one = jnp.int32(1)
    ge4 = jnp.where(c >= 4, one, 0)
    ge8 = jnp.where(c >= 8, one, 0)
    return c + 4 * ge4 - 8 * ge8


def kind(i):
    return jnp.where((i < 4) | (i == 8), 0, 1).astype(jnp.int32)


def head_norm(x):
    hats, invs = [], []
    for h in range(HEADS):
        part = x[:, h * HD : (h + 1) * HD]
        cen = part - jnp.mean(part, axis=1, keepdims=True)
        inv = lax.rsqrt(jnp.mean(cen * cen, axis=1, keepdims=True) + EPS)
        hats.append(cen * inv)
        invs.append(jnp.broadcast_to(inv, cen.shape))
    return jnp.concatenate(hats, axis=1), jnp.concatenate(invs, axis=1)


def head_norm_back(up, hat, inv):
    outs = []
    for h in range(HEADS):
        s = slice(h * HD, (h + 1) * HD)
        u, n = up[:, s], hat[:, s]
        outs.append(
            inv[:, s]
            * (u - jnp.mean(u, axis=1, keepdims=True) - n * jnp.mean(u * n, axis=1, keepdims=True))
        )
    return jnp.concatenate(outs, axis=1)


def kernel(
    tok, cot, wd, wu, wp, wq, upd, tgr, gd, gu, gw, gq,
    xraw, craw, gout,
    wg, part, rsd, rsu, br, rows, fm, ft, fl, std, acc, gp, gc, gs, gx,
    stage, yrec, xsend, xrec, st_own, st_in, st_tot, fs_own, fs_z, fs_mid, fs_y,
    qlow, kvg, kvp, kvr, hats, qn,
    loc_sem, wl_sem, my_ss, my_rs, w_ss, w_rs, rd_ss, rd_rs, ru_ss, ru_rs, ad_ss, ad_rs, au_ss, au_rs,
    g_ss, g_rs, kv_ss, kv_rs, kp_ss, kp_rs, y_ss, y_rs, x_ss, x_rs, st_ss, st_rs, fz_ss, fz_rs, fy_ss, fy_rs,
):
    dp, m, my = lax.axis_index("dp"), lax.axis_index("mx"), lax.axis_index("my")
    xh, co = dp // 2, lax.rem(dp, 2)
    xl, yy = my // 4, lax.rem(my, 4)
    dp_x = lax.rem(dp + 2, 4)
    dp_c = xh * 2 + 1 - co
    my_x = lax.rem(my + 4, 8)
    own_p = m // 2
    far_p, plus_p, minus_p = lax.rem(own_p + 2, 4), lax.rem(own_p + 1, 4), lax.rem(own_p + 3, 4)

    def at_dp(i):
        return {"dp": i, "mx": m, "my": my}

    def at_mx(i):
        return {"dp": dp, "mx": lax.rem(i + 16, 8), "my": my}

    def at_my(i):
        return {"dp": dp, "mx": m, "my": i}

    def y_of(k):
        return lax.rem(yy + k, 4)

    barrier = pltpu.get_barrier_semaphore()
    peers = [at_dp(lax.rem(dp + k, 4)) for k in (1, 2, 3)]
    peers += [at_mx(m + k) for k in range(1, 8)]
    peers += [at_my(lax.rem(my + k, 8)) for k in range(1, 8)]
    for p in peers:
        pl.semaphore_signal(barrier, inc=1, device_id=p, device_id_type=MESH)

    def piece(i, down, up, proj, qkv):
        if i < 4:
            return down.at[:, i * CW : (i + 1) * CW]
        if i < 8:
            return up.at[:, (i - 4) * CW : (i - 3) * CW]
        return proj if i == 8 else qkv.at[i - 9]

    own_c = pltpu.make_async_copy(cot, craw, loc_sem.at[0])
    own_x = pltpu.make_async_copy(tok, xraw, loc_sem.at[1])
    own_c.start()
    own_x.start()
    own_w = [pltpu.make_async_copy(piece(i, wd, wu, wp, wq), wg.at[i, dp], wl_sem.at[i]) for i in range(NC)]
    for i in ORDER:
        own_w[i].start()
    own_c.wait()
    for p in range(NP):
        ft[0, p, my] = jnp.transpose(craw[p * PT : (p + 1) * PT, :].astype(F32), (1, 0)).astype(BF16)
    own_x.wait()
    for p in range(NP):
        ft[1, p, my] = jnp.transpose(xraw[p * PT : (p + 1) * PT, :].astype(F32), (1, 0)).astype(BF16)
    pl.semaphore_wait(barrier, len(peers))

    def block(j, p, who):
        return ft.at[1, :, who] if j else ft.at[0, p, who]

    def slot(j, p):
        return NP if j else p

    def my_first(j, p):
        b, q = block(j, p, my), slot(j, p)
        return rcopy(b, b, my_ss.at[q, 0], my_rs.at[q, 0], at_my(my_x))

    def my_own(j, p, k):
        b, q = block(j, p, my), slot(j, p)
        return rcopy(b, b, my_ss.at[q, k], my_rs.at[q, k], at_my(xl * 4 + y_of(k)))

    def my_fwd(j, p, k):
        b, q = block(j, p, my_x), slot(j, p)
        return rcopy(b, b, my_ss.at[q, 3 + k], my_rs.at[q, 3 + k], at_my(xl * 4 + y_of(k)))

    def my_wait_first(j, p):
        b, q = block(j, p, my_x), slot(j, p)
        rcopy(b, b, my_ss.at[q, 0], my_rs.at[q, 0], at_my(my_x)).wait_recv()

    def my_wait(j, p):
        q = slot(j, p)
        for k in (1, 3, 2):
            a = block(j, p, xl * 4 + y_of(4 - k))
            b = block(j, p, (1 - xl) * 4 + y_of(4 - k))
            rcopy(a, a, my_ss.at[q, k], my_rs.at[q, k], at_my(my_x)).wait_recv()
            rcopy(b, b, my_ss.at[q, 3 + k], my_rs.at[q, 3 + k], at_my(my_x)).wait_recv()

    def my_sent(j, p):
        my_first(j, p).wait_send()
        for k in (1, 3, 2):
            my_own(j, p, k).wait_send()
            my_fwd(j, p, k).wait_send()

    def w_x(i):
        return rcopy(wg.at[i, dp], wg.at[i, dp], w_ss.at[i, 0], w_rs.at[i, 0], at_dp(dp_x))

    def w_c(i):
        return rcopy(wg.at[i, dp], wg.at[i, dp], w_ss.at[i, 1], w_rs.at[i, 1], at_dp(dp_c))

    def w_f(i):
        return rcopy(wg.at[i, dp_x], wg.at[i, dp_x], w_ss.at[i, 2], w_rs.at[i, 2], at_dp(dp_c))

    def w_wait(i, step, who):
        rcopy(wg.at[i, who], wg.at[i, who], w_ss.at[i, step], w_rs.at[i, step], at_dp(dp_c)).wait_recv()

    def w_forward(i):
        w_wait(i, 0, dp_x)
        w_f(i).start()

    def start_own(j, p):
        for k in (1, 3, 2):
            my_own(j, p, k).start()

    def start_fwd(j, p):
        my_wait_first(j, p)
        for k in (1, 3, 2):
            my_fwd(j, p, k).start()

    my_first(0, far_p).start()
    own_w[0].wait()
    w_x(0).start()
    w_c(0).start()
    start_own(0, far_p)
    for p in (plus_p, minus_p, own_p):
        my_first(0, p).start()
    own_w[1].wait()
    w_x(1).start()
    w_c(1).start()
    start_own(0, plus_p)
    start_fwd(0, far_p)
    start_own(0, minus_p)
    start_fwd(0, plus_p)
    my_first(1, 0).start()
    for i in ORDER[2:]:
        own_w[i].wait()
        w_x(i).start()
        w_c(i).start()
    start_own(0, own_p)
    start_fwd(0, minus_p)
    start_fwd(0, own_p)
    start_own(1, 0)
    acc[...] = jnp.zeros_like(acc)

    def cot_pair(p):
        my_wait(0, p)
        v = ft[0, p].reshape(KB, PT)
        fm[0, p] = jnp.transpose(v.astype(F32), (1, 0)).astype(BF16)

    def stats_send():
        my_wait(1, 0)
        my_sent(1, 0)
        for p in range(NP):
            xs = ft[1, p].reshape(KB, PT).astype(F32)
            std[p] = xs
            total = jnp.sum(xs, axis=0, keepdims=True)
            cen = xs - total * (1.0 / KB)
            st_own[0:1, p * PT : (p + 1) * PT] = total
            st_own[1:2, p * PT : (p + 1) * PT] = jnp.sum(cen * cen, axis=0, keepdims=True)
            fl[0, :, p * PT : (p + 1) * PT] = ft[0, p].reshape(KB, PT)
        for k in range(1, 8):
            rcopy(st_own, st_in.at[k - 1], st_ss.at[k - 1], st_rs.at[k - 1], at_mx(m + k)).start()

    def stats_done():
        for k in range(1, 8):
            rcopy(st_own, st_in.at[k - 1], st_ss.at[k - 1], st_rs.at[k - 1], at_mx(m + k)).wait()
        total = st_own[0:1, :]
        for k in range(7):
            total = total + st_in[k, 0:1, :]
        mean = total * (1.0 / D)
        spread = jnp.zeros_like(mean)
        for k in range(8):
            s, q = (st_own[0:1, :], st_own[1:2, :]) if k == 7 else (st_in[k, 0:1, :], st_in[k, 1:2, :])
            off = s * (1.0 / KB) - mean
            spread = spread + q + KB * off * off
        inv = lax.rsqrt(spread * (1.0 / D) + EPS)
        st_tot[...] = inv
        for p in range(NP):
            c = slice(p * PT, (p + 1) * PT)
            v = (std[p] - mean[:, c]) * inv[:, c]
            std[p] = v
            fl[1, :, c] = v.astype(BF16)
            fm[1, p] = jnp.transpose(v, (1, 0)).astype(BF16)

    def attn_open():
        q_hat, q_inv = head_norm(br[9])
        k_hat, k_inv = head_norm(br[10])
        hats[0], hats[1], hats[2], hats[3] = q_hat, q_inv, k_hat, k_inv
        qlow[...] = q_hat.astype(BF16)
        kvg[dp, :, :CW] = k_hat.astype(BF16)
        kvg[dp, :, CW:] = br[11].astype(BF16)
        for k in (1, 2, 3):
            rcopy(kvg.at[dp], kvg.at[dp], kv_ss.at[k - 1], kv_rs.at[k - 1], at_dp(lax.rem(dp + k, 4))).start()

    def attn_mid():
        for k in (1, 2, 3):
            s = lax.rem(dp + 4 - k, 4)
            rcopy(kvg.at[s], kvg.at[s], kv_ss.at[k - 1], kv_rs.at[k - 1], at_dp(dp_c)).wait_recv()
            rcopy(kvg.at[dp], kvg.at[dp], kv_ss.at[k - 1], kv_rs.at[k - 1], at_dp(dp_c)).wait_send()
        for h in range(HEADS):
            s = slice(h * HD, (h + 1) * HD)
            q = qlow[:, s]
            keys = kvg[:, :, s].reshape(DP * PAT, HD)
            vals = kvg[:, :, CW + h * HD : CW + (h + 1) * HD].reshape(DP * PAT, HD)
            ag = br[8, :, s].astype(BF16)
            raised = jnp.exp(dot(q, keys, NT) * FACTOR)
            probs = raised / jnp.sum(raised, axis=1, keepdims=True)
            plow = probs.astype(BF16)
            rows[8, m, :, s] = dot(plow, vals).astype(BF16)
            pgrad = dot(ag, vals, NT)
            sgrad = probs * (pgrad - jnp.sum(probs * pgrad, axis=1, keepdims=True))
            slow = (sgrad * FACTOR).astype(BF16)
            qn[:, s] = dot(slow, keys)
            vpart = dot(jnp.transpose(plow.astype(F32), (1, 0)).astype(BF16), ag)
            kpart = dot(jnp.transpose(slow.astype(F32), (1, 0)).astype(BF16), q)
            kvp[:, :, s] = kpart.astype(BF16).reshape(DP, PAT, HD)
            kvp[:, :, CW + h * HD : CW + (h + 1) * HD] = vpart.astype(BF16).reshape(DP, PAT, HD)
        for k in (1, 2, 3):
            t = lax.rem(dp + k, 4)
            rcopy(kvp.at[t], kvr.at[k - 1], kp_ss.at[k - 1], kp_rs.at[k - 1], at_dp(t)).start()

    def attn_close():
        sums = kvp[dp].astype(F32)
        for k in (1, 2, 3):
            t = lax.rem(dp + k, 4)
            rcopy(kvp.at[t], kvr.at[k - 1], kp_ss.at[k - 1], kp_rs.at[k - 1], at_dp(t)).wait()
            sums = sums + kvr[k - 1].astype(F32)
        rows[9, m] = head_norm_back(qn[...], hats[0], hats[1]).astype(BF16)
        rows[10, m] = head_norm_back(sums[:, :CW], hats[2], hats[3]).astype(BF16)
        rows[11, m] = sums[:, CW:].astype(BF16)

    def y_copy(j, p, k):
        return rcopy(
            stage.at[j, p, y_of(k)], yrec.at[j, p, k - 1], y_ss.at[j, p, k - 1], y_rs.at[j, p, k - 1], at_my(xl * 4 + y_of(k))
        )

    def x_copy(j, p):
        return rcopy(xsend.at[j, p], xrec.at[j, p], x_ss.at[j, p], x_rs.at[j, p], at_my(my_x))

    def sum_open(j, p):
        for y in range(4):
            for half in range(2):
                stage[j, p, y, half] = acc[j, p, half * 4 + y].astype(BF16)
        for k in (1, 3, 2):
            y_copy(j, p, k).start()
        if j:
            v = acc[1, p].reshape(KB, PT)
            fs_own[p, 0:1, :] = jnp.sum(v, axis=0, keepdims=True)
            fs_own[p, 1:2, :] = jnp.sum(v * std[p], axis=0, keepdims=True)

    def sum_mid(j, p):
        total = acc[j, p, my_x]
        for k in (1, 3, 2):
            y_copy(j, p, k).wait()
        for k in (1, 2, 3):
            total = total + yrec[j, p, k - 1, 1 - xl].astype(F32)
        xsend[j, p] = total.astype(BF16)
        x_copy(j, p).start()

    def sum_close(j, p):
        total = acc[j, p, my]
        for k in (1, 2, 3):
            total = total + yrec[j, p, k - 1, xl].astype(F32)
        x_copy(j, p).wait()
        return total + xrec[j, p].astype(F32)

    def img(x):
        return lax.rem(x + 16, 8)

    def halfd(ref, s):
        return ref.at[pl.ds(0, HALF)] if s == 0 else ref

    def halfu(ref, s):
        return ref.at[pl.ds(HALF, HALF)] if s == 0 else ref

    def rd(c, s):
        i = rs_id(c)
        return rcopy(
            halfd(part.at[i, img(m - 4 + s)], s), halfd(rsd.at[i, s], s), rd_ss.at[c, s], rd_rs.at[c, s], at_mx(m - 1)
        )

    def ru(c, s):
        i = rs_id(c)
        return rcopy(
            halfu(part.at[i, img(m + 4 - s)], s), halfu(rsu.at[i, s], s), ru_ss.at[c, s], ru_rs.at[c, s], at_mx(m + 1)
        )

    def rs_middle(c, s):
        i = rs_id(c)
        lo, hi = (slice(0, HALF), slice(HALF, PAT)) if s == 1 else (slice(0, PAT), slice(0, PAT))
        rd(c, s - 1).wait_recv()
        b = img(m - 4 + s)
        part[i, b, lo] = (part[i, b, lo].astype(F32) + rsd[i, s - 1, lo].astype(F32)).astype(BF16)
        rd(c, s).start()
        ru(c, s - 1).wait_recv()
        b = img(m + 4 - s)
        part[i, b, hi] = (part[i, b, hi].astype(F32) + rsu[i, s - 1, hi].astype(F32)).astype(BF16)
        ru(c, s).start()

    def rs_pair(c, p):
        i = rs_id(c)
        res = dot(fm[kind(i), p], wg[i].reshape(KB, CW)).astype(BF16)
        part[i, pl.ds(2 * p, 2)] = res.reshape(2, PAT, CW)

    def rs_far(c):
        i = rs_id(c)
        w_wait(i, 1, dp_c)
        w_wait(i, 2, 3 - dp)
        rs_pair(c, far_p)

    def rs_send(c):
        rd(c, 0).start()
        ru(c, 0).start()

    def rs_final(c):
        i = rs_id(c)
        rd(c, 3).wait_recv()
        ru(c, 3).wait_recv()
        br[i] = part[i, m].astype(F32) + rsd[i, 3].astype(F32) + rsu[i, 3].astype(F32)

    def gelu(c):
        i = rs_id(c)
        u = br[i]
        phi = 0.5 + 0.5 * lax.erf(u * 0.7071067811865476)
        rows[i - 4, m] = (u * phi).astype(BF16)
        slope = phi + u * (0.3989422804014327 * jnp.exp(-0.5 * u * u))
        rows[i, m] = (br[i - 4] * slope).astype(BF16)

    def ad(a, s):
        b = halfd(rows.at[a, img(m + s)], 3 - s)
        return rcopy(b, b, ad_ss.at[a, s], ad_rs.at[a, s], at_mx(m - 1))

    def au(a, s):
        b = halfu(rows.at[a, img(m - s)], 3 - s)
        return rcopy(b, b, au_ss.at[a, s], au_rs.at[a, s], at_mx(m + 1))

    def ad_wait(a, s):
        b = halfd(rows.at[a, img(m + s + 1)], 3 - s)
        rcopy(b, b, ad_ss.at[a, s], ad_rs.at[a, s], at_mx(m - 1)).wait_recv()

    def au_wait(a, s):
        b = halfu(rows.at[a, img(m - s - 1)], 3 - s)
        rcopy(b, b, au_ss.at[a, s], au_rs.at[a, s], at_mx(m + 1)).wait_recv()

    def ag_open(a):
        ad(a, 0).start()
        au(a, 0).start()

    def ag_middle(a, s):
        ad_wait(a, s - 1)
        ad(a, s).start()
        au_wait(a, s - 1)
        au(a, s).start()

    def ag_pair(a, p):
        r = rows[a, pl.ds(2 * p, 2)].reshape(PT, CW)
        j = kind(a)
        acc[j, p] = acc[j, p] + dot(wg[a].reshape(KB, CW), r, NT).reshape(MY, FW, PT)

    def g_c(a, h):
        return rcopy(gp.at[a, h * 2 + 1 - co], gc.at[a, h], g_ss.at[a, h], g_rs.at[a, h], at_dp(dp_c))

    def g_x(a):
        return rcopy(gs.at[a], gx.at[a], g_ss.at[a, 2], g_rs.at[a, 2], at_dp(dp_x))

    def ag_far(a):
        ad_wait(a, 3)
        au_wait(a, 3)
        ag_pair(a, far_p)

    def g_open(a):
        r = rows[a].reshape(TOK, CW)
        j = kind(a)
        for h in range(4):
            gp[a, h] = dot(fl[j, h * KS : (h + 1) * KS, :], r).astype(BF16)
        for h in range(2):
            g_c(a, h).start()

    def g_mid(a):
        for h in range(2):
            g_c(a, h).wait()
        gs[a] = (gp[a, dp_x].astype(F32) + gc[a, 1 - xh].astype(F32)).astype(BF16)
        g_x(a).start()

    def g_close(a):
        g_x(a).wait()
        gout[a] = (gp[a, dp].astype(F32) + gc[a, xh].astype(F32) + gx[a].astype(F32)).astype(BF16)

    def when_in(v, lo, hi):
        return pl.when((v >= lo) & (v < hi))

    def at_pos(v, step, first=0):
        @when_in(v, 0, POS)
        def _():
            def one(c, _):
                step(c)
                return 0

            lax.fori_loop(jnp.where(v == 0, first, v + 1), v + 2, one, 0)

    w_forward(jnp.int32(0))
    cot_pair(far_p)
    rs_far(jnp.int32(0))
    rs_send(jnp.int32(0))
    start_fwd(1, 0)
    w_forward(jnp.int32(1))
    rs_far(jnp.int32(1))

    def tick(t, _):
        u = t - AG0

        def middle(s):
            at_pos(t - s, lambda c: rs_middle(c, s))
            when_in(u - s, 0, NC)(lambda: ag_middle(u - s, s))

        at_pos(t, rs_send, first=1)
        when_in(u, 0, NC)(lambda: ag_open(u))
        middle(1)

        @pl.when(t + 2 < NC)
        def _():
            w_forward(rs_id(t + 2))

        when_in(u - 5, 0, NC - 2)(lambda: g_mid(u - 5))
        middle(2)

        @pl.when(t == 0)
        def _():
            cot_pair(plus_p)
            cot_pair(minus_p)

        def sides(c):
            rs_pair(c, plus_p)
            rs_pair(c, minus_p)

        at_pos(t, sides)

        @pl.when(t == 1)
        def _():
            cot_pair(own_p)

        at_pos(t - 1, lambda c: rs_pair(c, own_p))
        when_in(u - 1, 0, NC)(lambda: ag_pair(u - 1, own_p))

        @when_in(u - 4, 0, NC - 1)
        def _():
            ag_pair(u - 4, plus_p)
            ag_pair(u - 4, minus_p)

        middle(3)
        pl.when(t == 3)(stats_done)

        @pl.when(t + 2 < NC)
        def _():
            rs_far(t + 2)

        when_in(u - 7, 0, NC - 4)(lambda: g_close(u - 7))
        at_pos(t - 4, rs_final)
        when_in(t - 3, 8, NC)(lambda: gelu(t - 3))
        @when_in(u - 4, 0, NC - 1)
        def _():
            ag_far(u - 4)
            g_open(u - 4)

        pl.when(t == 2)(stats_send)
        pl.when(t == 10)(attn_open)
        pl.when(t == 12)(attn_mid)
        pl.when(t == 15)(attn_close)

        pl.when(u == 9)(lambda: sum_open(0, own_p))

        @pl.when(u == 12)
        def _():
            sum_open(1, own_p)
            sum_open(0, plus_p)
            sum_open(0, minus_p)
            sum_mid(0, own_p)
            sum_open(0, far_p)

        @pl.when(u == 14)
        def _():
            sum_mid(1, own_p)
            for p in (plus_p, minus_p, far_p):
                sum_mid(0, p)

        @pl.when(u == 8)
        def _():
            for p in range(NP):
                my_sent(0, p)

        @when_in(u, 0, NC)
        def _():
            w_x(u).wait_send()
            w_c(u).wait_send()
            w_f(u).wait_send()

        for s in (4, 3, 2, 1):

            def sent(c, s=s):
                rd(c, s - 1).wait_send()
                ru(c, s - 1).wait_send()

            at_pos(t - s, sent)

            @when_in(u - s, 0, NC)
            def _(s=s):
                ad(u - s, s - 1).wait_send()
                au(u - s, s - 1).wait_send()

        return 0

    lax.fori_loop(0, LAST, tick, 0)

    def fz(k):
        return rcopy(fs_own, fs_z.at[k - 1], fz_ss.at[k - 1], fz_rs.at[k - 1], at_mx(m + k))

    def fy(k):
        return rcopy(fs_mid, fs_y.at[k - 1], fy_ss.at[k - 1], fy_rs.at[k - 1], at_my(lax.rem(my + k, 8)))

    for p in (plus_p, minus_p):
        ag_pair(NC - 1, p)
        sum_open(1, p)
    g_mid(NC - 2)
    ag_far(NC - 1)
    sum_open(1, far_p)
    for k in range(1, 8):
        fz(k).start()
    g_open(NC - 1)
    sum_mid(1, plus_p)
    sum_mid(1, minus_p)
    g_mid(NC - 1)
    for k in range(1, 8):
        fz(k).wait()
    tot = fs_own[...]
    for k in range(7):
        tot = tot + fs_z[k]
    fs_mid[...] = tot
    for k in range(1, 8):
        fy(k).start()
    sum_mid(1, far_p)
    out_copies = [pltpu.make_async_copy(gout.at[i], piece(i, gd, gu, gw, gq), wl_sem.at[i]) for i in range(NC)]
    for i in range(NC - 4):
        out_copies[i].start()
    ad(NC - 1, 3).wait_send()
    au(NC - 1, 3).wait_send()
    for p in range(NP):
        upd[p * PT : (p + 1) * PT, :] = jnp.transpose(sum_close(0, p), (1, 0)).astype(BF16)
    for i in range(NC - 4, NC):
        g_close(i)
        out_copies[i].start()
    for k in range(1, 8):
        fy(k).wait()
    tot = fs_mid[...]
    for k in range(7):
        tot = tot + fs_y[k]
    tot = tot * (1.0 / D)
    for p in range(NP):
        own = std[p, pl.ds(pl.multiple_of(my * FW, FW), FW), :]
        grad = sum_close(1, p) - tot[p, 0:1, :] - own * tot[p, 1:2, :]
        tgr[p * PT : (p + 1) * PT, :] = jnp.transpose(st_tot[:, p * PT : (p + 1) * PT] * grad, (1, 0)).astype(BF16)
    for c in out_copies:
        c.wait()


def copy_kernel(*refs):
    n = (len(refs) - 2) // 3
    src, dst, held = refs[:n], refs[n : 2 * n], refs[2 * n : 3 * n]
    sin, sout = refs[3 * n :]
    come = [pltpu.make_async_copy(src[i], held[i], sin.at[i]) for i in range(n)]
    go = [pltpu.make_async_copy(held[i], dst[i], sout.at[i]) for i in range(n)]
    for c in come:
        c.start()
    for i in range(n):
        come[i].wait()
        go[i].start()
    for c in go:
        c.wait()


def copied(*arrays):
    far = pl.BlockSpec(memory_space=pl.ANY)
    n = len(arrays)
    return pl.pallas_call(
        copy_kernel,
        out_shape=tuple(jax.ShapeDtypeStruct(a.shape, a.dtype) for a in arrays),
        in_specs=[far] * n,
        out_specs=(far,) * n,
        scratch_shapes=[pltpu.VMEM(a.shape, a.dtype) for a in arrays] + [pltpu.SemaphoreType.DMA((n,))] * 2,
        compiler_params=pltpu.CompilerParams(vmem_limit_bytes=60 * 2**20),
    )(*arrays)


def fused(tok, cot, wd, wu, wp, wq):
    vm, sem = pltpu.VMEM, pltpu.SemaphoreType.DMA
    scratch = [
        vm((TOK, FW), BF16),
        vm((TOK, FW), BF16),
        vm((NC, KS, CW), BF16),
        vm((NC, DP, KS, CW), BF16),
        vm((NC, IMG, PAT, CW), BF16),
        vm((NC, 4, PAT, CW), BF16),
        vm((NC, 4, PAT, CW), BF16),
        vm((NC, PAT, CW), F32),
        vm((NC, IMG, PAT, CW), BF16),
        vm((2, NP, PT, KB), BF16),
        vm((2, NP, MY, FW, PT), BF16),
        vm((2, KB, TOK), BF16),
        vm((NP, KB, PT), F32),
        vm((2, NP, MY, FW, PT), F32),
        vm((NC, DP, KS, CW), BF16),
        vm((NC, 2, KS, CW), BF16),
        vm((NC, KS, CW), BF16),
        vm((NC, KS, CW), BF16),
        vm((2, NP, 4, 2, FW, PT), BF16),
        vm((2, NP, 3, 2, FW, PT), BF16),
        vm((2, NP, FW, PT), BF16),
        vm((2, NP, FW, PT), BF16),
        vm((2, TOK), F32),
        vm((7, 2, TOK), F32),
        vm((1, TOK), F32),
        vm((NP, 2, PT), F32),
        vm((7, NP, 2, PT), F32),
        vm((NP, 2, PT), F32),
        vm((7, NP, 2, PT), F32),
        vm((PAT, CW), BF16),
        vm((DP, PAT, 2 * CW), BF16),
        vm((DP, PAT, 2 * CW), BF16),
        vm((3, PAT, 2 * CW), BF16),
        vm((4, PAT, CW), F32),
        vm((PAT, CW), F32),
        sem((2,)), sem((NC,)),
        sem((NP + 1, 7)), sem((NP + 1, 7)),
        sem((NC, 3)), sem((NC, 3)),
        sem((NC, 4)), sem((NC, 4)),
        sem((NC, 4)), sem((NC, 4)),
        sem((NC, 4)), sem((NC, 4)),
        sem((NC, 4)), sem((NC, 4)),
        sem((NC, 3)), sem((NC, 3)),
        sem((3,)), sem((3,)),
        sem((3,)), sem((3,)),
        sem((2, NP, 3)), sem((2, NP, 3)),
        sem((2, NP)), sem((2, NP)),
        sem((7,)), sem((7,)),
        sem((7,)), sem((7,)),
        sem((7,)), sem((7,)),
    ]
    whole = pl.BlockSpec(memory_space=pltpu.VMEM)
    far = pl.BlockSpec(memory_space=pl.ANY)
    return pl.pallas_call(
        kernel,
        out_shape=(
            jax.ShapeDtypeStruct((TOK, FW), BF16),
            jax.ShapeDtypeStruct((TOK, FW), BF16),
            jax.ShapeDtypeStruct((KS, 4 * CW), BF16),
            jax.ShapeDtypeStruct((KS, 4 * CW), BF16),
            jax.ShapeDtypeStruct((KS, CW), BF16),
            jax.ShapeDtypeStruct((3, KS, CW), BF16),
        ),
        in_specs=[far] * 6,
        out_specs=(whole, whole, far, far, far, far),
        scratch_shapes=scratch,
        compiler_params=pltpu.CompilerParams(
            collective_id=0, has_side_effects=True, vmem_limit_bytes=60 * 2**20
        ),
    )(tok, cot, wd, wu, wp, wq)


def body(tokens, w_qkv, w_up, w_proj, w_down, cotangent):
    upd, tgr, gd, gu, gw, gq = copied(
        *fused(tokens.reshape(TOK, FW), cotangent.reshape(TOK, FW), w_down.T, w_up, w_proj.T, w_qkv.transpose(1, 0, 2))
    )
    shape = (IMG, PAT, FW)
    return (upd.reshape(shape), tgr.reshape(shape), gq.transpose(1, 0, 2), gu, gw.T, gd.T)


def solution(mesh):
    in_specs = (
        P(None, "dp", ("mx", "my")),
        P(("mx", "dp"), None, "my"),
        P(("mx", "dp"), "my"),
        P("my", ("mx", "dp")),
        P("my", ("mx", "dp")),
        P(None, "dp", ("mx", "my")),
    )
    out_specs = (
        P(None, "dp", ("mx", "my")),
        P(None, "dp", ("mx", "my")),
        P(("mx", "dp"), None, "my"),
        P(("mx", "dp"), "my"),
        P("my", ("mx", "dp")),
        P("my", ("mx", "dp")),
    )
    return jax.shard_map(body, mesh=mesh, in_specs=in_specs, out_specs=out_specs, check_vma=False)
```

```python
import functools

import jax
import jax.numpy as jnp
from jax import lax
from jax.experimental import pallas as pl
from jax.experimental.pallas import tpu as pltpu
from jax.sharding import PartitionSpec as P

MESH = pl.DeviceIdType.MESH
F32, BF16 = jnp.float32, jnp.bfloat16

D = 6144
HD = 128
EPS = 1e-06
DP, MX, MY = 4, 8, 8
IMG, PAT = 8, 64
TOK = IMG * PAT
HALF = PAT // 2
NP = IMG // 2
PT = 2 * PAT
FW = 96
KB = MY * FW
KS = KB // DP
CW = 384
NC = 12
HEADS = CW // HD
FACTOR = HD ** (-0.5)
POS = NC - 1
AG0 = 12
LAST = AG0 + NC + 3
ORDER = (0, 1, 2, 3, 8, 9, 10, 11, 4, 5, 6, 7)

NN = (((1,), (0,)), ((), ()))
NT = (((1,), (1,)), ((), ()))


def dot(a, b, dims=NN):
    return lax.dot_general(a, b, dims, preferred_element_type=F32)


def rcopy(src, dst, ssem, rsem, dev):
    return pltpu.make_async_remote_copy(
        src_ref=src, dst_ref=dst, send_sem=ssem, recv_sem=rsem, device_id=dev, device_id_type=MESH
    )


def rs_id(c):
    one = jnp.int32(1)
    ge4 = jnp.where(c >= 4, one, 0)
    ge8 = jnp.where(c >= 8, one, 0)
    return c + 4 * ge4 - 8 * ge8


def kind(i):
    return jnp.where((i < 4) | (i == 8), 0, 1).astype(jnp.int32)


def head_norm(x):
    hats, invs = [], []
    for h in range(HEADS):
        part = x[:, h * HD : (h + 1) * HD]
        cen = part - jnp.mean(part, axis=1, keepdims=True)
        inv = lax.rsqrt(jnp.mean(cen * cen, axis=1, keepdims=True) + EPS)
        hats.append(cen * inv)
        invs.append(jnp.broadcast_to(inv, cen.shape))
    return jnp.concatenate(hats, axis=1), jnp.concatenate(invs, axis=1)


def head_norm_back(up, hat, inv):
    outs = []
    for h in range(HEADS):
        s = slice(h * HD, (h + 1) * HD)
        u, n = up[:, s], hat[:, s]
        outs.append(
            inv[:, s]
            * (u - jnp.mean(u, axis=1, keepdims=True) - n * jnp.mean(u * n, axis=1, keepdims=True))
        )
    return jnp.concatenate(outs, axis=1)


def kernel(
    tok, cot, wd, wu, wp, wq, upd, tgr, gd, gu, gw, gq,
    xraw, craw, gout,
    wg, part, rsd, rsu, br, rows, fm, ft, fl, std, acc, gp, gc, gs, gx,
    stage, yrec, xsend, xrec, st_own, st_in, st_tot, fs_own, fs_z, fs_mid, fs_y,
    qlow, kvg, kvp, kvr, hats, qn,
    loc_sem, wl_sem, my_ss, my_rs, w_ss, w_rs, rd_ss, rd_rs, ru_ss, ru_rs, ad_ss, ad_rs, au_ss, au_rs,
    g_ss, g_rs, kv_ss, kv_rs, kp_ss, kp_rs, y_ss, y_rs, x_ss, x_rs, st_ss, st_rs, fz_ss, fz_rs, fy_ss, fy_rs,
):
    dp, m, my = lax.axis_index("dp"), lax.axis_index("mx"), lax.axis_index("my")
    xh, co = dp // 2, lax.rem(dp, 2)
    xl, yy = my // 4, lax.rem(my, 4)
    dp_x = lax.rem(dp + 2, 4)
    dp_c = xh * 2 + 1 - co
    my_x = lax.rem(my + 4, 8)
    own_p = m // 2
    far_p, plus_p, minus_p = lax.rem(own_p + 2, 4), lax.rem(own_p + 1, 4), lax.rem(own_p + 3, 4)

    def at_dp(i):
        return {"dp": i, "mx": m, "my": my}

    def at_mx(i):
        return {"dp": dp, "mx": lax.rem(i + 16, 8), "my": my}

    def at_my(i):
        return {"dp": dp, "mx": m, "my": i}

    def y_of(k):
        return lax.rem(yy + k, 4)

    barrier = pltpu.get_barrier_semaphore()
    peers = [at_dp(lax.rem(dp + k, 4)) for k in (1, 2, 3)]
    peers += [at_mx(m + k) for k in range(1, 8)]
    peers += [at_my(lax.rem(my + k, 8)) for k in range(1, 8)]
    for p in peers:
        pl.semaphore_signal(barrier, inc=1, device_id=p, device_id_type=MESH)

    def piece(i, down, up, proj, qkv):
        if i < 4:
            return down.at[:, i * CW : (i + 1) * CW]
        if i < 8:
            return up.at[:, (i - 4) * CW : (i - 3) * CW]
        return proj if i == 8 else qkv.at[i - 9]

    own_c = pltpu.make_async_copy(cot, craw, loc_sem.at[0])
    own_x = pltpu.make_async_copy(tok, xraw, loc_sem.at[1])
    own_c.start()
    own_x.start()
    own_w = [pltpu.make_async_copy(piece(i, wd, wu, wp, wq), wg.at[i, dp], wl_sem.at[i]) for i in range(NC)]
    for i in ORDER:
        own_w[i].start()
    own_c.wait()
    for p in range(NP):
        ft[0, p, my] = jnp.transpose(craw[p * PT : (p + 1) * PT, :].astype(F32), (1, 0)).astype(BF16)
    own_x.wait()
    for p in range(NP):
        ft[1, p, my] = jnp.transpose(xraw[p * PT : (p + 1) * PT, :].astype(F32), (1, 0)).astype(BF16)
    pl.semaphore_wait(barrier, len(peers))

    def block(j, p, who):
        return ft.at[1, :, who] if j else ft.at[0, p, who]

    def slot(j, p):
        return NP if j else p

    def my_first(j, p):
        b, q = block(j, p, my), slot(j, p)
        return rcopy(b, b, my_ss.at[q, 0], my_rs.at[q, 0], at_my(my_x))

    def my_own(j, p, k):
        b, q = block(j, p, my), slot(j, p)
        return rcopy(b, b, my_ss.at[q, k], my_rs.at[q, k], at_my(xl * 4 + y_of(k)))

    def my_fwd(j, p, k):
        b, q = block(j, p, my_x), slot(j, p)
        return rcopy(b, b, my_ss.at[q, 3 + k], my_rs.at[q, 3 + k], at_my(xl * 4 + y_of(k)))

    def my_wait_first(j, p):
        b, q = block(j, p, my_x), slot(j, p)
        rcopy(b, b, my_ss.at[q, 0], my_rs.at[q, 0], at_my(my_x)).wait_recv()

    def my_wait(j, p):
        q = slot(j, p)
        for k in (1, 3, 2):
            a = block(j, p, xl * 4 + y_of(4 - k))
            b = block(j, p, (1 - xl) * 4 + y_of(4 - k))
            rcopy(a, a, my_ss.at[q, k], my_rs.at[q, k], at_my(my_x)).wait_recv()
            rcopy(b, b, my_ss.at[q, 3 + k], my_rs.at[q, 3 + k], at_my(my_x)).wait_recv()

    def my_sent(j, p):
        my_first(j, p).wait_send()
        for k in (1, 3, 2):
            my_own(j, p, k).wait_send()
            my_fwd(j, p, k).wait_send()

    def w_x(i):
        return rcopy(wg.at[i, dp], wg.at[i, dp], w_ss.at[i, 0], w_rs.at[i, 0], at_dp(dp_x))

    def w_c(i):
        return rcopy(wg.at[i, dp], wg.at[i, dp], w_ss.at[i, 1], w_rs.at[i, 1], at_dp(dp_c))

    def w_f(i):
        return rcopy(wg.at[i, dp_x], wg.at[i, dp_x], w_ss.at[i, 2], w_rs.at[i, 2], at_dp(dp_c))

    def w_wait(i, step, who):
        rcopy(wg.at[i, who], wg.at[i, who], w_ss.at[i, step], w_rs.at[i, step], at_dp(dp_c)).wait_recv()

    def w_forward(i):
        w_wait(i, 0, dp_x)
        w_f(i).start()

    def start_own(j, p):
        for k in (1, 3, 2):
            my_own(j, p, k).start()

    def start_fwd(j, p):
        my_wait_first(j, p)
        for k in (1, 3, 2):
            my_fwd(j, p, k).start()

    my_first(0, far_p).start()
    own_w[0].wait()
    w_x(0).start()
    w_c(0).start()
    start_own(0, far_p)
    for p in (plus_p, minus_p, own_p):
        my_first(0, p).start()
    own_w[1].wait()
    w_x(1).start()
    w_c(1).start()
    start_own(0, plus_p)
    start_fwd(0, far_p)
    start_own(0, minus_p)
    start_fwd(0, plus_p)
    my_first(1, 0).start()
    for i in ORDER[2:]:
        own_w[i].wait()
        w_x(i).start()
        w_c(i).start()
    start_own(0, own_p)
    start_fwd(0, minus_p)
    start_fwd(0, own_p)
    start_own(1, 0)
    acc[...] = jnp.zeros_like(acc)

    def cot_pair(p):
        my_wait(0, p)
        v = ft[0, p].reshape(KB, PT)
        fm[0, p] = jnp.transpose(v.astype(F32), (1, 0)).astype(BF16)

    def stats_send():
        my_wait(1, 0)
        my_sent(1, 0)
        for p in range(NP):
            xs = ft[1, p].reshape(KB, PT).astype(F32)
            std[p] = xs
            total = jnp.sum(xs, axis=0, keepdims=True)
            cen = xs - total * (1.0 / KB)
            st_own[0:1, p * PT : (p + 1) * PT] = total
            st_own[1:2, p * PT : (p + 1) * PT] = jnp.sum(cen * cen, axis=0, keepdims=True)
            fl[0, :, p * PT : (p + 1) * PT] = ft[0, p].reshape(KB, PT)
        for k in range(1, 8):
            rcopy(st_own, st_in.at[k - 1], st_ss.at[k - 1], st_rs.at[k - 1], at_mx(m + k)).start()

    def stats_done():
        for k in range(1, 8):
            rcopy(st_own, st_in.at[k - 1], st_ss.at[k - 1], st_rs.at[k - 1], at_mx(m + k)).wait()
        total = st_own[0:1, :]
        for k in range(7):
            total = total + st_in[k, 0:1, :]
        mean = total * (1.0 / D)
        spread = jnp.zeros_like(mean)
        for k in range(8):
            s, q = (st_own[0:1, :], st_own[1:2, :]) if k == 7 else (st_in[k, 0:1, :], st_in[k, 1:2, :])
            off = s * (1.0 / KB) - mean
            spread = spread + q + KB * off * off
        inv = lax.rsqrt(spread * (1.0 / D) + EPS)
        st_tot[...] = inv
        for p in range(NP):
            c = slice(p * PT, (p + 1) * PT)
            v = (std[p] - mean[:, c]) * inv[:, c]
            std[p] = v
            fl[1, :, c] = v.astype(BF16)
            fm[1, p] = jnp.transpose(v, (1, 0)).astype(BF16)

    def attn_open():
        q_hat, q_inv = head_norm(br[9])
        k_hat, k_inv = head_norm(br[10])
        hats[0], hats[1], hats[2], hats[3] = q_hat, q_inv, k_hat, k_inv
        qlow[...] = q_hat.astype(BF16)
        kvg[dp, :, :CW] = k_hat.astype(BF16)
        kvg[dp, :, CW:] = br[11].astype(BF16)
        for k in (1, 2, 3):
            rcopy(kvg.at[dp], kvg.at[dp], kv_ss.at[k - 1], kv_rs.at[k - 1], at_dp(lax.rem(dp + k, 4))).start()

    def attn_mid():
        for k in (1, 2, 3):
            s = lax.rem(dp + 4 - k, 4)
            rcopy(kvg.at[s], kvg.at[s], kv_ss.at[k - 1], kv_rs.at[k - 1], at_dp(dp_c)).wait_recv()
            rcopy(kvg.at[dp], kvg.at[dp], kv_ss.at[k - 1], kv_rs.at[k - 1], at_dp(dp_c)).wait_send()
        for h in range(HEADS):
            s = slice(h * HD, (h + 1) * HD)
            q = qlow[:, s]
            keys = kvg[:, :, s].reshape(DP * PAT, HD)
            vals = kvg[:, :, CW + h * HD : CW + (h + 1) * HD].reshape(DP * PAT, HD)
            ag = br[8, :, s].astype(BF16)
            raised = jnp.exp(dot(q, keys, NT) * FACTOR)
            probs = raised / jnp.sum(raised, axis=1, keepdims=True)
            plow = probs.astype(BF16)
            rows[8, m, :, s] = dot(plow, vals).astype(BF16)
            pgrad = dot(ag, vals, NT)
            sgrad = probs * (pgrad - jnp.sum(probs * pgrad, axis=1, keepdims=True))
            slow = (sgrad * FACTOR).astype(BF16)
            qn[:, s] = dot(slow, keys)
            vpart = dot(jnp.transpose(plow.astype(F32), (1, 0)).astype(BF16), ag)
            kpart = dot(jnp.transpose(slow.astype(F32), (1, 0)).astype(BF16), q)
            kvp[:, :, s] = kpart.astype(BF16).reshape(DP, PAT, HD)
            kvp[:, :, CW + h * HD : CW + (h + 1) * HD] = vpart.astype(BF16).reshape(DP, PAT, HD)
        for k in (1, 2, 3):
            t = lax.rem(dp + k, 4)
            rcopy(kvp.at[t], kvr.at[k - 1], kp_ss.at[k - 1], kp_rs.at[k - 1], at_dp(t)).start()

    def attn_close():
        sums = kvp[dp].astype(F32)
        for k in (1, 2, 3):
            t = lax.rem(dp + k, 4)
            rcopy(kvp.at[t], kvr.at[k - 1], kp_ss.at[k - 1], kp_rs.at[k - 1], at_dp(t)).wait()
            sums = sums + kvr[k - 1].astype(F32)
        rows[9, m] = head_norm_back(qn[...], hats[0], hats[1]).astype(BF16)
        rows[10, m] = head_norm_back(sums[:, :CW], hats[2], hats[3]).astype(BF16)
        rows[11, m] = sums[:, CW:].astype(BF16)

    def y_copy(j, p, k):
        return rcopy(
            stage.at[j, p, y_of(k)], yrec.at[j, p, k - 1], y_ss.at[j, p, k - 1], y_rs.at[j, p, k - 1], at_my(xl * 4 + y_of(k))
        )

    def x_copy(j, p):
        return rcopy(xsend.at[j, p], xrec.at[j, p], x_ss.at[j, p], x_rs.at[j, p], at_my(my_x))

    def sum_open(j, p):
        for y in range(4):
            for half in range(2):
                stage[j, p, y, half] = acc[j, p, half * 4 + y].astype(BF16)
        for k in (1, 3, 2):
            y_copy(j, p, k).start()
        if j:
            v = acc[1, p].reshape(KB, PT)
            fs_own[p, 0:1, :] = jnp.sum(v, axis=0, keepdims=True)
            fs_own[p, 1:2, :] = jnp.sum(v * std[p], axis=0, keepdims=True)

    def sum_mid(j, p):
        total = acc[j, p, my_x]
        for k in (1, 3, 2):
            y_copy(j, p, k).wait()
        for k in (1, 2, 3):
            total = total + yrec[j, p, k - 1, 1 - xl].astype(F32)
        xsend[j, p] = total.astype(BF16)
        x_copy(j, p).start()

    def sum_close(j, p):
        total = acc[j, p, my]
        for k in (1, 2, 3):
            total = total + yrec[j, p, k - 1, xl].astype(F32)
        x_copy(j, p).wait()
        return total + xrec[j, p].astype(F32)

    def img(x):
        return lax.rem(x + 16, 8)

    def halfd(ref, s):
        return ref.at[pl.ds(0, HALF)] if s == 0 else ref

    def halfu(ref, s):
        return ref.at[pl.ds(HALF, HALF)] if s == 0 else ref

    def rd(c, s):
        i = rs_id(c)
        return rcopy(
            halfd(part.at[i, img(m - 4 + s)], s), halfd(rsd.at[i, s], s), rd_ss.at[c, s], rd_rs.at[c, s], at_mx(m - 1)
        )

    def ru(c, s):
        i = rs_id(c)
        return rcopy(
            halfu(part.at[i, img(m + 4 - s)], s), halfu(rsu.at[i, s], s), ru_ss.at[c, s], ru_rs.at[c, s], at_mx(m + 1)
        )

    def rs_middle(c, s):
        i = rs_id(c)
        lo, hi = (slice(0, HALF), slice(HALF, PAT)) if s == 1 else (slice(0, PAT), slice(0, PAT))
        rd(c, s - 1).wait_recv()
        b = img(m - 4 + s)
        part[i, b, lo] = (part[i, b, lo].astype(F32) + rsd[i, s - 1, lo].astype(F32)).astype(BF16)
        rd(c, s).start()
        ru(c, s - 1).wait_recv()
        b = img(m + 4 - s)
        part[i, b, hi] = (part[i, b, hi].astype(F32) + rsu[i, s - 1, hi].astype(F32)).astype(BF16)
        ru(c, s).start()

    def rs_pair(c, p):
        i = rs_id(c)
        res = dot(fm[kind(i), p], wg[i].reshape(KB, CW)).astype(BF16)
        part[i, pl.ds(2 * p, 2)] = res.reshape(2, PAT, CW)

    def rs_far(c):
        i = rs_id(c)
        w_wait(i, 1, dp_c)
        w_wait(i, 2, 3 - dp)
        rs_pair(c, far_p)

    def rs_send(c):
        rd(c, 0).start()
        ru(c, 0).start()

    def rs_final(c):
        i = rs_id(c)
        rd(c, 3).wait_recv()
        ru(c, 3).wait_recv()
        br[i] = part[i, m].astype(F32) + rsd[i, 3].astype(F32) + rsu[i, 3].astype(F32)

    def gelu(c):
        i = rs_id(c)
        u = br[i]
        phi = 0.5 + 0.5 * lax.erf(u * 0.7071067811865476)
        rows[i - 4, m] = (u * phi).astype(BF16)
        slope = phi + u * (0.3989422804014327 * jnp.exp(-0.5 * u * u))
        rows[i, m] = (br[i - 4] * slope).astype(BF16)

    def ad(a, s):
        b = halfd(rows.at[a, img(m + s)], 3 - s)
        return rcopy(b, b, ad_ss.at[a, s], ad_rs.at[a, s], at_mx(m - 1))

    def au(a, s):
        b = halfu(rows.at[a, img(m - s)], 3 - s)
        return rcopy(b, b, au_ss.at[a, s], au_rs.at[a, s], at_mx(m + 1))

    def ad_wait(a, s):
        b = halfd(rows.at[a, img(m + s + 1)], 3 - s)
        rcopy(b, b, ad_ss.at[a, s], ad_rs.at[a, s], at_mx(m - 1)).wait_recv()

    def au_wait(a, s):
        b = halfu(rows.at[a, img(m - s - 1)], 3 - s)
        rcopy(b, b, au_ss.at[a, s], au_rs.at[a, s], at_mx(m + 1)).wait_recv()

    def ag_open(a):
        ad(a, 0).start()
        au(a, 0).start()

    def ag_middle(a, s):
        ad_wait(a, s - 1)
        ad(a, s).start()
        au_wait(a, s - 1)
        au(a, s).start()

    def ag_pair(a, p):
        r = rows[a, pl.ds(2 * p, 2)].reshape(PT, CW)
        j = kind(a)
        acc[j, p] = acc[j, p] + dot(wg[a].reshape(KB, CW), r, NT).reshape(MY, FW, PT)

    def g_c(a, h):
        return rcopy(gp.at[a, h * 2 + 1 - co], gc.at[a, h], g_ss.at[a, h], g_rs.at[a, h], at_dp(dp_c))

    def g_x(a):
        return rcopy(gs.at[a], gx.at[a], g_ss.at[a, 2], g_rs.at[a, 2], at_dp(dp_x))

    def ag_far(a):
        ad_wait(a, 3)
        au_wait(a, 3)
        ag_pair(a, far_p)

    def g_open(a):
        r = rows[a].reshape(TOK, CW)
        j = kind(a)
        for h in range(4):
            gp[a, h] = dot(fl[j, h * KS : (h + 1) * KS, :], r).astype(BF16)
        for h in range(2):
            g_c(a, h).start()

    def g_mid(a):
        for h in range(2):
            g_c(a, h).wait()
        gs[a] = (gp[a, dp_x].astype(F32) + gc[a, 1 - xh].astype(F32)).astype(BF16)
        g_x(a).start()

    def g_close(a):
        g_x(a).wait()
        gout[a] = (gp[a, dp].astype(F32) + gc[a, xh].astype(F32) + gx[a].astype(F32)).astype(BF16)

    def when_in(v, lo, hi):
        return pl.when((v >= lo) & (v < hi))

    def at_pos(v, step, first=0):
        @when_in(v, 0, POS)
        def _():
            def one(c, _):
                step(c)
                return 0

            lax.fori_loop(jnp.where(v == 0, first, v + 1), v + 2, one, 0)

    w_forward(jnp.int32(0))
    cot_pair(far_p)
    rs_far(jnp.int32(0))
    rs_send(jnp.int32(0))
    start_fwd(1, 0)
    w_forward(jnp.int32(1))
    rs_far(jnp.int32(1))

    def tick(t, _):
        u = t - AG0

        def middle(s):
            at_pos(t - s, lambda c: rs_middle(c, s))
            when_in(u - s, 0, NC)(lambda: ag_middle(u - s, s))

        at_pos(t, rs_send, first=1)
        when_in(u, 0, NC)(lambda: ag_open(u))
        middle(1)

        @pl.when(t + 2 < NC)
        def _():
            w_forward(rs_id(t + 2))

        when_in(u - 5, 0, NC - 2)(lambda: g_mid(u - 5))
        middle(2)

        @pl.when(t == 0)
        def _():
            cot_pair(plus_p)
            cot_pair(minus_p)

        def sides(c):
            rs_pair(c, plus_p)
            rs_pair(c, minus_p)

        at_pos(t, sides)

        @pl.when(t == 1)
        def _():
            cot_pair(own_p)

        at_pos(t - 1, lambda c: rs_pair(c, own_p))
        when_in(u - 1, 0, NC)(lambda: ag_pair(u - 1, own_p))

        @when_in(u - 4, 0, NC - 1)
        def _():
            ag_pair(u - 4, plus_p)
            ag_pair(u - 4, minus_p)

        middle(3)
        pl.when(t == 3)(stats_done)

        @pl.when(t + 2 < NC)
        def _():
            rs_far(t + 2)

        when_in(u - 7, 0, NC - 4)(lambda: g_close(u - 7))
        at_pos(t - 4, rs_final)
        when_in(t - 3, 8, NC)(lambda: gelu(t - 3))
        @when_in(u - 4, 0, NC - 1)
        def _():
            ag_far(u - 4)
            g_open(u - 4)

        pl.when(t == 2)(stats_send)
        pl.when(t == 10)(attn_open)
        pl.when(t == 12)(attn_mid)
        pl.when(t == 15)(attn_close)

        pl.when(u == 9)(lambda: sum_open(0, own_p))

        @pl.when(u == 12)
        def _():
            sum_open(1, own_p)
            sum_open(0, plus_p)
            sum_open(0, minus_p)
            sum_mid(0, own_p)
            sum_open(0, far_p)

        @pl.when(u == 14)
        def _():
            sum_mid(1, own_p)
            for p in (plus_p, minus_p, far_p):
                sum_mid(0, p)

        @pl.when(u == 8)
        def _():
            for p in range(NP):
                my_sent(0, p)

        @when_in(u, 0, NC)
        def _():
            w_x(u).wait_send()
            w_c(u).wait_send()
            w_f(u).wait_send()

        for s in (4, 3, 2, 1):

            def sent(c, s=s):
                rd(c, s - 1).wait_send()
                ru(c, s - 1).wait_send()

            at_pos(t - s, sent)

            @when_in(u - s, 0, NC)
            def _(s=s):
                ad(u - s, s - 1).wait_send()
                au(u - s, s - 1).wait_send()

        return 0

    lax.fori_loop(0, LAST, tick, 0)

    def fz(k):
        return rcopy(fs_own, fs_z.at[k - 1], fz_ss.at[k - 1], fz_rs.at[k - 1], at_mx(m + k))

    def fy(k):
        return rcopy(fs_mid, fs_y.at[k - 1], fy_ss.at[k - 1], fy_rs.at[k - 1], at_my(lax.rem(my + k, 8)))

    for p in (plus_p, minus_p):
        ag_pair(NC - 1, p)
        sum_open(1, p)
    g_mid(NC - 2)
    ad_wait(NC - 1, 3)
    au_wait(NC - 1, 3)
    g_open(NC - 1)
    ag_pair(NC - 1, far_p)
    sum_open(1, far_p)
    for k in range(1, 8):
        fz(k).start()
    g_mid(NC - 1)
    sum_mid(1, plus_p)
    sum_mid(1, minus_p)
    for k in range(1, 8):
        fz(k).wait()
    tot = fs_own[...]
    for k in range(7):
        tot = tot + fs_z[k]
    fs_mid[...] = tot
    for k in range(1, 8):
        fy(k).start()
    sum_mid(1, far_p)
    out_copies = [pltpu.make_async_copy(gout.at[i], piece(i, gd, gu, gw, gq), wl_sem.at[i]) for i in range(NC)]
    for i in range(NC - 4):
        out_copies[i].start()
    ad(NC - 1, 3).wait_send()
    au(NC - 1, 3).wait_send()
    for p in range(NP):
        upd[p * PT : (p + 1) * PT, :] = jnp.transpose(sum_close(0, p), (1, 0)).astype(BF16)
    for i in range(NC - 4, NC):
        g_close(i)
        out_copies[i].start()
    for k in range(1, 8):
        fy(k).wait()
    tot = fs_mid[...]
    for k in range(7):
        tot = tot + fs_y[k]
    tot = tot * (1.0 / D)
    for p in range(NP):
        own = std[p, pl.ds(pl.multiple_of(my * FW, FW), FW), :]
        grad = sum_close(1, p) - tot[p, 0:1, :] - own * tot[p, 1:2, :]
        tgr[p * PT : (p + 1) * PT, :] = jnp.transpose(st_tot[:, p * PT : (p + 1) * PT] * grad, (1, 0)).astype(BF16)
    for c in out_copies:
        c.wait()


def copy_kernel(*refs):
    n = (len(refs) - 2) // 3
    src, dst, held = refs[:n], refs[n : 2 * n], refs[2 * n : 3 * n]
    sin, sout = refs[3 * n :]
    come = [pltpu.make_async_copy(src[i], held[i], sin.at[i]) for i in range(n)]
    go = [pltpu.make_async_copy(held[i], dst[i], sout.at[i]) for i in range(n)]
    for c in come:
        c.start()
    for i in range(n):
        come[i].wait()
        go[i].start()
    for c in go:
        c.wait()


def copied(*arrays):
    far = pl.BlockSpec(memory_space=pl.ANY)
    n = len(arrays)
    return pl.pallas_call(
        copy_kernel,
        out_shape=tuple(jax.ShapeDtypeStruct(a.shape, a.dtype) for a in arrays),
        in_specs=[far] * n,
        out_specs=(far,) * n,
        scratch_shapes=[pltpu.VMEM(a.shape, a.dtype) for a in arrays] + [pltpu.SemaphoreType.DMA((n,))] * 2,
        compiler_params=pltpu.CompilerParams(vmem_limit_bytes=60 * 2**20),
    )(*arrays)


def fused(tok, cot, wd, wu, wp, wq):
    vm, sem = pltpu.VMEM, pltpu.SemaphoreType.DMA
    scratch = [
        vm((TOK, FW), BF16),
        vm((TOK, FW), BF16),
        vm((NC, KS, CW), BF16),
        vm((NC, DP, KS, CW), BF16),
        vm((NC, IMG, PAT, CW), BF16),
        vm((NC, 4, PAT, CW), BF16),
        vm((NC, 4, PAT, CW), BF16),
        vm((NC, PAT, CW), F32),
        vm((NC, IMG, PAT, CW), BF16),
        vm((2, NP, PT, KB), BF16),
        vm((2, NP, MY, FW, PT), BF16),
        vm((2, KB, TOK), BF16),
        vm((NP, KB, PT), F32),
        vm((2, NP, MY, FW, PT), F32),
        vm((NC, DP, KS, CW), BF16),
        vm((NC, 2, KS, CW), BF16),
        vm((NC, KS, CW), BF16),
        vm((NC, KS, CW), BF16),
        vm((2, NP, 4, 2, FW, PT), BF16),
        vm((2, NP, 3, 2, FW, PT), BF16),
        vm((2, NP, FW, PT), BF16),
        vm((2, NP, FW, PT), BF16),
        vm((2, TOK), F32),
        vm((7, 2, TOK), F32),
        vm((1, TOK), F32),
        vm((NP, 2, PT), F32),
        vm((7, NP, 2, PT), F32),
        vm((NP, 2, PT), F32),
        vm((7, NP, 2, PT), F32),
        vm((PAT, CW), BF16),
        vm((DP, PAT, 2 * CW), BF16),
        vm((DP, PAT, 2 * CW), BF16),
        vm((3, PAT, 2 * CW), BF16),
        vm((4, PAT, CW), F32),
        vm((PAT, CW), F32),
        sem((2,)), sem((NC,)),
        sem((NP + 1, 7)), sem((NP + 1, 7)),
        sem((NC, 3)), sem((NC, 3)),
        sem((NC, 4)), sem((NC, 4)),
        sem((NC, 4)), sem((NC, 4)),
        sem((NC, 4)), sem((NC, 4)),
        sem((NC, 4)), sem((NC, 4)),
        sem((NC, 3)), sem((NC, 3)),
        sem((3,)), sem((3,)),
        sem((3,)), sem((3,)),
        sem((2, NP, 3)), sem((2, NP, 3)),
        sem((2, NP)), sem((2, NP)),
        sem((7,)), sem((7,)),
        sem((7,)), sem((7,)),
        sem((7,)), sem((7,)),
    ]
    whole = pl.BlockSpec(memory_space=pltpu.VMEM)
    far = pl.BlockSpec(memory_space=pl.ANY)
    return pl.pallas_call(
        kernel,
        out_shape=(
            jax.ShapeDtypeStruct((TOK, FW), BF16),
            jax.ShapeDtypeStruct((TOK, FW), BF16),
            jax.ShapeDtypeStruct((KS, 4 * CW), BF16),
            jax.ShapeDtypeStruct((KS, 4 * CW), BF16),
            jax.ShapeDtypeStruct((KS, CW), BF16),
            jax.ShapeDtypeStruct((3, KS, CW), BF16),
        ),
        in_specs=[far] * 6,
        out_specs=(whole, whole, far, far, far, far),
        scratch_shapes=scratch,
        compiler_params=pltpu.CompilerParams(
            collective_id=0, has_side_effects=True, vmem_limit_bytes=60 * 2**20
        ),
    )(tok, cot, wd, wu, wp, wq)


def body(tokens, w_qkv, w_up, w_proj, w_down, cotangent):
    upd, tgr, gd, gu, gw, gq = copied(
        *fused(tokens.reshape(TOK, FW), cotangent.reshape(TOK, FW), w_down.T, w_up, w_proj.T, w_qkv.transpose(1, 0, 2))
    )
    shape = (IMG, PAT, FW)
    return (upd.reshape(shape), tgr.reshape(shape), gq.transpose(1, 0, 2), gu, gw.T, gd.T)


def solution(mesh):
    in_specs = (
        P(None, "dp", ("mx", "my")),
        P(("mx", "dp"), None, "my"),
        P(("mx", "dp"), "my"),
        P("my", ("mx", "dp")),
        P("my", ("mx", "dp")),
        P(None, "dp", ("mx", "my")),
    )
    out_specs = (
        P(None, "dp", ("mx", "my")),
        P(None, "dp", ("mx", "my")),
        P(("mx", "dp"), None, "my"),
        P(("mx", "dp"), "my"),
        P("my", ("mx", "dp")),
        P("my", ("mx", "dp")),
    )
    return jax.shard_map(body, mesh=mesh, in_specs=in_specs, out_specs=out_specs, check_vma=False)
```

```python
import functools

import jax
import jax.numpy as jnp
from jax import lax
from jax.experimental import pallas as pl
from jax.experimental.pallas import tpu as pltpu
from jax.sharding import PartitionSpec as P

MESH = pl.DeviceIdType.MESH
F32, BF16 = jnp.float32, jnp.bfloat16

D = 6144
HD = 128
EPS = 1e-06
DP, MX, MY = 4, 8, 8
IMG, PAT = 8, 64
TOK = IMG * PAT
HALF = PAT // 2
NP = IMG // 2
PT = 2 * PAT
FW = 96
KB = MY * FW
KS = KB // DP
CW = 384
NC = 12
HEADS = CW // HD
FACTOR = HD ** (-0.5)
POS = NC - 1
AG0 = 12
LAST = AG0 + NC + 3
ORDER = (0, 1, 2, 3, 8, 9, 10, 11, 4, 5, 6, 7)

NN = (((1,), (0,)), ((), ()))
NT = (((1,), (1,)), ((), ()))


def dot(a, b, dims=NN):
    return lax.dot_general(a, b, dims, preferred_element_type=F32)


def rcopy(src, dst, ssem, rsem, dev):
    return pltpu.make_async_remote_copy(
        src_ref=src, dst_ref=dst, send_sem=ssem, recv_sem=rsem, device_id=dev, device_id_type=MESH
    )


def rs_id(c):
    one = jnp.int32(1)
    ge4 = jnp.where(c >= 4, one, 0)
    ge8 = jnp.where(c >= 8, one, 0)
    return c + 4 * ge4 - 8 * ge8


def kind(i):
    return jnp.where((i < 4) | (i == 8), 0, 1).astype(jnp.int32)


def head_norm(x):
    hats, invs = [], []
    for h in range(HEADS):
        part = x[:, h * HD : (h + 1) * HD]
        cen = part - jnp.mean(part, axis=1, keepdims=True)
        inv = lax.rsqrt(jnp.mean(cen * cen, axis=1, keepdims=True) + EPS)
        hats.append(cen * inv)
        invs.append(jnp.broadcast_to(inv, cen.shape))
    return jnp.concatenate(hats, axis=1), jnp.concatenate(invs, axis=1)


def head_norm_back(up, hat, inv):
    outs = []
    for h in range(HEADS):
        s = slice(h * HD, (h + 1) * HD)
        u, n = up[:, s], hat[:, s]
        outs.append(
            inv[:, s]
            * (u - jnp.mean(u, axis=1, keepdims=True) - n * jnp.mean(u * n, axis=1, keepdims=True))
        )
    return jnp.concatenate(outs, axis=1)


def kernel(
    tok, cot, wd, wu, wp, wq, upd, tgr, gd, gu, gw, gq,
    xraw, craw, gout,
    wg, part, rsd, rsu, br, rows, fm, ft, fl, std, acc, gp, gc, gs, gx,
    stage, yrec, xsend, xrec, st_own, st_in, st_tot, fs_own, fs_z, fs_mid, fs_y,
    qlow, kvg, kvp, kvr, hats, qn,
    loc_sem, wl_sem, my_ss, my_rs, w_ss, w_rs, rd_ss, rd_rs, ru_ss, ru_rs, ad_ss, ad_rs, au_ss, au_rs,
    g_ss, g_rs, kv_ss, kv_rs, kp_ss, kp_rs, y_ss, y_rs, x_ss, x_rs, st_ss, st_rs, fz_ss, fz_rs, fy_ss, fy_rs,
):
    dp, m, my = lax.axis_index("dp"), lax.axis_index("mx"), lax.axis_index("my")
    xh, co = dp // 2, lax.rem(dp, 2)
    xl, yy = my // 4, lax.rem(my, 4)
    dp_x = lax.rem(dp + 2, 4)
    dp_c = xh * 2 + 1 - co
    my_x = lax.rem(my + 4, 8)
    own_p = m // 2
    far_p, plus_p, minus_p = lax.rem(own_p + 2, 4), lax.rem(own_p + 1, 4), lax.rem(own_p + 3, 4)

    def at_dp(i):
        return {"dp": i, "mx": m, "my": my}

    def at_mx(i):
        return {"dp": dp, "mx": lax.rem(i + 16, 8), "my": my}

    def at_my(i):
        return {"dp": dp, "mx": m, "my": i}

    def y_of(k):
        return lax.rem(yy + k, 4)

    barrier = pltpu.get_barrier_semaphore()
    peers = [at_dp(lax.rem(dp + k, 4)) for k in (1, 2, 3)]
    peers += [at_mx(m + k) for k in range(1, 8)]
    peers += [at_my(lax.rem(my + k, 8)) for k in range(1, 8)]
    for p in peers:
        pl.semaphore_signal(barrier, inc=1, device_id=p, device_id_type=MESH)

    def piece(i, down, up, proj, qkv):
        if i < 4:
            return down.at[:, i * CW : (i + 1) * CW]
        if i < 8:
            return up.at[:, (i - 4) * CW : (i - 3) * CW]
        return proj if i == 8 else qkv.at[i - 9]

    own_c = pltpu.make_async_copy(cot, craw, loc_sem.at[0])
    own_x = pltpu.make_async_copy(tok, xraw, loc_sem.at[1])
    own_c.start()
    own_x.start()
    own_w = [pltpu.make_async_copy(piece(i, wd, wu, wp, wq), wg.at[i, dp], wl_sem.at[i]) for i in range(NC)]
    for i in ORDER:
        own_w[i].start()
    own_c.wait()
    for p in range(NP):
        ft[0, p, my] = jnp.transpose(craw[p * PT : (p + 1) * PT, :].astype(F32), (1, 0)).astype(BF16)
    own_x.wait()
    for p in range(NP):
        ft[1, p, my] = jnp.transpose(xraw[p * PT : (p + 1) * PT, :].astype(F32), (1, 0)).astype(BF16)
    pl.semaphore_wait(barrier, len(peers))

    def block(j, p, who):
        return ft.at[1, :, who] if j else ft.at[0, p, who]

    def slot(j, p):
        return NP if j else p

    def my_first(j, p):
        b, q = block(j, p, my), slot(j, p)
        return rcopy(b, b, my_ss.at[q, 0], my_rs.at[q, 0], at_my(my_x))

    def my_own(j, p, k):
        b, q = block(j, p, my), slot(j, p)
        return rcopy(b, b, my_ss.at[q, k], my_rs.at[q, k], at_my(xl * 4 + y_of(k)))

    def my_fwd(j, p, k):
        b, q = block(j, p, my_x), slot(j, p)
        return rcopy(b, b, my_ss.at[q, 3 + k], my_rs.at[q, 3 + k], at_my(xl * 4 + y_of(k)))

    def my_wait_first(j, p):
        b, q = block(j, p, my_x), slot(j, p)
        rcopy(b, b, my_ss.at[q, 0], my_rs.at[q, 0], at_my(my_x)).wait_recv()

    def my_wait(j, p):
        q = slot(j, p)
        for k in (1, 3, 2):
            a = block(j, p, xl * 4 + y_of(4 - k))
            b = block(j, p, (1 - xl) * 4 + y_of(4 - k))
            rcopy(a, a, my_ss.at[q, k], my_rs.at[q, k], at_my(my_x)).wait_recv()
            rcopy(b, b, my_ss.at[q, 3 + k], my_rs.at[q, 3 + k], at_my(my_x)).wait_recv()

    def my_sent(j, p):
        my_first(j, p).wait_send()
        for k in (1, 3, 2):
            my_own(j, p, k).wait_send()
            my_fwd(j, p, k).wait_send()

    def w_x(i):
        return rcopy(wg.at[i, dp], wg.at[i, dp], w_ss.at[i, 0], w_rs.at[i, 0], at_dp(dp_x))

    def w_c(i):
        return rcopy(wg.at[i, dp], wg.at[i, dp], w_ss.at[i, 1], w_rs.at[i, 1], at_dp(dp_c))

    def w_f(i):
        return rcopy(wg.at[i, dp_x], wg.at[i, dp_x], w_ss.at[i, 2], w_rs.at[i, 2], at_dp(dp_c))

    def w_wait(i, step, who):
        rcopy(wg.at[i, who], wg.at[i, who], w_ss.at[i, step], w_rs.at[i, step], at_dp(dp_c)).wait_recv()

    def w_forward(i):
        w_wait(i, 0, dp_x)
        w_f(i).start()

    def start_own(j, p):
        for k in (1, 3, 2):
            my_own(j, p, k).start()

    def start_fwd(j, p):
        my_wait_first(j, p)
        for k in (1, 3, 2):
            my_fwd(j, p, k).start()

    my_first(0, far_p).start()
    own_w[0].wait()
    w_x(0).start()
    w_c(0).start()
    start_own(0, far_p)
    for p in (plus_p, minus_p, own_p):
        my_first(0, p).start()
    own_w[1].wait()
    w_x(1).start()
    w_c(1).start()
    start_own(0, plus_p)
    start_fwd(0, far_p)
    start_own(0, minus_p)
    start_fwd(0, plus_p)
    my_first(1, 0).start()
    for i in ORDER[2:]:
        own_w[i].wait()
        w_x(i).start()
        w_c(i).start()
    start_own(0, own_p)
    start_fwd(0, minus_p)
    start_fwd(0, own_p)
    start_own(1, 0)
    acc[...] = jnp.zeros_like(acc)

    def cot_pair(p):
        my_wait(0, p)
        v = ft[0, p].reshape(KB, PT)
        fm[0, p] = jnp.transpose(v.astype(F32), (1, 0)).astype(BF16)

    def stats_send():
        my_wait(1, 0)
        my_sent(1, 0)
        for p in range(NP):
            xs = ft[1, p].reshape(KB, PT).astype(F32)
            std[p] = xs
            total = jnp.sum(xs, axis=0, keepdims=True)
            cen = xs - total * (1.0 / KB)
            st_own[0:1, p * PT : (p + 1) * PT] = total
            st_own[1:2, p * PT : (p + 1) * PT] = jnp.sum(cen * cen, axis=0, keepdims=True)
            fl[0, :, p * PT : (p + 1) * PT] = ft[0, p].reshape(KB, PT)
        for k in range(1, 8):
            rcopy(st_own, st_in.at[k - 1], st_ss.at[k - 1], st_rs.at[k - 1], at_mx(m + k)).start()

    def stats_done():
        for k in range(1, 8):
            rcopy(st_own, st_in.at[k - 1], st_ss.at[k - 1], st_rs.at[k - 1], at_mx(m + k)).wait()
        total = st_own[0:1, :]
        for k in range(7):
            total = total + st_in[k, 0:1, :]
        mean = total * (1.0 / D)
        spread = jnp.zeros_like(mean)
        for k in range(8):
            s, q = (st_own[0:1, :], st_own[1:2, :]) if k == 7 else (st_in[k, 0:1, :], st_in[k, 1:2, :])
            off = s * (1.0 / KB) - mean
            spread = spread + q + KB * off * off
        inv = lax.rsqrt(spread * (1.0 / D) + EPS)
        st_tot[...] = inv
        for p in range(NP):
            c = slice(p * PT, (p + 1) * PT)
            v = (std[p] - mean[:, c]) * inv[:, c]
            std[p] = v
            fl[1, :, c] = v.astype(BF16)
            fm[1, p] = jnp.transpose(v, (1, 0)).astype(BF16)

    def attn_open():
        q_hat, q_inv = head_norm(br[9])
        k_hat, k_inv = head_norm(br[10])
        hats[0], hats[1], hats[2], hats[3] = q_hat, q_inv, k_hat, k_inv
        qlow[...] = q_hat.astype(BF16)
        kvg[dp, :, :CW] = k_hat.astype(BF16)
        kvg[dp, :, CW:] = br[11].astype(BF16)
        for k in (1, 2, 3):
            rcopy(kvg.at[dp], kvg.at[dp], kv_ss.at[k - 1], kv_rs.at[k - 1], at_dp(lax.rem(dp + k, 4))).start()

    def attn_mid():
        for k in (1, 2, 3):
            s = lax.rem(dp + 4 - k, 4)
            rcopy(kvg.at[s], kvg.at[s], kv_ss.at[k - 1], kv_rs.at[k - 1], at_dp(dp_c)).wait_recv()
            rcopy(kvg.at[dp], kvg.at[dp], kv_ss.at[k - 1], kv_rs.at[k - 1], at_dp(dp_c)).wait_send()
        for h in range(HEADS):
            s = slice(h * HD, (h + 1) * HD)
            q = qlow[:, s]
            keys = kvg[:, :, s].reshape(DP * PAT, HD)
            vals = kvg[:, :, CW + h * HD : CW + (h + 1) * HD].reshape(DP * PAT, HD)
            ag = br[8, :, s].astype(BF16)
            raised = jnp.exp(dot(q, keys, NT) * FACTOR)
            probs = raised / jnp.sum(raised, axis=1, keepdims=True)
            plow = probs.astype(BF16)
            rows[8, m, :, s] = dot(plow, vals).astype(BF16)
            pgrad = dot(ag, vals, NT)
            sgrad = probs * (pgrad - jnp.sum(probs * pgrad, axis=1, keepdims=True))
            slow = (sgrad * FACTOR).astype(BF16)
            qn[:, s] = dot(slow, keys)
            vpart = dot(jnp.transpose(plow.astype(F32), (1, 0)).astype(BF16), ag)
            kpart = dot(jnp.transpose(slow.astype(F32), (1, 0)).astype(BF16), q)
            kvp[:, :, s] = kpart.astype(BF16).reshape(DP, PAT, HD)
            kvp[:, :, CW + h * HD : CW + (h + 1) * HD] = vpart.astype(BF16).reshape(DP, PAT, HD)
        for k in (1, 2, 3):
            t = lax.rem(dp + k, 4)
            rcopy(kvp.at[t], kvr.at[k - 1], kp_ss.at[k - 1], kp_rs.at[k - 1], at_dp(t)).start()

    def attn_close():
        sums = kvp[dp].astype(F32)
        for k in (1, 2, 3):
            t = lax.rem(dp + k, 4)
            rcopy(kvp.at[t], kvr.at[k - 1], kp_ss.at[k - 1], kp_rs.at[k - 1], at_dp(t)).wait()
            sums = sums + kvr[k - 1].astype(F32)
        rows[9, m] = head_norm_back(qn[...], hats[0], hats[1]).astype(BF16)
        rows[10, m] = head_norm_back(sums[:, :CW], hats[2], hats[3]).astype(BF16)
        rows[11, m] = sums[:, CW:].astype(BF16)

    def y_copy(j, p, k):
        return rcopy(
            stage.at[j, p, y_of(k)], yrec.at[j, p, k - 1], y_ss.at[j, p, k - 1], y_rs.at[j, p, k - 1], at_my(xl * 4 + y_of(k))
        )

    def x_copy(j, p):
        return rcopy(xsend.at[j, p], xrec.at[j, p], x_ss.at[j, p], x_rs.at[j, p], at_my(my_x))

    def sum_open(j, p):
        for y in range(4):
            for half in range(2):
                stage[j, p, y, half] = acc[j, p, half * 4 + y].astype(BF16)
        for k in (1, 3, 2):
            y_copy(j, p, k).start()
        if j:
            v = acc[1, p].reshape(KB, PT)
            fs_own[p, 0:1, :] = jnp.sum(v, axis=0, keepdims=True)
            fs_own[p, 1:2, :] = jnp.sum(v * std[p], axis=0, keepdims=True)

    def sum_mid(j, p):
        total = acc[j, p, my_x]
        for k in (1, 3, 2):
            y_copy(j, p, k).wait()
        for k in (1, 2, 3):
            total = total + yrec[j, p, k - 1, 1 - xl].astype(F32)
        xsend[j, p] = total.astype(BF16)
        x_copy(j, p).start()

    def sum_close(j, p):
        total = acc[j, p, my]
        for k in (1, 2, 3):
            total = total + yrec[j, p, k - 1, xl].astype(F32)
        x_copy(j, p).wait()
        return total + xrec[j, p].astype(F32)

    def img(x):
        return lax.rem(x + 16, 8)

    def halfd(ref, s):
        return ref.at[pl.ds(0, HALF)] if s == 0 else ref

    def halfu(ref, s):
        return ref.at[pl.ds(HALF, HALF)] if s == 0 else ref

    def rd(c, s):
        i = rs_id(c)
        return rcopy(
            halfd(part.at[i, img(m - 4 + s)], s), halfd(rsd.at[i, s], s), rd_ss.at[c, s], rd_rs.at[c, s], at_mx(m - 1)
        )

    def ru(c, s):
        i = rs_id(c)
        return rcopy(
            halfu(part.at[i, img(m + 4 - s)], s), halfu(rsu.at[i, s], s), ru_ss.at[c, s], ru_rs.at[c, s], at_mx(m + 1)
        )

    def rs_middle(c, s):
        i = rs_id(c)
        lo, hi = (slice(0, HALF), slice(HALF, PAT)) if s == 1 else (slice(0, PAT), slice(0, PAT))
        rd(c, s - 1).wait_recv()
        b = img(m - 4 + s)
        part[i, b, lo] = (part[i, b, lo].astype(F32) + rsd[i, s - 1, lo].astype(F32)).astype(BF16)
        rd(c, s).start()
        ru(c, s - 1).wait_recv()
        b = img(m + 4 - s)
        part[i, b, hi] = (part[i, b, hi].astype(F32) + rsu[i, s - 1, hi].astype(F32)).astype(BF16)
        ru(c, s).start()

    def rs_pair(c, p):
        i = rs_id(c)
        res = dot(fm[kind(i), p], wg[i].reshape(KB, CW)).astype(BF16)
        part[i, pl.ds(2 * p, 2)] = res.reshape(2, PAT, CW)

    def rs_far(c):
        i = rs_id(c)
        w_wait(i, 1, dp_c)
        w_wait(i, 2, 3 - dp)
        rs_pair(c, far_p)

    def rs_send(c):
        rd(c, 0).start()
        ru(c, 0).start()

    def rs_final(c):
        i = rs_id(c)
        rd(c, 3).wait_recv()
        ru(c, 3).wait_recv()
        br[i] = part[i, m].astype(F32) + rsd[i, 3].astype(F32) + rsu[i, 3].astype(F32)

    def gelu(c):
        i = rs_id(c)
        u = br[i]
        phi = 0.5 + 0.5 * lax.erf(u * 0.7071067811865476)
        rows[i - 4, m] = (u * phi).astype(BF16)
        slope = phi + u * (0.3989422804014327 * jnp.exp(-0.5 * u * u))
        rows[i, m] = (br[i - 4] * slope).astype(BF16)

    def ad(a, s):
        b = halfd(rows.at[a, img(m + s)], 3 - s)
        return rcopy(b, b, ad_ss.at[a, s], ad_rs.at[a, s], at_mx(m - 1))

    def au(a, s):
        b = halfu(rows.at[a, img(m - s)], 3 - s)
        return rcopy(b, b, au_ss.at[a, s], au_rs.at[a, s], at_mx(m + 1))

    def ad_wait(a, s):
        b = halfd(rows.at[a, img(m + s + 1)], 3 - s)
        rcopy(b, b, ad_ss.at[a, s], ad_rs.at[a, s], at_mx(m - 1)).wait_recv()

    def au_wait(a, s):
        b = halfu(rows.at[a, img(m - s - 1)], 3 - s)
        rcopy(b, b, au_ss.at[a, s], au_rs.at[a, s], at_mx(m + 1)).wait_recv()

    def ag_open(a):
        ad(a, 0).start()
        au(a, 0).start()

    def ag_middle(a, s):
        ad_wait(a, s - 1)
        ad(a, s).start()
        au_wait(a, s - 1)
        au(a, s).start()

    def ag_pair(a, p):
        r = rows[a, pl.ds(2 * p, 2)].reshape(PT, CW)
        j = kind(a)
        acc[j, p] = acc[j, p] + dot(wg[a].reshape(KB, CW), r, NT).reshape(MY, FW, PT)

    def g_c(a, h):
        return rcopy(gp.at[a, h * 2 + 1 - co], gc.at[a, h], g_ss.at[a, h], g_rs.at[a, h], at_dp(dp_c))

    def g_x(a):
        return rcopy(gs.at[a], gx.at[a], g_ss.at[a, 2], g_rs.at[a, 2], at_dp(dp_x))

    def ag_far(a):
        ad_wait(a, 3)
        au_wait(a, 3)
        ag_pair(a, far_p)

    def g_open(a):
        r = rows[a].reshape(TOK, CW)
        j = kind(a)
        for h in range(4):
            gp[a, h] = dot(fl[j, h * KS : (h + 1) * KS, :], r).astype(BF16)
        for h in range(2):
            g_c(a, h).start()

    def g_mid(a):
        for h in range(2):
            g_c(a, h).wait()
        gs[a] = (gp[a, dp_x].astype(F32) + gc[a, 1 - xh].astype(F32)).astype(BF16)
        g_x(a).start()

    def g_close(a):
        g_x(a).wait()
        gout[a] = (gp[a, dp].astype(F32) + gc[a, xh].astype(F32) + gx[a].astype(F32)).astype(BF16)

    def when_in(v, lo, hi):
        return pl.when((v >= lo) & (v < hi))

    def at_pos(v, step, first=0):
        @when_in(v, 0, POS)
        def _():
            def one(c, _):
                step(c)
                return 0

            lax.fori_loop(jnp.where(v == 0, first, v + 1), v + 2, one, 0)

    w_forward(jnp.int32(0))
    cot_pair(far_p)
    rs_far(jnp.int32(0))
    rs_send(jnp.int32(0))
    start_fwd(1, 0)
    w_forward(jnp.int32(1))
    rs_far(jnp.int32(1))

    def tick(t, _):
        u = t - AG0

        def middle(s):
            at_pos(t - s, lambda c: rs_middle(c, s))
            when_in(u - s, 0, NC)(lambda: ag_middle(u - s, s))

        at_pos(t, rs_send, first=1)
        when_in(u, 0, NC)(lambda: ag_open(u))
        middle(1)

        @pl.when(t + 2 < NC)
        def _():
            w_forward(rs_id(t + 2))

        when_in(u - 5, 0, NC - 2)(lambda: g_mid(u - 5))
        middle(2)

        @pl.when(t == 0)
        def _():
            cot_pair(plus_p)
            cot_pair(minus_p)

        def sides(c):
            rs_pair(c, plus_p)
            rs_pair(c, minus_p)

        at_pos(t, sides)

        @pl.when(t == 1)
        def _():
            cot_pair(own_p)

        at_pos(t - 1, lambda c: rs_pair(c, own_p))
        when_in(u - 1, 0, NC)(lambda: ag_pair(u - 1, own_p))

        @when_in(u - 4, 0, NC - 1)
        def _():
            ag_pair(u - 4, plus_p)
            ag_pair(u - 4, minus_p)

        middle(3)
        pl.when(t == 3)(stats_done)

        @pl.when(t + 2 < NC)
        def _():
            rs_far(t + 2)

        when_in(u - 7, 0, NC - 4)(lambda: g_close(u - 7))
        at_pos(t - 4, rs_final)
        when_in(t - 3, 8, NC)(lambda: gelu(t - 3))
        @when_in(u - 4, 0, NC - 1)
        def _():
            ag_far(u - 4)
            g_open(u - 4)

        pl.when(t == 2)(stats_send)
        pl.when(t == 10)(attn_open)
        pl.when(t == 12)(attn_mid)
        pl.when(t == 15)(attn_close)

        pl.when(u == 9)(lambda: sum_open(0, own_p))

        @pl.when(u == 12)
        def _():
            sum_open(1, own_p)
            sum_open(0, plus_p)
            sum_open(0, minus_p)
            sum_mid(0, own_p)
            sum_open(0, far_p)

        @pl.when(u == 14)
        def _():
            sum_mid(1, own_p)
            for p in (plus_p, minus_p, far_p):
                sum_mid(0, p)

        @pl.when(u == 8)
        def _():
            for p in range(NP):
                my_sent(0, p)

        @when_in(u, 0, NC)
        def _():
            w_x(u).wait_send()
            w_c(u).wait_send()
            w_f(u).wait_send()

        for s in (4, 3, 2, 1):

            def sent(c, s=s):
                rd(c, s - 1).wait_send()
                ru(c, s - 1).wait_send()

            at_pos(t - s, sent)

            @when_in(u - s, 0, NC)
            def _(s=s):
                ad(u - s, s - 1).wait_send()
                au(u - s, s - 1).wait_send()

        return 0

    lax.fori_loop(0, LAST, tick, 0)

    def fz(k):
        return rcopy(fs_own, fs_z.at[k - 1], fz_ss.at[k - 1], fz_rs.at[k - 1], at_mx(m + k))

    def fy(k):
        return rcopy(fs_mid, fs_y.at[k - 1], fy_ss.at[k - 1], fy_rs.at[k - 1], at_my(lax.rem(my + k, 8)))

    for p in (plus_p, minus_p):
        ag_pair(NC - 1, p)
        sum_open(1, p)
    g_mid(NC - 2)
    ad_wait(NC - 1, 3)
    au_wait(NC - 1, 3)
    g_open(NC - 1)
    ag_pair(NC - 1, far_p)
    sum_open(1, far_p)
    for k in range(1, 8):
        fz(k).start()
    g_mid(NC - 1)
    sum_mid(1, plus_p)
    sum_mid(1, minus_p)
    out_copies = [pltpu.make_async_copy(gout.at[i], piece(i, gd, gu, gw, gq), wl_sem.at[i]) for i in range(NC)]
    g_close(NC - 4)
    for i in range(NC - 3):
        out_copies[i].start()
    for p in range(NP):
        upd[p * PT : (p + 1) * PT, :] = jnp.transpose(sum_close(0, p), (1, 0)).astype(BF16)
    for k in range(1, 8):
        fz(k).wait()
    tot = fs_own[...]
    for k in range(7):
        tot = tot + fs_z[k]
    fs_mid[...] = tot
    for k in range(1, 8):
        fy(k).start()
    sum_mid(1, far_p)
    ad(NC - 1, 3).wait_send()
    au(NC - 1, 3).wait_send()
    for i in range(NC - 3, NC):
        g_close(i)
        out_copies[i].start()
    for k in range(1, 8):
        fy(k).wait()
    tot = fs_mid[...]
    for k in range(7):
        tot = tot + fs_y[k]
    tot = tot * (1.0 / D)
    for p in range(NP):
        own = std[p, pl.ds(pl.multiple_of(my * FW, FW), FW), :]
        grad = sum_close(1, p) - tot[p, 0:1, :] - own * tot[p, 1:2, :]
        tgr[p * PT : (p + 1) * PT, :] = jnp.transpose(st_tot[:, p * PT : (p + 1) * PT] * grad, (1, 0)).astype(BF16)
    for c in out_copies:
        c.wait()


def copy_kernel(*refs):
    n = (len(refs) - 2) // 3
    src, dst, held = refs[:n], refs[n : 2 * n], refs[2 * n : 3 * n]
    sin, sout = refs[3 * n :]
    come = [pltpu.make_async_copy(src[i], held[i], sin.at[i]) for i in range(n)]
    go = [pltpu.make_async_copy(held[i], dst[i], sout.at[i]) for i in range(n)]
    for c in come:
        c.start()
    for i in range(n):
        come[i].wait()
        go[i].start()
    for c in go:
        c.wait()


def copied(*arrays):
    far = pl.BlockSpec(memory_space=pl.ANY)
    n = len(arrays)
    return pl.pallas_call(
        copy_kernel,
        out_shape=tuple(jax.ShapeDtypeStruct(a.shape, a.dtype) for a in arrays),
        in_specs=[far] * n,
        out_specs=(far,) * n,
        scratch_shapes=[pltpu.VMEM(a.shape, a.dtype) for a in arrays] + [pltpu.SemaphoreType.DMA((n,))] * 2,
        compiler_params=pltpu.CompilerParams(vmem_limit_bytes=60 * 2**20),
    )(*arrays)


def fused(tok, cot, wd, wu, wp, wq):
    vm, sem = pltpu.VMEM, pltpu.SemaphoreType.DMA
    scratch = [
        vm((TOK, FW), BF16),
        vm((TOK, FW), BF16),
        vm((NC, KS, CW), BF16),
        vm((NC, DP, KS, CW), BF16),
        vm((NC, IMG, PAT, CW), BF16),
        vm((NC, 4, PAT, CW), BF16),
        vm((NC, 4, PAT, CW), BF16),
        vm((NC, PAT, CW), F32),
        vm((NC, IMG, PAT, CW), BF16),
        vm((2, NP, PT, KB), BF16),
        vm((2, NP, MY, FW, PT), BF16),
        vm((2, KB, TOK), BF16),
        vm((NP, KB, PT), F32),
        vm((2, NP, MY, FW, PT), F32),
        vm((NC, DP, KS, CW), BF16),
        vm((NC, 2, KS, CW), BF16),
        vm((NC, KS, CW), BF16),
        vm((NC, KS, CW), BF16),
        vm((2, NP, 4, 2, FW, PT), BF16),
        vm((2, NP, 3, 2, FW, PT), BF16),
        vm((2, NP, FW, PT), BF16),
        vm((2, NP, FW, PT), BF16),
        vm((2, TOK), F32),
        vm((7, 2, TOK), F32),
        vm((1, TOK), F32),
        vm((NP, 2, PT), F32),
        vm((7, NP, 2, PT), F32),
        vm((NP, 2, PT), F32),
        vm((7, NP, 2, PT), F32),
        vm((PAT, CW), BF16),
        vm((DP, PAT, 2 * CW), BF16),
        vm((DP, PAT, 2 * CW), BF16),
        vm((3, PAT, 2 * CW), BF16),
        vm((4, PAT, CW), F32),
        vm((PAT, CW), F32),
        sem((2,)), sem((NC,)),
        sem((NP + 1, 7)), sem((NP + 1, 7)),
        sem((NC, 3)), sem((NC, 3)),
        sem((NC, 4)), sem((NC, 4)),
        sem((NC, 4)), sem((NC, 4)),
        sem((NC, 4)), sem((NC, 4)),
        sem((NC, 4)), sem((NC, 4)),
        sem((NC, 3)), sem((NC, 3)),
        sem((3,)), sem((3,)),
        sem((3,)), sem((3,)),
        sem((2, NP, 3)), sem((2, NP, 3)),
        sem((2, NP)), sem((2, NP)),
        sem((7,)), sem((7,)),
        sem((7,)), sem((7,)),
        sem((7,)), sem((7,)),
    ]
    whole = pl.BlockSpec(memory_space=pltpu.VMEM)
    far = pl.BlockSpec(memory_space=pl.ANY)
    return pl.pallas_call(
        kernel,
        out_shape=(
            jax.ShapeDtypeStruct((TOK, FW), BF16),
            jax.ShapeDtypeStruct((TOK, FW), BF16),
            jax.ShapeDtypeStruct((KS, 4 * CW), BF16),
            jax.ShapeDtypeStruct((KS, 4 * CW), BF16),
            jax.ShapeDtypeStruct((KS, CW), BF16),
            jax.ShapeDtypeStruct((3, KS, CW), BF16),
        ),
        in_specs=[far] * 6,
        out_specs=(whole, whole, far, far, far, far),
        scratch_shapes=scratch,
        compiler_params=pltpu.CompilerParams(
            collective_id=0, has_side_effects=True, vmem_limit_bytes=60 * 2**20
        ),
    )(tok, cot, wd, wu, wp, wq)


def body(tokens, w_qkv, w_up, w_proj, w_down, cotangent):
    upd, tgr, gd, gu, gw, gq = copied(
        *fused(tokens.reshape(TOK, FW), cotangent.reshape(TOK, FW), w_down.T, w_up, w_proj.T, w_qkv.transpose(1, 0, 2))
    )
    shape = (IMG, PAT, FW)
    return (upd.reshape(shape), tgr.reshape(shape), gq.transpose(1, 0, 2), gu, gw.T, gd.T)


def solution(mesh):
    in_specs = (
        P(None, "dp", ("mx", "my")),
        P(("mx", "dp"), None, "my"),
        P(("mx", "dp"), "my"),
        P("my", ("mx", "dp")),
        P("my", ("mx", "dp")),
        P(None, "dp", ("mx", "my")),
    )
    out_specs = (
        P(None, "dp", ("mx", "my")),
        P(None, "dp", ("mx", "my")),
        P(("mx", "dp"), None, "my"),
        P(("mx", "dp"), "my"),
        P("my", ("mx", "dp")),
        P("my", ("mx", "dp")),
    )
    return jax.shard_map(body, mesh=mesh, in_specs=in_specs, out_specs=out_specs, check_vma=False)
```
